32 devices in a mesh: section: 2 (over core), dp: 16 (over z, y, x).
Axes of the slice: x: 2, y: 2, z: 4, core: 2. Of those that a mesh axis runs over, the one named last changes fastest.
Arguments:
- codebook_embed: bfloat16 [2, 2048, 3, 1024], P(None, 'dp'), may hold values from -6 to 6
- item_lengths: int32 [2, 16, 8], P(None, 'dp'), may hold values from 1 to 64, 128 in all within a row
- gain_attn: float32 [2, 1024], P('section'), may hold values from 0.5 to 1.5
- w_qkv: bfloat16 [2, 1024, 3072], P('section'), may hold values from -0.1875 to 0.1875
- w_out: bfloat16 [2, 1024, 1024], P('section'), may hold values from -0.375 to 0.375
- gain_mlp: float32 [2, 1024], P('section'), may hold values from 0.5 to 1.5
- w_up: bfloat16 [2, 1024, 4096], P('section'), may hold values from -0.1875 to 0.1875
- w_down: bfloat16 [2, 4096, 1024], P('section'), may hold values from -0.09375 to 0.09375
- cotangent: bfloat16 [2, 2048, 3, 1024], P(None, 'dp'), may hold values from -6 to 6
Outputs:
- local_out: bfloat16 [2, 2048, 3, 1024], P(None, 'dp', None, 'section')
- embed_grad: float32 [2, 2048, 3, 1024], P(None, 'dp', None, 'section')
- grad_gain_attn: float32 [2, 1024], P('section', 'dp')
- grad_w_qkv: float32 [2, 1024, 3072], P('section', 'dp')
- grad_w_out: float32 [2, 1024, 1024], P('section', 'dp')
- grad_gain_mlp: float32 [2, 1024], P('section', 'dp')
- grad_w_up: float32 [2, 1024, 4096], P('section', 'dp')
- grad_w_down: float32 [2, 4096, 1024], P('section', 'dp')
The draws below stay inside these ranges and needn't reach their ends.
Inputs may be any that keep to these rules, and one draw needn't show every extreme that they name: `item_lengths`: for every micro-batch and index of dp the 8 lengths sum to 128 and the largest is exactly 64.
All inputs are finite; a program needn't handle non-finite values.
Results may differ from the reference program's by a relative error of at most 0.015.
Values may be sent and summed in bfloat16 or wider, within the bound.
No kernel may reach another device: no remote copies, remote signals or barrier semaphores. Data moves between devices by JAX's collectives and lax.ppermute only.
A program may use at most 576 MiB of HBM per device.

```python
import math
import jax
import jax.numpy as jnp
import numpy as np
from jax import lax

D = 1024
HEADS = 16
FF = 4096
CB = 3
MB = 2
FR = 128
ITEMS = 8
LONGEST = 64
BLOCKS = 16
FRAMES = 2048


def levels(stream_key, dims, split, low, high):
    def one(axis_at, parts):
        steps = jax.random.uniform(jax.random.fold_in(jax.random.fold_in(stream_key, 6), axis_at), (parts,), jnp.float32, low / len(split), high / len(split))
        return jnp.repeat(jnp.exp(steps), dims[axis_at] // parts).reshape((-1,) + (1,) * (len(dims) - axis_at - 1))

    level = one(*split[0])
    for cut in split[1:]:
        level = level * one(*cut)
    return level


def length_profile(amount, total, limit, slope):
    loads = [(1 << 20) // math.isqrt(rank ** slope) + 1 for rank in range(2, amount + 1)]
    rest, counts = total - limit - (amount - 1), [1] * (amount - 1)
    while rest > 0:
        candidates = [i for i in range(amount - 1) if counts[i] < limit]
        pool, budget = sum([loads[i] for i in candidates]), rest
        for i in candidates:
            more = min(limit - counts[i], max(1, budget * loads[i] // pool), rest)
            counts[i] = counts[i] + more
            rest = rest - more
    return np.array([limit] + counts)


def ragged(stream_key, count, total, limit, skew):
    if count == 2:
        one = jax.random.randint(stream_key, (), max(1, total - limit), min(limit, total - 1) + 1)
        return jnp.stack([one, total - one])
    sizes = jnp.asarray(length_profile(count, total, limit, skew), jnp.int32)
    twos = (count - 1) // 2
    giver, receiver = sizes[1:1 + 2 * twos:2], sizes[2:2 + 2 * twos:2]
    room = jnp.minimum(giver - 1, limit - receiver)
    moved = jax.random.randint(jax.random.fold_in(stream_key, 1), (twos,), 0, 1 << 20) % (room + 1)
    sizes = sizes.at[1:1 + 2 * twos:2].set(giver - moved).at[2:2 + 2 * twos:2].set(receiver + moved)
    return sizes[jax.random.permutation(jax.random.fold_in(stream_key, 2), count)]


def centred(stream_key, extent, scale, bound, pieces=(), kind=jnp.bfloat16):
    drawn = jax.random.normal(stream_key, extent, jnp.float32) * scale
    if len(pieces) > 0:
        drawn = levels(stream_key, extent, pieces, -0.22, 0.18) * drawn
    return jnp.clip(drawn, min=-bound, max=bound).astype(kind)


def setup_inputs(seed: int = 0) -> dict:
    keys = jax.random.split(jax.random.key(seed), 10)
    return {
        "codebook_embed": centred(keys[0], (MB, FRAMES, CB, D), 1.0, 6.0, ((1, 16),)),
        "item_lengths": jax.vmap(lambda own: ragged(own, ITEMS, FR, LONGEST, 2))(jax.random.split(keys[1], MB * BLOCKS)).reshape((MB, BLOCKS, ITEMS)).astype(jnp.int32),
        "gain_attn": jnp.clip(1.0 + 0.1 * jax.random.normal(keys[2], (2, D), jnp.float32), 0.5, 1.5),
        "w_qkv": centred(keys[3], (2, D, 3 * D), D ** -0.5, 0.1875, ((0, 2),)),
        "w_out": centred(keys[4], (2, D, D), (D // 4) ** -0.5, 0.375, ((0, 2),)),
        "gain_mlp": jnp.clip(1.0 + 0.1 * jax.random.normal(keys[5], (2, D), jnp.float32), 0.5, 1.5),
        "w_up": centred(keys[6], (2, D, FF), D ** -0.5, 0.1875, ((0, 2),)),
        "w_down": centred(keys[7], (2, FF, D), FF ** -0.5, 0.09375, ((0, 2),)),
        "cotangent": centred(keys[8], (MB, FRAMES, CB, D), 1.0, 6.0, ((1, 16),)),
    }


@jax.custom_vjp
def low(v):
    return lax.optimization_barrier(v.astype(jnp.bfloat16)).astype(jnp.float32)

@jax.custom_vjp
def low_back(v):
    return v

def low_keep(v):
    return (low(v), None)

def low_pass(kept, grad):
    return (grad,)

def back_keep(v):
    return (v, None)

def back_low(kept, grad):
    return (low(grad),)
low.defvjp(low_keep, low_pass)
low_back.defvjp(back_keep, back_low)
EPSILON = 1e-05
PRECISE = lax.Precision.HIGHEST

def normalize(layer_in, gain):
    return layer_in * lax.rsqrt(lax.optimization_barrier(jnp.mean(layer_in * layer_in, axis=-1, keepdims=True)) + EPSILON) * gain

def product(left, right):
    return jnp.dot(left, right, precision=PRECISE)

def frame_mask(lengths, row_count):
    item_ends = jnp.cumsum(lengths)
    position = jnp.arange(row_count, dtype=jnp.int32)
    item_owner = lax.optimization_barrier(jnp.sum((position[:, None] >= item_ends[None, :]).astype(jnp.int32), axis=1))
    same_item = item_owner[:, None] == item_owner[None, :]
    return (same_item & (position[:, None] >= position[None, :]))[None, None]

def code_mask(length):
    position = jnp.arange(length, dtype=jnp.int32)
    return (position[:, None] >= position[None, :])[None, None]

def residual_block(layer_in, groups, allowed, gain_one, w_qkv, w_out, gain_two, w_up, w_down):
    row_count, features = layer_in.shape
    head_width = features // HEADS
    normed = low(normalize(layer_in, gain_one))
    packed = low(low_back(product(normed, w_qkv)))
    shaped = packed.reshape(groups, row_count // groups, 3, HEADS, head_width)
    queries, key_rows, values = (shaped[:, :, 0], shaped[:, :, 1], shaped[:, :, 2])
    scores = low_back(jnp.einsum('gqhd,gkhd->ghqk', queries, key_rows, precision=PRECISE) * head_width ** (-0.5))
    scores = jnp.where(allowed, scores, -1e+30)
    row_peak = lax.optimization_barrier(jnp.max(scores, axis=-1, keepdims=True))
    exponent = jnp.exp(scores - row_peak)
    attn_probs = low(exponent / lax.optimization_barrier(jnp.sum(exponent, axis=-1, keepdims=True)))
    mixture = jnp.einsum('ghqk,gkhd->gqhd', attn_probs, values, precision=PRECISE).reshape(row_count, features)
    middle = layer_in + low_back(product(low(low_back(mixture)), w_out))
    normed_two = low(normalize(middle, gain_two))
    hidden = low_back(product(normed_two, w_up))
    return middle + low_back(product(low(jax.nn.gelu(hidden)), w_down))

def one_buffer(weight_set, embed_rows, lengths):
    frames, books, features = embed_rows.shape
    global_set = tuple((matrix[0] for matrix in weight_set))
    local_set = tuple((matrix[1] for matrix in weight_set))
    frame_in = lax.optimization_barrier(jnp.sum(embed_rows, axis=1)) * books ** (-0.5)
    frame_out = residual_block(frame_in, 1, frame_mask(lengths, frames), *global_set)
    sent_states = low_back(low(frame_out))
    local_in = (embed_rows + sent_states[:, None, :]).reshape(frames * books, features)
    layer_out = residual_block(local_in, frames, code_mask(books), *local_set)
    return low(layer_out).reshape(frames, books, features)

def reference(codebook_embed, item_lengths, gain_attn, w_qkv, w_out, gain_mlp, w_up, w_down, cotangent):
    embed_rows = codebook_embed.astype(jnp.float32).reshape(MB * BLOCKS, FR, CB, D)
    lengths_all = item_lengths.reshape(MB * BLOCKS, ITEMS).astype(jnp.int32)
    weight_set = tuple((matrix.astype(jnp.float32) for matrix in (gain_attn, w_qkv, w_out, gain_mlp, w_up, w_down)))

    def forward(embed_all, weight_all):

        def per_buffer(buffer_pair):
            return one_buffer(weight_all, buffer_pair[0], buffer_pair[1])
        return lax.map(jax.checkpoint(per_buffer), (embed_all, lengths_all))
    layer_out, pullback = jax.vjp(forward, embed_rows, weight_set)
    embed_grad, weight_grads = pullback(cotangent.astype(jnp.float32).reshape(layer_out.shape))
    shape_out = (MB, FRAMES, CB, D)
    return (layer_out.astype(jnp.bfloat16).reshape(shape_out), embed_grad.reshape(shape_out), weight_grads[0], weight_grads[1], weight_grads[2], weight_grads[3], weight_grads[4], weight_grads[5])
```

```python
import functools

import jax
import jax.numpy as jnp
from jax import lax
from jax.experimental import pallas as pl
from jax.experimental.pallas import tpu as pltpu
from jax.sharding import PartitionSpec as P

HEADS = 16
EPSILON = 1e-05
BF16 = jnp.bfloat16
F32 = jnp.float32
GROUP = 4


def dot(left, right):
    return jnp.dot(left, right, preferred_element_type=F32)


def dot_t(left, right):
    return lax.dot_general(left, right, (((1,), (1,)), ((), ())), preferred_element_type=F32)


def t_dot(left, right):
    return lax.dot_general(left, right, (((0,), (0,)), ((), ())), preferred_element_type=F32)


def head_sum(product, reduce_mat):
    high = product.astype(BF16)
    low = (product - high.astype(F32)).astype(BF16)
    return dot(high, reduce_mat) + dot(low, reduce_mat)


def head_mats(lanes, width):
    row = lax.broadcasted_iota(jnp.int32, (lanes, 128), 0)
    col = lax.broadcasted_iota(jnp.int32, (lanes, 128), 1)
    reduce_mat = (row // width == col).astype(BF16)
    row = lax.broadcasted_iota(jnp.int32, (128, lanes), 0)
    col = lax.broadcasted_iota(jnp.int32, (128, lanes), 1)
    return reduce_mat, (col // width == row).astype(BF16)


def local_probs(q, k, reduce_mat, scale):
    probs = {}
    for a in range(len(q)):
        scores = [head_sum(q[a] * k[b], reduce_mat) * scale for b in range(a + 1)]
        peak = functools.reduce(jnp.maximum, scores)
        parts = [jnp.exp(s - peak) for s in scores]
        total = functools.reduce(lambda u, v: u + v, parts)
        for b in range(a + 1):
            probs[a, b] = parts[b] / total
    return probs


def local_attn_fwd_kernel(width, q_ref, k_ref, v_ref, o_ref):
    books, _, lanes = q_ref.shape
    reduce_mat, expand_mat = head_mats(lanes, width)
    q = [q_ref[a].astype(F32) for a in range(books)]
    k = [k_ref[a].astype(F32) for a in range(books)]
    v = [v_ref[a].astype(F32) for a in range(books)]
    probs = local_probs(q, k, reduce_mat, width**-0.5)
    for a in range(books):
        mixed = [dot(probs[a, b].astype(BF16), expand_mat) * v[b] for b in range(a + 1)]
        o_ref[a] = functools.reduce(lambda s, t: s + t, mixed).astype(BF16)


def local_attn_bwd_kernel(width, q_ref, k_ref, v_ref, g_ref, dq_ref, dk_ref, dv_ref):
    books, _, lanes = q_ref.shape
    scale = width**-0.5
    reduce_mat, expand_mat = head_mats(lanes, width)
    q = [q_ref[a].astype(F32) for a in range(books)]
    k = [k_ref[a].astype(F32) for a in range(books)]
    v = [v_ref[a].astype(F32) for a in range(books)]
    g = [g_ref[a].astype(F32) for a in range(books)]
    probs = local_probs(q, k, reduce_mat, scale)
    dq = [0.0] * books
    dk = [0.0] * books
    dv = [0.0] * books
    for a in range(books):
        dprobs = [head_sum(g[a] * v[b], reduce_mat) for b in range(a + 1)]
        inner = functools.reduce(
            lambda s, t: s + t, [dprobs[b] * probs[a, b] for b in range(a + 1)]
        )
        for b in range(a + 1):
            dscore = dot((probs[a, b] * (dprobs[b] - inner)).astype(BF16), expand_mat)
            dq[a] = dq[a] + dscore * k[b]
            dk[b] = dk[b] + dscore * q[a]
            dv[b] = dv[b] + dot(probs[a, b].astype(BF16), expand_mat) * g[a]
    for a in range(books):
        dq_ref[a] = (dq[a] * scale).astype(BF16)
        dk_ref[a] = (dk[a] * scale).astype(BF16)
        dv_ref[a] = dv[a].astype(BF16)


def local_attn(packed, books, grads=None):
    micros, _, frames, wide = packed.shape
    features = wide // 3
    width = features // HEADS
    lanes = GROUP * width
    groups = features // lanes

    def spec(part):
        return pl.BlockSpec(
            (None, books, frames, lanes), lambda m, h: (m, 0, 0, part * groups + h)
        )

    own = spec(0)
    shape = jax.ShapeDtypeStruct((micros, books, frames, features), BF16)
    if grads is None:
        return pl.pallas_call(
            functools.partial(local_attn_fwd_kernel, width),
            grid=(micros, groups),
            in_specs=[spec(0), spec(1), spec(2)],
            out_specs=own,
            out_shape=shape,
            name="local_attn_fwd",
        )(packed, packed, packed)
    return pl.pallas_call(
        functools.partial(local_attn_bwd_kernel, width),
        grid=(micros, groups),
        in_specs=[spec(0), spec(1), spec(2), own],
        out_specs=[own] * 3,
        out_shape=[shape] * 3,
        name="local_attn_bwd",
    )(packed, packed, packed, grads)


def item_mask(lengths_ref, micro, frames, items):
    row = lax.broadcasted_iota(jnp.int32, (frames, frames), 0)
    col = lax.broadcasted_iota(jnp.int32, (frames, frames), 1)
    row_item = jnp.zeros((frames, frames), jnp.int32)
    col_item = jnp.zeros((frames, frames), jnp.int32)
    end = 0
    for i in range(items):
        end = end + lengths_ref[micro, 0, i]
        row_item = row_item + (row >= end).astype(jnp.int32)
        col_item = col_item + (col >= end).astype(jnp.int32)
    return (row_item == col_item) & (row >= col)


def head_parts(block, width):
    per = 128 // width
    lane = lax.broadcasted_iota(jnp.int32, (block.shape[0], 128), 1)
    parts = []
    for h in range(block.shape[1] // width):
        tile = block[:, (h // per) * 128 : (h // per + 1) * 128]
        parts.append(jnp.where(lane // width == h % per, tile, jnp.zeros_like(tile)))
    return parts


def frame_probs(q, k, mask, scale):
    scores = jnp.where(mask, dot_t(q, k) * scale, -1e30)
    parts = jnp.exp(scores - jnp.max(scores, axis=-1, keepdims=True))
    return parts / jnp.sum(parts, axis=-1, keepdims=True)


def global_attn_fwd_kernel(width, items, lengths_ref, q_ref, k_ref, v_ref, o_ref):
    frames, lanes = q_ref.shape
    mask = item_mask(lengths_ref, pl.program_id(0), frames, items)
    per = 128 // width
    q = head_parts(q_ref[...], width)
    v = head_parts(v_ref[...], width)
    mixed = [0.0] * (lanes // 128)
    for h in range(lanes // width):
        tile = slice((h // per) * 128, (h // per + 1) * 128)
        probs = frame_probs(q[h], k_ref[:, tile], mask, width**-0.5)
        mixed[h // per] = mixed[h // per] + dot(probs.astype(BF16), v[h])
    for i, tile in enumerate(mixed):
        o_ref[:, i * 128 : (i + 1) * 128] = tile.astype(BF16)


def global_attn_bwd_kernel(
    width, items, lengths_ref, q_ref, k_ref, v_ref, g_ref, dq_ref, dk_ref, dv_ref
):
    frames, lanes = q_ref.shape
    scale = width**-0.5
    mask = item_mask(lengths_ref, pl.program_id(0), frames, items)
    per = 128 // width
    q = head_parts(q_ref[...], width)
    k = head_parts(k_ref[...], width)
    g = head_parts(g_ref[...], width)
    tiles = lanes // 128
    dq, dk, dv = [0.0] * tiles, [0.0] * tiles, [0.0] * tiles
    for h in range(lanes // width):
        t = h // per
        tile = slice(t * 128, (t + 1) * 128)
        probs = frame_probs(q[h], k_ref[:, tile], mask, scale)
        dv[t] = dv[t] + t_dot(probs.astype(BF16), g[h])
        dprobs = dot_t(g[h], v_ref[:, tile])
        inner = jnp.sum(dprobs * probs, axis=-1, keepdims=True)
        dscore = (probs * (dprobs - inner)).astype(BF16)
        dq[t] = dq[t] + dot(dscore, k[h])
        dk[t] = dk[t] + t_dot(dscore, q[h])
    for t in range(tiles):
        tile = slice(t * 128, (t + 1) * 128)
        dq_ref[:, tile] = (dq[t] * scale).astype(BF16)
        dk_ref[:, tile] = (dk[t] * scale).astype(BF16)
        dv_ref[:, tile] = dv[t].astype(BF16)


def global_attn(packed, lengths, grads=None):
    micros, frames, wide = packed.shape
    features = wide // 3
    width = features // HEADS
    lanes = GROUP * width
    groups = features // lanes
    items = lengths.shape[-1]

    def spec(part):
        return pl.BlockSpec((None, frames, lanes), lambda m, h, _: (m, 0, part * groups + h))

    own = spec(0)
    shape = jax.ShapeDtypeStruct((micros, frames, features), BF16)
    operands = (lengths, packed, packed, packed)
    if grads is None:
        kernel, ins, outs, shapes = global_attn_fwd_kernel, [], own, shape
    else:
        kernel, ins, outs, shapes = global_attn_bwd_kernel, [own], [own] * 3, [shape] * 3
        operands = operands + (grads,)
    return pl.pallas_call(
        functools.partial(kernel, width, items),
        grid_spec=pltpu.PrefetchScalarGridSpec(
            num_scalar_prefetch=1,
            grid=(micros, groups),
            in_specs=[spec(0), spec(1), spec(2)] + ins,
            out_specs=outs,
        ),
        out_shape=shapes,
        name="global_attn_fwd" if grads is None else "global_attn_bwd",
    )(*operands)


def rstd(rows):
    return lax.rsqrt(jnp.mean(rows * rows, axis=-1, keepdims=True) + EPSILON)


def gelu_parts(hidden):
    c = 0.7978845608028654
    square = hidden * hidden
    t = jnp.tanh(c * hidden * (1.0 + 0.044715 * square))
    value = 0.5 * hidden * (1.0 + t)
    slope = 0.5 * (1.0 + t) + 0.5 * hidden * (1.0 - t * t) * c * (1.0 + 3 * 0.044715 * square)
    return value.astype(BF16), slope.astype(BF16)


def layer_forward(weights, rows, attend):
    gain_one, w_qkv, w_out, gain_two, w_up, w_down = weights
    normed = (rows * rstd(rows) * gain_one).astype(BF16)
    packed = dot(normed, w_qkv).astype(BF16)
    mixture = attend(packed)
    middle = rows + dot(mixture, w_out)
    normed_two = (middle * rstd(middle) * gain_two).astype(BF16)
    active, slope = gelu_parts(dot(normed_two, w_up))
    result = middle + dot(active, w_down)
    return result, (rows, normed, packed, mixture, middle, normed_two, active, slope)


def norm_backward(grad, rows, gain):
    scale = rstd(rows)
    plain = rows * scale
    grad_gain = jnp.sum(grad * plain, axis=0)
    lead = grad * gain
    return scale * (lead - plain * jnp.mean(lead * plain, axis=-1, keepdims=True)), grad_gain


def layer_backward(weights, stored, low_out, grad_out, attend_back, reduce):
    gain_one, w_qkv, w_out, gain_two, w_up, w_down = weights
    rows, normed, packed, mixture, middle, normed_two, active, slope = stored
    grad_down = reduce(active, low_out)
    grad_hidden = (slope.astype(F32) * dot_t(low_out, w_down)).astype(BF16)
    grad_up = reduce(normed_two, grad_hidden)
    grad_middle, grad_gain_two = norm_backward(dot_t(grad_hidden, w_up), middle, gain_two)
    grad_middle = grad_middle + grad_out
    low_middle = grad_middle.astype(BF16)
    grad_wout = reduce(mixture, low_middle)
    grad_packed = attend_back(packed, dot_t(low_middle, w_out).astype(BF16))
    grad_qkv = reduce(normed, grad_packed)
    grad_in, grad_gain_one = norm_backward(dot_t(grad_packed, w_qkv), rows, gain_one)
    grads = (grad_gain_one, grad_qkv, grad_wout, grad_gain_two, grad_up, grad_down)
    return grad_in + grad_middle, grads


def swap(size, by):
    return [(i, i ^ by) for i in range(size)]


class Reducer:
    def __init__(self, core, size, spots):
        self.core, self.size = core, size
        self.index = lax.axis_index("dp")
        self.spots = spots
        self.depth = size // 4

    def permute(self, array, pairs):
        base = self.core * self.size
        return lax.ppermute(array, ("section", "dp"), [(base + i, base + j) for i, j in pairs])

    def quarters(self, left):
        rows, columns = left.shape
        block = columns // self.size
        if block % 128 == 0:
            split = left.reshape(rows, self.depth, 2, 2, block)
            x, y = self.index % 2, (self.index // 2) % 2
            out = {}
            for dy in range(2):
                for dx in range(2):
                    one = lax.dynamic_index_in_dim(split, y ^ dy, 2, keepdims=False)
                    one = lax.dynamic_index_in_dim(one, x ^ dx, 2, keepdims=False)
                    out[dx, dy] = one.reshape(rows, self.depth * block)
            return out
        placed = dot(left, self.spots(columns)).astype(BF16)
        wide = self.depth * block
        return {
            (dx, dy): placed[:, (2 * dy + dx) * wide : (2 * dy + dx + 1) * wide]
            for dy in range(2)
            for dx in range(2)
        }

    def half(self, left, right, by_first, by_second, far, near):
        first = self.permute(t_dot(left[1, 1], right).astype(BF16), swap(self.size, by_first))
        second = self.permute(t_dot(left[near], right).astype(BF16), swap(self.size, by_first))
        onward = (t_dot(left[far], right) + first.astype(F32)).astype(BF16)
        onward = self.permute(onward, swap(self.size, by_second))
        return (t_dot(left[0, 0], right) + second.astype(F32) + onward.astype(F32)).astype(BF16)

    def along_z(self, total):
        if self.depth != 4:
            groups = [[4 * z + place for z in range(self.depth)] for place in range(4)]
            return lax.psum_scatter(
                total, "dp", scatter_dimension=0, axis_index_groups=groups, tiled=True
            )[0].astype(F32)
        z = self.index // 4

        def piece(at):
            return lax.dynamic_index_in_dim(
                total, jnp.clip(at, 0, self.depth - 1), 0, keepdims=False
            )

        up = down = None
        for step in range(1, self.depth):
            send_up = piece(self.depth - step + z)
            send_down = piece(z - self.depth + step)
            if up is not None:
                send_up = (send_up.astype(F32) + up.astype(F32)).astype(BF16)
                send_down = (send_down.astype(F32) + down.astype(F32)).astype(BF16)
            pairs = [(4 * k + i, 4 * k + 4 + i) for k in range(step) for i in range(4)]
            up = self.permute(send_up, pairs)
            last = self.size - 1
            down = self.permute(send_down, [(last - i, last - j) for i, j in pairs])
        return piece(z).astype(F32) + up.astype(F32) + down.astype(F32)

    def __call__(self, left, right):
        parts = right.shape[1] // 2
        quarters = self.quarters(left)
        total = jnp.concatenate(
            [
                self.half(quarters, right[:, :parts], 1, 2, (0, 1), (1, 0)),
                self.half(quarters, right[:, parts:], 2, 1, (1, 0), (0, 1)),
            ],
            axis=1,
        )
        return self.along_z(total.reshape(self.depth, -1, right.shape[1]))


def spots_of(size):
    index = lax.axis_index("dp")
    kept = {}

    def spots(columns):
        if columns not in kept:
            block, depth = columns // size, size // 4
            source = lax.broadcasted_iota(jnp.int32, (columns, columns), 0)
            target = lax.broadcasted_iota(jnp.int32, (columns, columns), 1)
            place = target // (depth * block)
            z = (target // block) % depth
            at = (z * 4 + (place ^ (index % 4))) * block + target % block
            kept[columns] = (source == at).astype(BF16)
        return kept[columns]

    return spots


def sum_over_dp(array, size):
    if size & (size - 1):
        return lax.psum(array, "dp")
    by = 1
    while by < size:
        array = array + lax.ppermute(array, "dp", swap(size, by))
        by *= 2
    return array


def local(codebook_embed, item_lengths, gain_attn, w_qkv, w_out, gain_mlp, w_up, w_down, cotangent):
    section = lax.axis_index("section")
    size = lax.axis_size("dp")
    first_core = section == 0
    weights = (gain_attn[0], w_qkv[0], w_out[0], gain_mlp[0], w_up[0], w_down[0])
    micros, frames, books, features = codebook_embed.shape
    scale_in = books**-0.5
    half_width = features // 2
    spots = spots_of(size)

    embed = codebook_embed.transpose(0, 2, 1, 3).astype(F32)
    upstream = cotangent.transpose(0, 2, 1, 3).reshape(-1, features)

    frame_in = (jnp.sum(embed, axis=1) * scale_in).reshape(-1, features)
    frame_out, frame_kept = layer_forward(
        weights,
        frame_in,
        lambda packed: global_attn(
            packed.reshape(micros, frames, -1), item_lengths
        ).reshape(-1, features),
    )
    states = lax.ppermute(frame_out.astype(BF16), "section", [(0, 1)])
    states = states.astype(F32).reshape(micros, 1, frames, features)
    local_in = (embed + states).reshape(-1, features)
    local_out, local_kept = layer_forward(
        weights,
        local_in,
        lambda packed: local_attn(
            packed.reshape(micros, books, frames, -1), books
        ).reshape(-1, features),
    )
    local_out = local_out.astype(BF16)
    other_half = lax.ppermute(local_out[:, :half_width], "section", [(1, 0)])
    own_half = jnp.where(first_core, other_half, local_out[:, half_width:])

    def local_back(packed, grads):
        parts = local_attn(
            packed.reshape(micros, books, frames, -1),
            books,
            grads.reshape(micros, books, frames, -1),
        )
        return jnp.concatenate(parts, axis=-1).reshape(-1, 3 * features)

    def global_back(packed, grads):
        parts = global_attn(
            packed.reshape(micros, frames, -1), item_lengths, grads.reshape(micros, frames, -1)
        )
        return jnp.concatenate(parts, axis=-1).reshape(-1, 3 * features)

    local_grad, local_terms = layer_backward(
        weights, local_kept, upstream, upstream.astype(F32), local_back, Reducer(1, size, spots)
    )
    local_grad = local_grad.reshape(micros, books, frames, features)
    frame_grad = jnp.sum(local_grad, axis=1).astype(BF16).reshape(-1, features)
    frame_grad = lax.ppermute(frame_grad, "section", [(1, 0)])
    global_grad, global_terms = layer_backward(
        weights, frame_kept, frame_grad, frame_grad.astype(F32), global_back, Reducer(0, size, spots)
    )
    global_grad = (global_grad * scale_in).reshape(micros, 1, frames, features)

    sent_local = lax.ppermute(local_grad[..., :half_width].astype(BF16), "section", [(1, 0)])
    sent_global = lax.ppermute(global_grad[..., half_width:].astype(BF16), "section", [(0, 1)])
    embed_grad = jnp.where(
        first_core, sent_local.astype(F32), local_grad[..., half_width:]
    ) + jnp.where(first_core, global_grad[..., :half_width], sent_global.astype(F32))

    terms = [jnp.where(first_core, g, l) for g, l in zip(global_terms, local_terms)]
    gains = sum_over_dp(jnp.stack([terms[0], terms[3]]), size).reshape(2, size, -1)
    gains = lax.dynamic_index_in_dim(gains, lax.axis_index("dp"), 1, keepdims=False)

    def placed(rows):
        return rows.reshape(micros, books, frames, -1).transpose(0, 2, 1, 3)

    return (
        placed(own_half),
        placed(embed_grad),
        gains[:1],
        terms[1][None],
        terms[2][None],
        gains[1:],
        terms[4][None],
        terms[5][None],
    )


def solution(mesh):
    in_specs = (
        P(None, "dp", None, None),
        P(None, "dp", None),
        P("section", None),
        P("section", None, None),
        P("section", None, None),
        P("section", None),
        P("section", None, None),
        P("section", None, None),
        P(None, "dp", None, None),
    )
    out_specs = (
        P(None, "dp", None, "section"),
        P(None, "dp", None, "section"),
        P("section", "dp"),
        P("section", "dp", None),
        P("section", "dp", None),
        P("section", "dp"),
        P("section", "dp", None),
        P("section", "dp", None),
    )
    return jax.shard_map(local, mesh=mesh, in_specs=in_specs, out_specs=out_specs, check_vma=False)
```

```python
import functools

import jax
import jax.numpy as jnp
from jax import lax
from jax.experimental import pallas as pl
from jax.experimental.pallas import tpu as pltpu
from jax.sharding import PartitionSpec as P

HEADS = 16
EPSILON = 1e-05
BF16 = jnp.bfloat16
F32 = jnp.float32
VMEM_LIMIT = 48 * 1024 * 1024
CHUNK = 128
UNIT = 256


def dot(left, right):
    return jnp.dot(left, right, preferred_element_type=F32)


def dot_t(left, right):
    return lax.dot_general(left, right, (((1,), (1,)), ((), ())), preferred_element_type=F32)


def t_dot(left, right):
    return lax.dot_general(left, right, (((0,), (0,)), ((), ())), preferred_element_type=F32)


def add_all(terms):
    return functools.reduce(lambda s, t: s + t, terms)


def whole(shape):
    return pl.BlockSpec(shape, lambda *_: (0,) * len(shape))


def params():
    return pltpu.CompilerParams(vmem_limit_bytes=VMEM_LIMIT)


def sds(shape, dtype=BF16):
    return jax.ShapeDtypeStruct(shape, dtype)


def cost(flops, size):
    return pl.CostEstimate(flops=flops, bytes_accessed=size, transcendentals=0)


def weight_specs(weight, block, index):
    if not isinstance(weight, tuple):
        return [pl.BlockSpec(block, index)], [weight]

    def spec(place):
        def at(j, s):
            return tuple(jnp.where(s[0] == place, i, 0) for i in index(j, s))

        return pl.BlockSpec(block, at)

    return [spec(0), spec(1)], list(weight)


def read(core, refs):
    if len(refs) == 1:
        return refs[0][...]
    return jnp.where(core == 0, refs[0][...], refs[1][...])


def layer_call(kernel, name, core, grid, operands, outs, scratch, flops):
    specs, arrays, counts = [], [], []
    for operand in operands:
        if len(operand) == 3:
            more, given = weight_specs(*operand)
        else:
            more, given = [operand[1]], [operand[0]]
        specs, arrays = specs + more, arrays + given
        counts.append(len(given))

    def body(core_ref, *refs):
        refs, groups = list(refs), []
        for count in counts:
            groups.append(refs[:count])
            refs = refs[count:]
        kernel(core_ref[0], groups, *refs)

    size = sum(a.size * a.dtype.itemsize for a in arrays)
    size += sum(o.size * o.dtype.itemsize for o, _ in outs)
    return pl.pallas_call(
        body,
        grid_spec=pltpu.PrefetchScalarGridSpec(
            num_scalar_prefetch=1,
            grid=(grid,),
            in_specs=specs,
            out_specs=[spec for _, spec in outs],
            scratch_shapes=scratch,
        ),
        out_shape=[o for o, _ in outs],
        compiler_params=params(),
        cost_estimate=cost(flops, size),
        name=name,
    )(core, *arrays)


def rstd(rows):
    return lax.rsqrt(jnp.mean(rows * rows, axis=-1, keepdims=True) + EPSILON)


def by_chunks(rows, step):
    def one(i, carry):
        step(pl.ds(pl.multiple_of(i * CHUNK, CHUNK), CHUNK))
        return carry

    lax.fori_loop(0, rows // CHUNK, one, 0)


def norm_backward(grad, rows, gain):
    scale = rstd(rows)
    plain = rows * scale
    grad_gain = jnp.sum(grad * plain, axis=0, keepdims=True)
    lead = grad * gain
    return scale * (lead - plain * jnp.mean(lead * plain, axis=-1, keepdims=True)), grad_gain


def gelu_parts(hidden):
    c = 0.7978845608028654
    square = hidden * hidden
    t = jnp.tanh(hidden * (c + (c * 0.044715) * square))
    half = 0.5 + 0.5 * t
    slope = half + (hidden * half) * ((1.0 - t) * (c + (3 * 0.044715 * c) * square))
    return (hidden * half).astype(BF16), slope.astype(BF16)


def qkv_forward(core, rows, gain, w_qkv, tile=1024):
    count, features = rows.shape
    wide = 3 * features

    def kernel(core, ins, h_ref, p_ref):
        (x_ref,), gain_refs, w_refs = ins

        @pl.when(pl.program_id(0) == 0)
        def _():
            gain = read(core, gain_refs)

            def step(at):
                x = x_ref[at, :]
                h_ref[at, :] = (x * rstd(x) * gain).astype(BF16)

            by_chunks(count, step)

        p_ref[...] = dot(h_ref[...], read(core, w_refs)).astype(BF16)

    return layer_call(
        kernel,
        "qkv_forward",
        core,
        wide // tile,
        [
            (rows, whole(rows.shape)),
            (gain, (1, features), lambda j, s: (0, 0)),
            (w_qkv, (features, tile), lambda j, s: (0, j)),
        ],
        [
            (sds(rows.shape), whole(rows.shape)),
            (sds((count, wide)), pl.BlockSpec((count, tile), lambda j, s: (0, j))),
        ],
        [],
        2 * count * features * wide,
    )


def mlp_forward(core, rows, mixture, w_out, gain, w_up, w_down, joined, tile=1024):
    count, features = rows.shape
    wide = (w_up[0] if isinstance(w_up, tuple) else w_up).shape[1]

    def kernel(core, ins, m_ref, h_ref, *refs):
        (x_ref,), (o_ref,), wout_refs, gain_refs, wup_refs, wdown_refs = ins
        y_ref, acc_ref = refs[-2:]

        @pl.when(pl.program_id(0) == 0)
        def _():
            gain, w_out = read(core, gain_refs), read(core, wout_refs)

            def step(at):
                m = x_ref[at, :] + dot(o_ref[at, :], w_out)
                m_ref[at, :] = m
                acc_ref[at, :] = m
                h_ref[at, :] = (m * rstd(m) * gain).astype(BF16)

            by_chunks(count, step)

        g, slope = gelu_parts(dot(h_ref[...], read(core, wup_refs)))
        if joined:
            refs[0][0] = g
            refs[0][1] = slope
        else:
            refs[0][0] = g
            refs[1][0] = slope
        acc_ref[...] += dot(g, read(core, wdown_refs))

        @pl.when(pl.program_id(0) == pl.num_programs(0) - 1)
        def _():
            y_ref[...] = acc_ref[...].astype(BF16)

    planes = 2 if joined else 1
    wide_out = (sds((planes, count, wide)), pl.BlockSpec((planes, count, tile), lambda j, s: (0, 0, j)))
    same = whole(rows.shape)
    return layer_call(
        kernel,
        "mlp_forward",
        core,
        wide // tile,
        [
            (rows, same),
            (mixture, same),
            (w_out, (features, features), lambda j, s: (0, 0)),
            (gain, (1, features), lambda j, s: (0, 0)),
            (w_up, (features, tile), lambda j, s: (0, j)),
            (w_down, (tile, features), lambda j, s: (j, 0)),
        ],
        [(sds(rows.shape, F32), same), (sds(rows.shape), same)]
        + [wide_out] * (3 - planes)
        + [(sds(rows.shape), same)],
        [pltpu.VMEM(rows.shape, F32)],
        2 * count * features * (features + 2 * wide),
    )


def mlp_backward(core, low_out, slope, middle, w_out, gain, w_up, w_down, tile=1024):
    count, features = low_out.shape
    wide = slope[0].shape[2]
    tiles = wide // tile
    half = tiles // 2

    def kernel(core, ins, own_ref, other_ref, dm_ref, low_ref, do_ref, gg_ref, acc_ref):
        (dy_ref,), (s_ref,), (m_ref,), gain_refs, wdown_refs, wup_refs, wout_refs = ins
        j = pl.program_id(0)
        dz = (s_ref[0].astype(F32) * dot_t(dy_ref[...], read(core, wdown_refs))).astype(BF16)

        @pl.when(j < half)
        def _():
            other_ref[0] = dz

        @pl.when(j >= half)
        def _():
            own_ref[0] = dz

        term = dot_t(dz, read(core, wup_refs))

        @pl.when(j == 0)
        def _():
            acc_ref[...] = term

        @pl.when(j > 0)
        def _():
            acc_ref[...] += term

        @pl.when(j == tiles - 1)
        def _():
            gg_ref[...] = jnp.zeros_like(gg_ref)
            gain, w_out = read(core, gain_refs), read(core, wout_refs)

            def step(at):
                dm, gg = norm_backward(acc_ref[at, :], m_ref[0, at, :].astype(F32), gain)
                gg_ref[...] += gg
                dm = dm + dy_ref[at, :].astype(F32)
                dm_ref[at, :] = dm
                low = dm.astype(BF16)
                low_ref[at, :] = low
                do_ref[at, :] = dot_t(low, w_out).astype(BF16)

            by_chunks(count, step)

    def at(j, s):
        return (j + (1 - s[0]) * half) % tiles

    same = whole(low_out.shape)
    return layer_call(
        kernel,
        "mlp_backward",
        core,
        tiles,
        [
            (low_out, same),
            (
                slope[0],
                pl.BlockSpec(
                    (1, count, tile), lambda j, s: (slope[1], s[0] * slope[2], at(j, s))
                ),
            ),
            (
                middle[0],
                pl.BlockSpec(
                    (1, count, features), lambda j, s: (middle[1], s[0] * middle[2], 0)
                ),
            ),
            (gain, (1, features), lambda j, s: (0, 0)),
            (w_down, (tile, features), lambda j, s: (at(j, s), 0)),
            (w_up, (features, tile), lambda j, s: (0, at(j, s))),
            (w_out, (features, features), lambda j, s: (0, 0)),
        ],
        [
            (
                sds((1, count, wide // 2)),
                pl.BlockSpec((1, count, tile), lambda j, s: (0, 0, jnp.maximum(j - half, 0))),
            ),
            (
                sds((1, count, wide // 2)),
                pl.BlockSpec((1, count, tile), lambda j, s: (0, 0, jnp.minimum(j, half - 1))),
            ),
            (sds(low_out.shape, F32), same),
            (sds(low_out.shape), same),
            (sds(low_out.shape), same),
            (sds((1, features), F32), whole((1, features))),
        ],
        [pltpu.VMEM(low_out.shape, F32)],
        2 * count * features * (features + 2 * wide),
    )


def qkv_backward(core, own, other, rows, grad_middle, gain, w_qkv, books, tile=512):
    count, features = rows.shape
    frames = count // books

    def kernel(core, ins, dx_ref, sum_ref, gg_ref, acc_ref):
        (own_ref,), (other_ref,), (x_ref,), (dm_ref,), gain_refs, w_refs = ins
        w = read(core, w_refs)
        j = pl.program_id(0)
        terms = []
        for i in range(3):
            part = jnp.where(core == i // 2, own_ref[i % 2], other_ref[i % 2])
            terms.append(dot_t(part, w[:, i * features : (i + 1) * features]))
        acc_ref[:, pl.ds(pl.multiple_of(j * tile, tile), tile)] = add_all(terms)

        @pl.when(j == pl.num_programs(0) - 1)
        def _():
            gg_ref[...] = jnp.zeros_like(gg_ref)
            gain = read(core, gain_refs)
            total = 0.0
            for b in range(books):
                at = slice(b * frames, (b + 1) * frames)
                dx, gg = norm_backward(acc_ref[at, :], x_ref[at, :], gain)
                gg_ref[...] += gg
                dx = dx + dm_ref[at, :]
                dx_ref[at, :] = dx
                total = total + dx
            sum_ref[...] = total.astype(BF16)

    same = whole(rows.shape)
    return layer_call(
        kernel,
        "qkv_backward",
        core,
        features // tile,
        [
            (own, whole(own.shape)),
            (other, whole(other.shape)),
            (rows, same),
            (grad_middle, same),
            (gain, (1, features), lambda j, s: (0, 0)),
            (w_qkv, (tile, 3 * features), lambda j, s: (j, 0)),
        ],
        [
            (sds(rows.shape, F32), same),
            (sds((frames, features)), whole((frames, features))),
            (sds((1, features), F32), whole((1, features))),
        ],
        [pltpu.VMEM(rows.shape, F32)],
        6 * count * features * features,
    )


def head_sum(product, reduce_mat):
    high = product.astype(BF16)
    low = (product - high.astype(F32)).astype(BF16)
    return dot(high, reduce_mat) + dot(low, reduce_mat)


def head_mats(lanes, width):
    row = lax.broadcasted_iota(jnp.int32, (lanes, 128), 0)
    col = lax.broadcasted_iota(jnp.int32, (lanes, 128), 1)
    reduce_mat = (row // width == col).astype(BF16)
    row = lax.broadcasted_iota(jnp.int32, (128, lanes), 0)
    col = lax.broadcasted_iota(jnp.int32, (128, lanes), 1)
    return reduce_mat, (col // width == row).astype(BF16)


def local_probs(q, k, reduce_mat, scale):
    probs = {}
    for a in range(len(q)):
        scores = [head_sum(q[a] * k[b], reduce_mat) * scale for b in range(a + 1)]
        peak = functools.reduce(jnp.maximum, scores)
        parts = [jnp.exp(s - peak) for s in scores]
        total = add_all(parts)
        for b in range(a + 1):
            probs[a, b] = parts[b] / total
    return probs


def local_attn_fwd_kernel(width, q_ref, k_ref, v_ref, o_ref):
    books, _, lanes = q_ref.shape
    reduce_mat, expand_mat = head_mats(lanes, width)
    q = [q_ref[a].astype(F32) for a in range(books)]
    k = [k_ref[a].astype(F32) for a in range(books)]
    v = [v_ref[a].astype(F32) for a in range(books)]
    probs = local_probs(q, k, reduce_mat, width**-0.5)
    for a in range(books):
        mixed = [dot(probs[a, b].astype(BF16), expand_mat) * v[b] for b in range(a + 1)]
        o_ref[a] = add_all(mixed).astype(BF16)


def by_half(core, parts, own_ref, other_ref):
    for c in range(2):

        @pl.when(core == c)
        def _():
            for i in range(2):
                own_ref[i] = parts[2 * c + i]
                other_ref[i] = parts[2 - 2 * c + i]


def local_attn_bwd_kernel(
    width, core_ref, q_ref, k_ref, v_ref, g_ref, m_ref, own_ref, other_ref
):
    books, _, lanes = q_ref.shape
    scale = width**-0.5
    reduce_mat, expand_mat = head_mats(lanes, width)
    q = [q_ref[a].astype(F32) for a in range(books)]
    k = [k_ref[a].astype(F32) for a in range(books)]
    v = [v_ref[a].astype(F32) for a in range(books)]
    g = [g_ref[a].astype(F32) for a in range(books)]
    probs = local_probs(q, k, reduce_mat, scale)
    dq = [0.0] * books
    dk = [0.0] * books
    dv = [0.0] * books
    for a in range(books):
        dprobs = [head_sum(g[a] * v[b], reduce_mat) for b in range(a + 1)]
        inner = add_all([dprobs[b] * probs[a, b] for b in range(a + 1)])
        for b in range(a + 1):
            dscore = dot((probs[a, b] * (dprobs[b] - inner)).astype(BF16), expand_mat)
            dq[a] = dq[a] + dscore * k[b]
            dk[b] = dk[b] + dscore * q[a]
            dv[b] = dv[b] + dot(probs[a, b].astype(BF16), expand_mat) * g[a]
    parts = [
        jnp.stack([(one * by).astype(BF16) for one in ones])
        for ones, by in ((dq, scale), (dk, scale), (dv, 1.0))
    ]
    by_half(core_ref[0], parts + [m_ref[...]], own_ref, other_ref)


def local_attn(packed, books, core=None, grads=None, lanes=256):
    count, wide = packed.shape
    features, frames = wide // 3, count // books
    width, groups = features // HEADS, features // lanes
    packed = packed.reshape(books, frames, wide)
    shape = (books, frames, features)

    def spec(part):
        return pl.BlockSpec((books, frames, lanes), lambda h, *_: (0, 0, part * groups + h))

    ins = [spec(0), spec(1), spec(2)]
    if grads is None:
        out = pl.pallas_call(
            functools.partial(local_attn_fwd_kernel, width),
            grid=(groups,),
            in_specs=ins,
            out_specs=spec(0),
            out_shape=sds(shape),
            compiler_params=params(),
            cost_estimate=cost(2000 * count * features, 8 * count * features),
            name="local_attn_forward",
        )(packed, packed, packed)
        return out.reshape(count, features)
    half = pl.BlockSpec((2, books, frames, lanes), lambda h, _: (0, 0, 0, h))
    out = pl.pallas_call(
        functools.partial(local_attn_bwd_kernel, width),
        grid_spec=pltpu.PrefetchScalarGridSpec(
            num_scalar_prefetch=1,
            grid=(groups,),
            in_specs=ins + [spec(0)] * 2,
            out_specs=[half] * 2,
        ),
        out_shape=[sds((2,) + shape)] * 2,
        compiler_params=params(),
        cost_estimate=cost(4000 * count * features, 16 * count * features),
        name="local_attn_backward",
    )(core, packed, packed, packed, grads[0].reshape(shape), grads[1].reshape(shape))
    return [one.reshape(2, count, features) for one in out]


def item_mask(lengths_ref, micro, frames, items):
    row = lax.broadcasted_iota(jnp.int32, (frames, frames), 0)
    col = lax.broadcasted_iota(jnp.int32, (frames, frames), 1)
    row_item = jnp.zeros((frames, frames), jnp.int32)
    col_item = jnp.zeros((frames, frames), jnp.int32)
    end = 0
    for i in range(items):
        end = end + lengths_ref[micro, 0, i]
        row_item = row_item + (row >= end).astype(jnp.int32)
        col_item = col_item + (col >= end).astype(jnp.int32)
    return (row_item == col_item) & (row >= col)


def head_parts(block, width):
    per = 128 // width
    lane = lax.broadcasted_iota(jnp.int32, (block.shape[0], 128), 1)
    parts = []
    for h in range(block.shape[1] // width):
        tile = block[:, (h // per) * 128 : (h // per + 1) * 128]
        parts.append(jnp.where(lane // width == h % per, tile, jnp.zeros_like(tile)))
    return parts


def frame_probs(q, k, mask, scale):
    scores = jnp.where(mask, dot_t(q, k) * scale, -1e30)
    parts = jnp.exp(scores - jnp.max(scores, axis=-1, keepdims=True))
    return parts / jnp.sum(parts, axis=-1, keepdims=True)


def global_attn_fwd_kernel(width, items, lengths_ref, q_ref, k_ref, v_ref, o_ref):
    frames, lanes = q_ref.shape
    mask = item_mask(lengths_ref, pl.program_id(0), frames, items)
    per = 128 // width
    q = head_parts(q_ref[...], width)
    v = head_parts(v_ref[...], width)
    mixed = [0.0] * (lanes // 128)
    for h in range(lanes // width):
        tile = slice((h // per) * 128, (h // per + 1) * 128)
        probs = frame_probs(q[h], k_ref[:, tile], mask, width**-0.5)
        mixed[h // per] = mixed[h // per] + dot(probs.astype(BF16), v[h])
    for i, tile in enumerate(mixed):
        o_ref[:, i * 128 : (i + 1) * 128] = tile.astype(BF16)


def global_attn_bwd_kernel(
    width, items, core_ref, lengths_ref, q_ref, k_ref, v_ref, g_ref, m_ref, own_ref, other_ref
):
    frames, lanes = q_ref.shape
    scale = width**-0.5
    mask = item_mask(lengths_ref, core_ref[0], frames, items)
    per = 128 // width
    q = head_parts(q_ref[...], width)
    k = head_parts(k_ref[...], width)
    g = head_parts(g_ref[...], width)
    tiles = lanes // 128
    dq, dk, dv = [0.0] * tiles, [0.0] * tiles, [0.0] * tiles
    for h in range(lanes // width):
        t = h // per
        tile = slice(t * 128, (t + 1) * 128)
        probs = frame_probs(q[h], k_ref[:, tile], mask, scale)
        dv[t] = dv[t] + t_dot(probs.astype(BF16), g[h])
        dprobs = dot_t(g[h], v_ref[:, tile])
        inner = jnp.sum(dprobs * probs, axis=-1, keepdims=True)
        dscore = (probs * (dprobs - inner)).astype(BF16)
        dq[t] = dq[t] + dot(dscore, k[h])
        dk[t] = dk[t] + t_dot(dscore, q[h])
    parts = [
        jnp.concatenate([(one * by).astype(BF16) for one in ones], axis=1)
        for ones, by in ((dq, scale), (dk, scale), (dv, 1.0))
    ]
    by_half(core_ref[0], parts + [m_ref[...]], own_ref, other_ref)


def global_attn_forward(packed, lengths, lanes=512):
    micros, _, items = lengths.shape
    count, wide = packed.shape
    features, frames = wide // 3, count // micros
    width, groups = features // HEADS, features // lanes

    def spec(part):
        return pl.BlockSpec((frames, lanes), lambda m, h, _: (m, part * groups + h))

    return pl.pallas_call(
        functools.partial(global_attn_fwd_kernel, width, items),
        grid_spec=pltpu.PrefetchScalarGridSpec(
            num_scalar_prefetch=1,
            grid=(micros, groups),
            in_specs=[spec(0), spec(1), spec(2)],
            out_specs=spec(0),
        ),
        out_shape=sds((count, features)),
        compiler_params=params(),
        cost_estimate=cost(3000 * count * features, 8 * count * features),
        name="global_attn_forward",
    )(lengths, packed, packed, packed)


def global_attn_backward(core, kept, first, lengths, grads, lanes=512):
    micros, _, items = lengths.shape
    _, count, features = kept.shape
    frames = count // micros
    width, groups = features // HEADS, features // lanes

    def spec(part):
        return pl.BlockSpec((None, frames, lanes), lambda h, c, _: (first + part, c[0], h))

    own = pl.BlockSpec((frames, lanes), lambda h, *_: (0, h))
    half = pl.BlockSpec((2, frames, lanes), lambda h, *_: (0, 0, h))
    return pl.pallas_call(
        functools.partial(global_attn_bwd_kernel, width, items),
        grid_spec=pltpu.PrefetchScalarGridSpec(
            num_scalar_prefetch=2,
            grid=(groups,),
            in_specs=[spec(0), spec(1), spec(2), own, own],
            out_specs=[half] * 2,
        ),
        out_shape=[sds((2, frames, features))] * 2,
        compiler_params=params(),
        cost_estimate=cost(4000 * frames * features, 16 * frames * features),
        name="global_attn_backward",
    )(core, lengths, kept, kept, kept, *grads)


def place_columns(arrays, spots):
    shape = arrays[0].shape

    def kernel(s_ref, *refs):
        for i in range(len(arrays)):
            refs[-1][i] = dot(refs[i][...], s_ref[...]).astype(BF16)

    return pl.pallas_call(
        kernel,
        out_shape=sds((len(arrays),) + shape),
        compiler_params=params(),
        cost_estimate=cost(
            2 * len(arrays) * shape[0] * shape[1] ** 2, 4 * len(arrays) * arrays[0].size
        ),
        name="place_columns",
    )(spots, *arrays)


def pack(arrays, features):
    count = arrays[0].shape[0]
    planes = [(i, c) for i, a in enumerate(arrays) for c in range(a.shape[1] // features)]

    def kernel(*refs):
        for plane, (i, c) in enumerate(planes):
            refs[-1][plane] = refs[i][:, c * features : (c + 1) * features].astype(BF16)

    return pl.pallas_call(
        kernel,
        out_shape=sds((len(planes), count, features)),
        compiler_params=params(),
        cost_estimate=cost(0, 4 * len(planes) * count * features),
        name="pack",
    )(*arrays)


class Group:
    def __init__(self, table, units, lefts, rights, tile, tiles, across):
        self.table, self.per = table, units // 4
        self.lefts, self.rights = lefts, rights
        self.tile, self.tiles, self.across = tile, tiles, across


def weight_grad(group, table, first, steps, per, addends, split):
    lefts, rights, tile = group.lefts, group.rights, group.tile
    ordered = len(lefts) == 1 or len(rights) == 1
    count = sum(a.shape[1] for a, _ in lefts)

    def joined(core, blocks):
        if len(blocks) == 1:
            return blocks[0]
        a, b = blocks
        if ordered:
            a, b = jnp.where(core == 0, a, b), jnp.where(core == 0, b, a)
        return jnp.concatenate([a, b], axis=0)

    def kernel(table_ref, *refs):
        core, refs = table_ref[0], list(refs)
        left_refs = [refs[i * per : (i + 1) * per] for i in range(len(lefts))]
        refs = refs[len(lefts) * per :]
        right = joined(core, [r[0] for r in refs[: len(rights)]])
        add_refs = refs[len(rights) : len(rights) + len(addends)]
        out_refs = refs[len(rights) + len(addends) :]
        for i in range(per):
            at = slice(i * UNIT, (i + 1) * UNIT)
            left = joined(core, [r[i][0] for r in left_refs])
            out = add_all([t_dot(left, right)] + [r[at, :].astype(F32) for r in add_refs])
            out = out.astype(BF16)
            if not split:
                out_refs[0][at, :] = out
            elif per == 1:
                out_refs[0][...] = out[: UNIT // 2]
                out_refs[1][...] = out[UNIT // 2 :]
            else:
                half = per // 2
                out_refs[i // half][(i % half) * UNIT : (i % half + 1) * UNIT, :] = out

    def left_spec(start, rows, i):
        return pl.BlockSpec(
            (1, rows, UNIT),
            lambda u, j, t: (group.across(j, t)[0], 0, t[start + first + u * per + i]),
        )

    def right_spec(rows):
        return pl.BlockSpec(
            (1, rows, tile), lambda u, j, t: (group.across(j, t)[1], 0, group.across(j, t)[2])
        )

    def block(skip, rows=per * UNIT):
        return pl.BlockSpec((rows, tile), lambda u, j, t: (skip + u, j))

    wide = group.tiles * tile
    if split:
        outs = [sds((per * UNIT // 2, wide))] * 2
        out_specs = [block(0, per * UNIT // 2)] * 2
    else:
        outs, out_specs = [sds((steps * per * UNIT, wide))], [block(0)]
    size = steps * per * UNIT * wide
    out = pl.pallas_call(
        kernel,
        grid_spec=pltpu.PrefetchScalarGridSpec(
            num_scalar_prefetch=1,
            grid=(steps, group.tiles),
            in_specs=[left_spec(start, a.shape[1], i) for a, start in lefts for i in range(per)]
            + [right_spec(a.shape[1]) for a in rights]
            + [block(skip) for _, skip in addends],
            out_specs=out_specs,
        ),
        out_shape=outs,
        compiler_params=params(),
        cost_estimate=cost(
            2 * count * size, 2 * (count * (steps * per * UNIT + wide) + size * (1 + len(addends)))
        ),
        name="weight_grad",
    )(table, *[a for a, _ in lefts for _ in range(per)], *rights, *[a for a, _ in addends])
    return out if split else out[0]


class Devices:
    def __init__(self, size):
        self.size = size
        self.core = lax.axis_index("section")
        self.index = lax.axis_index("dp")

    def bits(self, core, late):
        near = [1, 2] if core == 0 else [2, 1]
        far = [1 << b for b in range(2, self.size.bit_length() - 1)]
        return far + near if late else near + far

    def swap(self, array, step, late=False):
        pairs = []
        for core in range(2):
            by = self.bits(core, late)[step]
            pairs += [(core * self.size + i, core * self.size + (i ^ by)) for i in range(self.size)]
        return lax.ppermute(array, ("section", "dp"), pairs)

    def cores(self, array):
        return lax.ppermute(array, "section", [(0, 1), (1, 0)])

    def order(self, late=False):
        orders = []
        for core in range(2):
            bits = self.bits(core, late)
            order = [
                sum(bit for i, bit in enumerate(bits) if (spot >> (len(bits) - 1 - i)) & 1)
                for spot in range(self.size)
            ]
            orders.append(jnp.array(order, jnp.int32))
        return jnp.where(self.core == 0, orders[0], orders[1]) ^ self.index

    def columns(self, count, late=False):
        block = count // self.size
        order = self.order(late)
        return (order[:, None] * block + jnp.arange(block, dtype=jnp.int32)).reshape(-1)

    def spots(self, count):
        at = self.columns(count)[None, :]
        return (lax.broadcasted_iota(jnp.int32, (count, count), 0) == at).astype(BF16)

    def table(self, *orders):
        parts = [self.core[None].astype(jnp.int32)] + [jnp.asarray(o, jnp.int32) for o in orders]
        return jnp.concatenate(parts)

    def total(self, array):
        for step in range(self.size.bit_length() - 1):
            array = array + self.swap(array, step)
        return array


class Sum:
    def __init__(self, devices, line, group, late=False):
        self.devices, self.line, self.group, self.late = devices, line, group, late
        self.step = 0

    def grad(self, first, count, addends, split=False):
        group = self.group
        steps, per = (count, group.per) if group.per > 1 else (1, count)
        out = weight_grad(
            group, self.line.tie(group.table), first * group.per, steps, per, addends, split
        )
        self.line.mark(out[0] if split else out)
        return out

    def send(self, array):
        got = self.devices.swap(array, self.step, self.late)
        self.step += 1
        return got

    def first(self):
        self.one = self.send(self.grad(2, 2, []))

    def second(self):
        skip = 1
        self.two = self.send(self.grad(1, 1, [(self.one, skip)]))

    def third(self):
        self.kept, sent = self.grad(0, 1, [(self.one, 0), (self.two, 0)], split=True)
        self.got = self.send(sent)

    def last(self):
        total = self.kept
        steps = self.devices.size.bit_length() - 1
        while self.step < steps:
            half = total.shape[0] // 2
            sent = (total[half:].astype(F32) + self.got[half:].astype(F32)).astype(BF16)
            total = total[:half].astype(F32) + self.got[:half].astype(F32)
            if self.step < steps - 1:
                total = total.astype(BF16)
            self.got = self.send(sent)
        return total.astype(F32) + self.got.astype(F32)


class Line:
    def __init__(self):
        self.token = None

    def tie(self, table):
        if self.token is None:
            return table
        return lax.optimization_barrier((table, self.token))[0]

    def mark(self, token):
        self.token = token


def local(codebook_embed, item_lengths, gain_attn, w_qkv, w_out, gain_mlp, w_up, w_down, cotangent):
    size = lax.axis_size("dp")
    micros, frames, books, features = codebook_embed.shape
    half_width = features // 2
    scale_in = books**-0.5
    devices, line = Devices(size), Line()
    core = devices.core
    first_core = core == 0
    here = core[None].astype(jnp.int32)

    def run(kernel, *operands):
        out = kernel(line.tie(here), *operands)
        line.mark(out[0])
        return out

    gains = jnp.stack([gain_attn[0], gain_mlp[0]])
    own = [w_qkv[0], w_out[0], w_up[0], w_down[0]]
    gains_other = devices.cores(gains)
    other = [devices.cores(w) for w in own]
    global_weights = list(zip(own, other))
    local_weights = list(zip(other, own))
    global_gains = [(gains[i : i + 1], gains_other[i : i + 1]) for i in range(2)]
    local_gains = [(b, a) for a, b in global_gains]

    embed_all = codebook_embed.transpose(0, 2, 1, 3)
    frame_in = jnp.sum(embed_all.astype(F32), axis=1) * scale_in
    rows = frame_in.reshape(-1, features)
    normed, packed = run(qkv_forward, rows, gains[:1], own[0])
    mixture = global_attn_forward(packed, item_lengths)
    line.mark(mixture)
    middle, normed_two, active, result = run(
        lambda c: mlp_forward(c, rows, mixture, own[1], gains[1:], own[2], own[3], True)
    )

    def from_first(array):
        return lax.ppermute(array, "section", [(0, 1)])

    states = jnp.where(first_core, result[:frames], from_first(result[frames:]))
    kept = pack([normed, mixture, normed_two, packed, middle], features)
    kept = jnp.where(first_core, kept, from_first(kept))
    active = jnp.where(first_core, active, from_first(active))

    embed = lax.dynamic_index_in_dim(embed_all, core, 0, keepdims=False)
    frame_rows = lax.dynamic_index_in_dim(frame_in, core, 0, keepdims=False)
    local_rows = (embed.astype(F32) + states.astype(F32)[None]).reshape(-1, features)
    w_qkv_l, w_out_l, w_up_l, w_down_l = local_weights
    l_normed, l_packed = run(qkv_forward, local_rows, local_gains[0], w_qkv_l)
    l_mixture = local_attn(l_packed, books)
    line.mark(l_mixture)
    l_middle, l_normed_two, l_active, l_slope, l_out = run(
        lambda c: mlp_forward(
            c, local_rows, l_mixture, w_out_l, local_gains[1], w_up_l, w_down_l, False
        )
    )

    unit_rows = w_down.shape[1] // size == UNIT
    same = [0, 1, 2, 3]
    placed_table = devices.table(same, [0, 2, 1, 3])
    spots = devices.spots(features)

    def down_group(lefts, rights, late):
        if unit_rows:
            table = devices.table(devices.order(late))
        else:
            table = devices.table(range(lefts[0].shape[2] // UNIT))
            order = devices.columns(lefts[0].shape[2], late)
            lefts = [jnp.take(a[:1], order, axis=2) for a in lefts]
        units = lefts[0].shape[2] // UNIT
        return Group(
            table, units, [(a, 1) for a in lefts], rights, half_width, 1, lambda j, t: (0, 0, 0)
        )

    def up_group(lefts, rights):
        return Group(placed_table, 4, lefts, rights, features, 2, lambda j, t: (2, 0, j))

    def rest_group(lefts, rights):
        def across(j, t):
            return jnp.where(2 * t[0] + j == 3, 1, 0), j, 0

        return Group(placed_table, 4, lefts, rights, features, 2, across)

    def my_half(array):
        return jnp.where(first_core, array[..., :half_width], array[..., half_width:])

    def other_half(array):
        return jnp.where(first_core, array[..., half_width:], array[..., :half_width])

    upstream_all = cotangent.transpose(0, 2, 1, 3).reshape(micros, -1, features)
    upstream = lax.dynamic_index_in_dim(upstream_all, core, 0, keepdims=False)
    upstream_halves = my_half(upstream_all)
    l_active_got = devices.cores(l_active)
    l_placed = place_columns([l_normed, l_mixture, l_normed_two], spots)
    line.mark(l_placed)
    l_placed_got = devices.cores(l_placed)
    placed_pair = [(l_placed, 1), (l_placed_got, 5)]
    l_down = Sum(
        devices,
        line,
        down_group(
            [l_active, l_active_got],
            [
                lax.dynamic_index_in_dim(upstream_halves, core, 0),
                lax.dynamic_index_in_dim(upstream_halves, 1 - core, 0),
            ],
            False,
        ),
    )
    l_down.first()
    dz_own, dz_other, l_dm, l_low, l_do, l_gain_two = run(
        lambda c: mlp_backward(
            c, upstream, (l_slope, 0, 0), (l_middle[None], 0, 0), w_out_l, local_gains[1], w_up_l, w_down_l
        )
    )
    l_up = Sum(devices, line, up_group(placed_pair, [dz_own, devices.cores(dz_other)]))
    l_down.second()
    l_up.first()
    dp_own, dp_other = run(lambda c: local_attn(l_packed, books, c, (l_do, l_low)))
    l_rest = Sum(devices, line, rest_group(placed_pair, [dp_own, devices.cores(dp_other)]))
    local_grad, frame_grad, l_gain_one = run(
        lambda c: qkv_backward(
            c, dp_own, dp_other, local_rows, l_dm, local_gains[0], w_qkv_l, books
        )
    )
    l_down.third()
    l_up.second()
    l_rest.first()

    w_qkv_g, w_out_g, w_up_g, w_down_g = global_weights
    g_down = Sum(
        devices,
        line,
        down_group(
            [active],
            [my_half(frame_grad)[None], devices.cores(other_half(frame_grad))[None]],
            True,
        ),
        True,
    )
    dz_own, dz_other, g_dm, g_low, g_do, g_gain_two = run(
        lambda c: mlp_backward(
            c, frame_grad, (active, 1, 1), (kept, 6, 1), w_out_g, global_gains[1], w_up_g, w_down_g
        )
    )
    g_down.first()
    placed = place_columns([kept[0], kept[1], kept[2]], spots)
    g_up = Sum(devices, line, up_group([(placed, 1)], [dz_own, devices.cores(dz_other)]))
    dp_own, dp_other = run(
        lambda c: global_attn_backward(c, kept, 3, item_lengths, (g_do, g_low))
    )
    g_rest = Sum(devices, line, rest_group([(placed, 1)], [dp_own, devices.cores(dp_other)]))
    g_up.first()
    global_grad, _, g_gain_one = run(
        lambda c: qkv_backward(
            c, dp_own, dp_other, frame_rows, g_dm, global_gains[0], w_qkv_g, 1
        )
    )
    g_rest.first()
    l_up.third()
    l_rest.second()
    g_down.second()
    g_up.second()
    l_rest.third()
    g_rest.second()
    g_down.third()
    g_up.third()
    g_rest.third()
    l_down, l_up, l_rest, g_down, g_up, g_rest = [
        one.last() for one in (l_down, l_up, l_rest, g_down, g_up, g_rest)
    ]

    def halves(array):
        got = devices.cores(other_half(array).astype(BF16)).astype(array.dtype)
        mine = my_half(array)
        pair = jnp.where(first_core, jnp.stack([mine, got]), jnp.stack([got, mine]))
        return pair.transpose(0, 2, 1, 3)

    local_out = halves(l_out.reshape(books, frames, features))
    embed_grad = halves(
        local_grad.reshape(books, frames, features) + (global_grad * scale_in)[None]
    )

    def layer_sums(ours, theirs):
        sent = devices.cores(jnp.where(first_core, theirs, ours).astype(BF16)).astype(F32)
        mine = jnp.where(first_core, ours, theirs)
        return jnp.where(
            first_core,
            jnp.concatenate([mine, sent], axis=1),
            jnp.concatenate([sent, mine], axis=1),
        )

    down, up, rest = layer_sums(g_down, l_down), layer_sums(g_up, l_up), layer_sums(g_rest, l_rest)
    gain_sums = devices.total(jnp.concatenate([g_gain_one, g_gain_two, l_gain_one, l_gain_two]))
    gain_sums = gain_sums + devices.cores(gain_sums)
    gain_sums = jnp.where(first_core, gain_sums[:2], gain_sums[2:]).reshape(2, size, -1)
    gain_sums = lax.dynamic_index_in_dim(gain_sums, devices.index, 1, keepdims=False)

    return (
        local_out,
        embed_grad,
        gain_sums[:1],
        rest[None, :, : 3 * features],
        rest[None, :, 3 * features :],
        gain_sums[1:],
        up[None],
        down[None],
    )


def solution(mesh):
    in_specs = (
        P(None, "dp", None, None),
        P(None, "dp", None),
        P("section", None),
        P("section", None, None),
        P("section", None, None),
        P("section", None),
        P("section", None, None),
        P("section", None, None),
        P(None, "dp", None, None),
    )
    out_specs = (
        P(None, "dp", None, "section"),
        P(None, "dp", None, "section"),
        P("section", "dp"),
        P("section", "dp", None),
        P("section", "dp", None),
        P("section", "dp"),
        P("section", "dp", None),
        P("section", "dp", None),
    )
    return jax.shard_map(local, mesh=mesh, in_specs=in_specs, out_specs=out_specs, check_vma=False)
```

```python
import functools
import types

import jax
import jax.numpy as jnp
from jax import lax
from jax.experimental import pallas as pl
from jax.experimental.pallas import tpu as pltpu
from jax.sharding import PartitionSpec as P

HEADS = 16
EPSILON = 1e-05
BF16 = jnp.bfloat16
F32 = jnp.float32
VMEM_LIMIT = 48 * 1024 * 1024
CHUNK = 128
COST = 1.0
RIDER = 16
UNIT = 256


def dot(left, right):
    return jnp.dot(left, right, preferred_element_type=F32)


def dot_t(left, right):
    return lax.dot_general(left, right, (((1,), (1,)), ((), ())), preferred_element_type=F32)


def t_dot(left, right):
    return lax.dot_general(left, right, (((0,), (0,)), ((), ())), preferred_element_type=F32)


def add_all(terms):
    return functools.reduce(lambda s, t: s + t, terms)


def sds(shape, dtype=BF16):
    return jax.ShapeDtypeStruct(shape, dtype)


class Weight:
    def __init__(self, given, block, index, tiles):
        self.arrays = list(given) if isinstance(given, tuple) else [given]
        self.block, self.index, self.tiles = block, index, tiles
        self.slots = min(tiles, 2)


class Tiles:
    def __init__(self, weight, core, refs, held, sems):
        self.weight, self.core, self.refs, self.held, self.sems = weight, core, refs, held, sems

    def copy(self, place, j):
        block = self.weight.block
        at = zip(self.weight.index(j, self.core), block)
        at = tuple(pl.ds(pl.multiple_of(i * b, b), b) for i, b in at)
        slot = j % self.weight.slots
        return pltpu.make_async_copy(self.refs[place].at[at], self.held.at[slot], self.sems.at[slot])

    def start(self, j):
        for place in range(len(self.refs)):
            if len(self.refs) == 1:
                self.copy(place, j).start()
            else:

                @pl.when(self.core == place)
                def _():
                    self.copy(place, j).start()

    def get(self, j):
        self.copy(0, j).wait()
        return self.held[j % self.weight.slots]

    def ahead(self, j):
        @pl.when(j == 0)
        def _():
            self.start(0)

        if self.weight.tiles > 1:

            @pl.when(j + 1 < self.weight.tiles)
            def _():
                self.start(j + 1)


class Line:
    def __init__(self):
        self.behind = []

    def wait(self, *arrays):
        self.behind.extend(arrays)

    def launch(self, kernel, name, scalars, grid, ins, outs, scratch=(), flops=0):
        arrays, specs, counts, held = [], [], [], []
        for operand in ins:
            if isinstance(operand, Weight):
                specs.extend([pl.BlockSpec(memory_space=pl.ANY)] * len(operand.arrays))
                arrays.extend(operand.arrays)
                counts.append(operand)
                held.append(pltpu.VMEM((operand.slots,) + operand.block, operand.arrays[0].dtype))
                held.append(pltpu.SemaphoreType.DMA((operand.slots,)))
                continue
            given, block, index = operand
            if isinstance(given, tuple):
                for place in range(2):

                    def at(*args, place=place, index=index):
                        here = args[len(grid)][0] == place
                        return tuple(jnp.where(here, i, 0) for i in index(*args))

                    specs.append(pl.BlockSpec(block, at))
                arrays.extend(given)
                counts.append(2)
            else:
                specs.append(pl.BlockSpec(block, index))
                arrays.append(given)
                counts.append(1)
        skipped = len(self.behind)
        arrays.extend(self.behind)
        specs.extend([pl.BlockSpec(memory_space=pl.ANY)] * skipped)

        def body(*refs):
            scalar_refs, refs = refs[: len(scalars)], refs[len(scalars) :]
            groups, own = [], refs[len(refs) - len(held) :]
            for count in counts:
                if isinstance(count, Weight):
                    weight, count = count, len(count.arrays)
                    core = scalar_refs[0][0]
                    groups.append(Tiles(weight, core, list(refs[:count]), *own[:2]))
                    own = own[2:]
                else:
                    groups.append(list(refs[:count]))
                refs = refs[count:]
            refs = refs[skipped : len(refs) - len(held)]
            kernel(scalar_refs, groups, refs[: len(outs)], refs[len(outs) :])

        out = pl.pallas_call(
            body,
            grid_spec=pltpu.PrefetchScalarGridSpec(
                num_scalar_prefetch=len(scalars),
                grid=grid,
                in_specs=specs,
                out_specs=[pl.BlockSpec(block, index) for _, block, index in outs],
                scratch_shapes=list(scratch) + held,
            ),
            out_shape=[shape for shape, _, _ in outs],
            compiler_params=pltpu.CompilerParams(vmem_limit_bytes=VMEM_LIMIT),
            cost_estimate=pl.CostEstimate(
                flops=int(flops * COST),
                bytes_accessed=int(COST * sum(a.size * a.dtype.itemsize for a in arrays[: len(specs) - skipped])),
                transcendentals=0,
            ),
            name=name,
        )(*scalars, *arrays)
        self.behind = [out[0]]
        return out


def read(core, refs):
    if len(refs) == 1:
        return refs[0][...]
    return jnp.where(core == 0, refs[0][...], refs[1][...])


def origin(rank):
    return lambda *_: (0,) * rank


def whole(array):
    return array, array.shape, origin(array.ndim)


def full(shape, dtype=BF16):
    return sds(shape, dtype), shape, origin(len(shape))


def rstd(rows):
    return lax.rsqrt(jnp.mean(rows * rows, axis=-1, keepdims=True) + EPSILON)


def by_chunks(rows, step):
    def one(i, carry):
        step(pl.ds(pl.multiple_of(i * CHUNK, CHUNK), CHUNK))
        return carry

    lax.fori_loop(0, rows // CHUNK, one, 0)


def norm_backward(grad, rows, gain):
    scale = rstd(rows)
    plain = rows * scale
    grad_gain = jnp.sum(grad * plain, axis=0, keepdims=True)
    lead = grad * gain
    return scale * (lead - plain * jnp.mean(lead * plain, axis=-1, keepdims=True)), grad_gain


def gelu_parts(hidden):
    c = 0.7978845608028654
    square = hidden * hidden
    t = jnp.tanh(hidden * (c + (c * 0.044715) * square))
    half = 0.5 + 0.5 * t
    slope = half + (hidden * half) * ((1.0 - t) * (c + (3 * 0.044715 * c) * square))
    return (hidden * half).astype(BF16), slope.astype(BF16)


def qkv_forward(line, here, parts, make_rows, gain, w_qkv, tile=1024):
    features = gain[0].shape[1] if isinstance(gain, tuple) else gain.shape[1]
    count, wide = parts[0], 3 * features

    def kernel(scalars, ins, outs, _):
        core = scalars[0][0]
        gain_refs, w = ins[-2:]
        x_ref, h_ref, p_ref = outs
        j = pl.program_id(0)
        w.ahead(j)

        @pl.when(j == 0)
        def _():
            gain = read(core, gain_refs)
            for i, x in enumerate(make_rows(core, ins[:-2])):
                at = slice(i * CHUNK, (i + 1) * CHUNK)
                x_ref[at, :] = x
                h_ref[at, :] = (x * rstd(x) * gain).astype(BF16)

        p_ref[...] = dot(h_ref[...], w.get(j)).astype(BF16)

    return line.launch(
        kernel,
        "qkv_forward",
        [here],
        (wide // tile,),
        parts[1]
        + [
            (gain, (1, features), origin(2)),
            Weight(w_qkv, (features, tile), lambda j, core: (0, j), wide // tile),
        ],
        [
            full((count, features), F32),
            full((count, features)),
            (sds((count, wide)), (count, tile), lambda j, s: (0, j)),
        ],
        flops=2 * count * features * wide,
    )


def mlp_forward(line, here, rows, mixture, w_out, gain, w_up, w_down, joined, tile=1024):
    count, features = rows.shape
    wide = (w_up[0] if isinstance(w_up, tuple) else w_up).shape[1]

    def kernel(scalars, ins, outs, scratch):
        core = scalars[0][0]
        (x_ref,), (o_ref,), w_out, gain_refs, w_up, w_down = ins
        y_ref, m_ref, h_ref = outs[:3]
        (acc_ref,) = scratch
        j = pl.program_id(0)
        for w in (w_out, w_up, w_down):
            w.ahead(j)

        @pl.when(j == 0)
        def _():
            gain, wide_out = read(core, gain_refs), w_out.get(0)

            def step(at):
                m = x_ref[at, :] + dot(o_ref[at, :], wide_out)
                m_ref[at, :] = m
                acc_ref[at, :] = m
                h_ref[at, :] = (m * rstd(m) * gain).astype(BF16)

            by_chunks(count, step)

        g, slope = gelu_parts(dot(h_ref[...], w_up.get(j)))
        if joined:
            outs[3][0] = g
            outs[3][1] = slope
        else:
            outs[3][0] = g
            outs[4][0] = slope
        acc_ref[...] += dot(g, w_down.get(j))

        @pl.when(pl.program_id(0) == pl.num_programs(0) - 1)
        def _():
            y_ref[...] = acc_ref[...].astype(BF16)

    planes = 2 if joined else 1
    wide_out = (sds((planes, count, wide)), (planes, count, tile), lambda j, s: (0, 0, j))
    return line.launch(
        kernel,
        "mlp_forward",
        [here],
        (wide // tile,),
        [
            whole(rows),
            whole(mixture),
            Weight(w_out, (features, features), lambda j, core: (0, 0), 1),
            (gain, (1, features), origin(2)),
            Weight(w_up, (features, tile), lambda j, core: (0, j), wide // tile),
            Weight(w_down, (tile, features), lambda j, core: (j, 0), wide // tile),
        ],
        [full(rows.shape), full(rows.shape, F32), full(rows.shape)] + [wide_out] * (3 - planes),
        [pltpu.VMEM(rows.shape, F32)],
        flops=2 * count * features * (features + 2 * wide),
    )


def mlp_backward(line, here, low_out, slope, middle, w_out, gain, w_up, w_down, tile=1024):
    wide, features = w_down[0].shape
    count = low_out[3]
    tiles = wide // tile
    half = tiles // 2

    def kernel(scalars, ins, outs, scratch):
        core = scalars[0][0]
        (dy_ref,), s_refs, m_refs, gain_refs, w_down, w_up, w_out = ins
        low_ref, own_ref, other_ref, dm_ref, do_ref, gg_ref = outs
        (acc_ref,) = scratch
        j = pl.program_id(0)
        for w in (w_down, w_up, w_out):
            w.ahead(j)
        slope = read(core, s_refs)[0].astype(F32)
        dz = (slope * dot_t(dy_ref[0], w_down.get(j))).astype(BF16)

        @pl.when(j < half)
        def _():
            other_ref[0] = dz

        @pl.when(j >= half)
        def _():
            own_ref[0] = dz

        term = dot_t(dz, w_up.get(j))

        @pl.when(j == 0)
        def _():
            acc_ref[...] = term

        @pl.when(j > 0)
        def _():
            acc_ref[...] += term

        @pl.when(j == tiles - 1)
        def _():
            gg_ref[...] = jnp.zeros_like(gg_ref)
            gain, wide_out = read(core, gain_refs), w_out.get(0)

            def step(at):
                if len(m_refs) == 1:
                    m = m_refs[0][0, at, :].astype(F32)
                else:
                    m = jnp.where(core == 0, m_refs[0][0, at, :], m_refs[1][0, at, :]).astype(F32)
                dm, gg = norm_backward(acc_ref[at, :], m, gain)
                gg_ref[...] += gg
                dm = dm + dy_ref[0, at, :].astype(F32)
                dm_ref[at, :] = dm
                low = dm.astype(BF16)
                low_ref[at, :] = low
                do_ref[at, :] = dot_t(low, wide_out).astype(BF16)

            by_chunks(count, step)

    def at(j, core):
        return (j + (1 - core) * half) % tiles

    shape = (count, features)
    return line.launch(
        kernel,
        "mlp_backward",
        [here],
        (tiles,),
        [
            (low_out[0], (1,) + shape, lambda j, s: (low_out[1](s[0]), low_out[2](s[0]), 0)),
            (slope[0], (1, count, tile), lambda j, s: (slope[1], slope[2](s[0]), at(j, s[0]))),
            (middle[0], (1,) + shape, lambda j, s: (middle[1], middle[2](s[0]), 0)),
            (gain, (1, features), origin(2)),
            Weight(w_down, (tile, features), lambda j, core: (at(j, core), 0), tiles),
            Weight(w_up, (features, tile), lambda j, core: (0, at(j, core)), tiles),
            Weight(w_out, (features, features), lambda j, core: (0, 0), 1),
        ],
        [
            full(shape),
            (
                sds((1, count, wide // 2)),
                (1, count, tile),
                lambda j, s: (0, 0, jnp.maximum(j - half, 0)),
            ),
            (
                sds((1, count, wide // 2)),
                (1, count, tile),
                lambda j, s: (0, 0, jnp.minimum(j, half - 1)),
            ),
            full(shape, F32),
            full(shape),
            full((1, features), F32),
        ],
        [pltpu.VMEM(shape, F32)],
        flops=2 * count * features * (features + 2 * wide),
    )


def qkv_backward(line, here, own, other, rows, grad_middle, gain, w_qkv, books, tile=512):
    count, features = grad_middle.shape
    frames = count // books

    def kernel(scalars, ins, outs, scratch):
        core = scalars[0][0]
        (own_ref,), (other_ref,), (x_ref,), (dm_ref,), gain_refs, w_tiles = ins
        dx_ref, sum_ref, gg_ref = outs
        (acc_ref,) = scratch
        j = pl.program_id(0)
        w_tiles.ahead(j)
        w = w_tiles.get(j)
        terms = []
        for i in range(3):
            part = jnp.where(core == i // 2, own_ref[i % 2], other_ref[i % 2])
            terms.append(dot_t(part, w[:, i * features : (i + 1) * features]))
        acc_ref[:, pl.ds(pl.multiple_of(j * tile, tile), tile)] = add_all(terms)

        @pl.when(j == pl.num_programs(0) - 1)
        def _():
            gg_ref[...] = jnp.zeros_like(gg_ref)
            gain = read(core, gain_refs)
            total = 0.0
            for b in range(books):
                at = slice(b * frames, (b + 1) * frames)
                dx, gg = norm_backward(acc_ref[at, :], x_ref[at, :], gain)
                gg_ref[...] += gg
                dx = dx + dm_ref[at, :]
                dx_ref[at, :] = dx
                total = total + dx
            sum_ref[0] = total.astype(BF16)

    shape = (count, features)
    return line.launch(
        kernel,
        "qkv_backward",
        [here],
        (features // tile,),
        [
            whole(own),
            whole(other),
            (rows[0], shape, lambda j, s: (rows[1](s[0]), 0)),
            whole(grad_middle),
            (gain, (1, features), origin(2)),
            Weight(w_qkv, (tile, 3 * features), lambda j, core: (j, 0), features // tile),
        ],
        [full(shape, F32), full((1, frames, features)), full((1, features), F32)],
        [pltpu.VMEM(shape, F32)],
        flops=6 * count * features * features,
    )


def head_sum(product, reduce_mat):
    high = product.astype(BF16)
    low = (product - high.astype(F32)).astype(BF16)
    return dot(high, reduce_mat) + dot(low, reduce_mat)


def head_mats(lanes, width):
    row = lax.broadcasted_iota(jnp.int32, (lanes, 128), 0)
    col = lax.broadcasted_iota(jnp.int32, (lanes, 128), 1)
    reduce_mat = (row // width == col).astype(BF16)
    row = lax.broadcasted_iota(jnp.int32, (128, lanes), 0)
    col = lax.broadcasted_iota(jnp.int32, (128, lanes), 1)
    return reduce_mat, (col // width == row).astype(BF16)


def local_probs(q, k, reduce_mat, scale):
    probs = {}
    for a in range(len(q)):
        scores = [head_sum(q[a] * k[b], reduce_mat) * scale for b in range(a + 1)]
        peak = functools.reduce(jnp.maximum, scores)
        parts = [jnp.exp(s - peak) for s in scores]
        total = add_all(parts)
        for b in range(a + 1):
            probs[a, b] = parts[b] / total
    return probs


def local_attn_fwd_kernel(width, q_ref, k_ref, v_ref, o_ref):
    books, _, lanes = q_ref.shape
    reduce_mat, expand_mat = head_mats(lanes, width)
    q = [q_ref[a].astype(F32) for a in range(books)]
    k = [k_ref[a].astype(F32) for a in range(books)]
    v = [v_ref[a].astype(F32) for a in range(books)]
    probs = local_probs(q, k, reduce_mat, width**-0.5)
    for a in range(books):
        mixed = [dot(probs[a, b].astype(BF16), expand_mat) * v[b] for b in range(a + 1)]
        o_ref[a] = add_all(mixed).astype(BF16)


def by_half(core, parts, own_ref, other_ref):
    for c in range(2):

        @pl.when(core == c)
        def _():
            for i in range(2):
                own_ref[i] = parts[2 * c + i]
                other_ref[i] = parts[2 - 2 * c + i]


def local_attn_bwd_kernel(
    width, core, q_ref, k_ref, v_ref, g_ref, m_ref, own_ref, other_ref
):
    books, _, lanes = q_ref.shape
    scale = width**-0.5
    reduce_mat, expand_mat = head_mats(lanes, width)
    q = [q_ref[a].astype(F32) for a in range(books)]
    k = [k_ref[a].astype(F32) for a in range(books)]
    v = [v_ref[a].astype(F32) for a in range(books)]
    g = [g_ref[a].astype(F32) for a in range(books)]
    probs = local_probs(q, k, reduce_mat, scale)
    dq = [0.0] * books
    dk = [0.0] * books
    dv = [0.0] * books
    for a in range(books):
        dprobs = [head_sum(g[a] * v[b], reduce_mat) for b in range(a + 1)]
        inner = add_all([dprobs[b] * probs[a, b] for b in range(a + 1)])
        for b in range(a + 1):
            dscore = dot((probs[a, b] * (dprobs[b] - inner)).astype(BF16), expand_mat)
            dq[a] = dq[a] + dscore * k[b]
            dk[b] = dk[b] + dscore * q[a]
            dv[b] = dv[b] + dot(probs[a, b].astype(BF16), expand_mat) * g[a]
    parts = [
        jnp.stack([(one * by).astype(BF16) for one in ones])
        for ones, by in ((dq, scale), (dk, scale), (dv, 1.0))
    ]
    by_half(core, parts + [m_ref[...]], own_ref, other_ref)


def local_attn(line, here, packed, books, grads=None, lanes=512):
    count, wide = packed.shape
    features, frames = wide // 3, count // books
    width, groups = features // HEADS, features // lanes
    packed = packed.reshape(books, frames, wide)
    shape, block = (books, frames, features), (books, frames, lanes)

    def at(part):
        return lambda h, *_: (0, 0, part * groups + h)

    ins = [(packed, block, at(i)) for i in range(3)]
    if grads is None:

        def forward(scalars, ins, outs, _):
            local_attn_fwd_kernel(width, *[i[0] for i in ins], *outs)

        out = line.launch(
            forward,
            "local_attn_forward",
            [here],
            (groups,),
            ins,
            [(sds(shape), block, at(0))],
            flops=4000 * count * features,
        )
        return out[0].reshape(count, features)

    def backward(scalars, ins, outs, _):
        local_attn_bwd_kernel(width, scalars[0][0], *[i[0] for i in ins], *outs)

    ins += [(g.reshape(shape), block, at(0)) for g in grads]
    half = (sds((2,) + shape), (2,) + block, lambda h, *_: (0, 0, 0, h))
    out = line.launch(
        backward,
        "local_attn_backward",
        [here],
        (groups,),
        ins,
        [half] * 2,
        flops=10000 * count * features,
    )
    return [one.reshape(2, count, features) for one in out]


def item_mask(lengths_ref, micro, frames, items):
    row = lax.broadcasted_iota(jnp.int32, (frames, frames), 0)
    col = lax.broadcasted_iota(jnp.int32, (frames, frames), 1)
    row_item = jnp.zeros((frames, frames), jnp.int32)
    col_item = jnp.zeros((frames, frames), jnp.int32)
    end = 0
    for i in range(items):
        end = end + lengths_ref[micro, 0, i]
        row_item = row_item + (row >= end).astype(jnp.int32)
        col_item = col_item + (col >= end).astype(jnp.int32)
    return (row_item == col_item) & (row >= col)


def head_parts(block, width):
    per = 128 // width
    lane = lax.broadcasted_iota(jnp.int32, (block.shape[0], 128), 1)
    parts = []
    for h in range(block.shape[1] // width):
        tile = block[:, (h // per) * 128 : (h // per + 1) * 128]
        parts.append(jnp.where(lane // width == h % per, tile, jnp.zeros_like(tile)))
    return parts


def frame_probs(q, k, mask, scale):
    scores = jnp.where(mask, dot_t(q, k) * scale, -1e30)
    parts = jnp.exp(scores - jnp.max(scores, axis=-1, keepdims=True))
    return parts / jnp.sum(parts, axis=-1, keepdims=True)


def global_attn_fwd_kernel(width, items, lengths_ref, q_ref, k_ref, v_ref, o_ref):
    frames, lanes = q_ref.shape
    mask = item_mask(lengths_ref, pl.program_id(0), frames, items)
    per = 128 // width
    q = head_parts(q_ref[...], width)
    v = head_parts(v_ref[...], width)
    mixed = [0.0] * (lanes // 128)
    for h in range(lanes // width):
        tile = slice((h // per) * 128, (h // per + 1) * 128)
        probs = frame_probs(q[h], k_ref[:, tile], mask, width**-0.5)
        mixed[h // per] = mixed[h // per] + dot(probs.astype(BF16), v[h])
    for i, tile in enumerate(mixed):
        o_ref[:, i * 128 : (i + 1) * 128] = tile.astype(BF16)


def global_attn_bwd_kernel(
    width, items, core, lengths_ref, q, k, v, g_ref, m_ref, own_ref, other_ref
):
    frames, lanes = q.shape
    scale = width**-0.5
    mask = item_mask(lengths_ref, core, frames, items)
    per = 128 // width
    q = head_parts(q, width)
    wide_k, k = k, head_parts(k, width)
    g = head_parts(g_ref[...], width)
    tiles = lanes // 128
    dq, dk, dv = [0.0] * tiles, [0.0] * tiles, [0.0] * tiles
    for h in range(lanes // width):
        t = h // per
        tile = slice(t * 128, (t + 1) * 128)
        probs = frame_probs(q[h], wide_k[:, tile], mask, scale)
        dv[t] = dv[t] + t_dot(probs.astype(BF16), g[h])
        dprobs = dot_t(g[h], v[:, tile])
        inner = jnp.sum(dprobs * probs, axis=-1, keepdims=True)
        dscore = (probs * (dprobs - inner)).astype(BF16)
        dq[t] = dq[t] + dot(dscore, k[h])
        dk[t] = dk[t] + t_dot(dscore, q[h])
    parts = [
        jnp.concatenate([(one * by).astype(BF16) for one in ones], axis=1)
        for ones, by in ((dq, scale), (dk, scale), (dv, 1.0))
    ]
    by_half(core, parts + [m_ref[...]], own_ref, other_ref)


def global_attn_forward(line, packed, lengths, lanes=1024):
    micros, _, items = lengths.shape
    count, wide = packed.shape
    features, frames = wide // 3, count // micros
    width, groups = features // HEADS, features // lanes
    block = (frames, lanes)

    def at(part):
        return lambda m, h, _: (m, part * groups + h)

    def kernel(scalars, ins, outs, _):
        global_attn_fwd_kernel(width, items, scalars[0], *[i[0] for i in ins], *outs)

    return line.launch(
        kernel,
        "global_attn_forward",
        [lengths],
        (micros, groups),
        [(packed, block, at(i)) for i in range(3)],
        [(sds((count, features)), block, at(0))],
        flops=10000 * count * features,
    )[0]


def global_attn_backward(line, here, kept, first, lengths, grads, lanes=1024):
    micros, _, items = lengths.shape
    _, count, features = kept[0].shape
    frames = count // micros
    width, groups = features // HEADS, features // lanes
    block = (frames, lanes)

    def kernel(scalars, ins, outs, _):
        core = scalars[0][0]
        q, k, v = [read(core, i)[0] for i in ins[:3]]
        global_attn_bwd_kernel(
            width, items, core, scalars[1], q, k, v, ins[3][0], ins[4][0], *outs
        )

    half = (sds((2, frames, features)), (2,) + block, lambda h, *_: (0, 0, h))
    return line.launch(
        kernel,
        "global_attn_backward",
        [here, lengths],
        (groups,),
        [(kept, (1,) + block, lambda h, c, _, i=i: (first + i, c[0], h)) for i in range(3)]
        + [(g, block, lambda h, *_: (0, h)) for g in grads],
        [half] * 2,
        flops=30000 * frames * features,
    )


def place_columns(line, here, sources, rows, spots, cut=False):
    features = spots.shape[0]

    def kernel(scalars, ins, outs, _):
        for i, refs in enumerate(ins[1:]):
            block = read(scalars[0][0], refs).reshape(rows, features)
            placed = dot(block, ins[0][0][...]).astype(BF16)
            wide = features // len(outs)
            for k, out in enumerate(outs):
                out[i] = placed[:, k * wide : (k + 1) * wide]

    ins = [whole(spots)]
    for source in sources:
        if isinstance(source, tuple):
            ins.append((source[0], (1, rows, features), lambda _, s, plane=source[1]: (plane, 0, 0)))
        else:
            ins.append(whole(source))
    parts = 2 if cut else 1
    out = line.launch(
        kernel,
        "place_columns",
        [here],
        (1,),
        ins,
        [full((len(sources), rows, features // parts))] * parts,
        flops=2 * len(sources) * rows * features * features,
    )
    return out if cut else out[0]


def place_units(line, table, source, rows, units):
    per = 4

    def kernel(scalars, ins, outs, _):
        for i in range(per):
            outs[0][0, :, i * UNIT : (i + 1) * UNIT] = read(scalars[0][0], ins[i])[0]

    first, count = units

    def at(i):
        return lambda u, t: (0, 0, t[1 + first + u * per + i])

    return line.launch(
        kernel,
        "place_units",
        [table],
        (count // per,),
        [(source, (1, rows, UNIT), at(i)) for i in range(per)],
        [(sds((1, rows, count * UNIT)), (1, rows, per * UNIT), lambda u, t: (0, 0, u))],
    )[0]


def pack(line, here, arrays, features):
    count = arrays[0].shape[0]
    planes = [(i, c) for i, a in enumerate(arrays) for c in range(a.shape[1] // features)]

    def kernel(scalars, ins, outs, _):
        for plane, (i, c) in enumerate(planes):
            outs[0][plane] = ins[i][0][:, c * features : (c + 1) * features].astype(BF16)

    return line.launch(
        kernel,
        "pack",
        [here],
        (1,),
        [whole(a) for a in arrays],
        [full((len(planes), count, features))],
    )[0]


class Group:
    def __init__(self, table, units, lefts, rights, tile, tiles, plane):
        self.table, self.per = table, units // 4
        self.lefts, self.rights = lefts, rights
        self.tile, self.tiles, self.plane = tile, tiles, plane


def joined(core, blocks, ordered):
    if ordered:
        pairs = []
        for a, b in zip(blocks[::2], blocks[1::2]):
            pairs += [jnp.where(core == 0, a, b), jnp.where(core == 0, b, a)]
        blocks = pairs
    return blocks[0] if len(blocks) == 1 else jnp.concatenate(blocks, axis=0)


def weight_grad(line, group, first, steps, per, addends, split):
    lefts, rights, tile = group.lefts, group.rights, group.tile

    def kernel(scalars, ins, outs, _):
        core = scalars[0][0]
        left_refs = [ins[i * per : (i + 1) * per] for i in range(len(lefts))]
        ins = ins[len(lefts) * per :]
        right = joined(
            core, [r[0][0] for r in ins[: len(rights)]], len(rights) > len(lefts)
        )
        add_refs = [r[0] for r in ins[len(rights) :]]
        for i in range(per):
            at = slice(i * UNIT, (i + 1) * UNIT)
            left = joined(
                core, [read(core, r[i])[0] for r in left_refs], len(lefts) > len(rights)
            )
            out = add_all([t_dot(left, right)] + [r[at, :].astype(F32) for r in add_refs])
            out = out.astype(BF16)
            if not split:
                outs[0][at, :] = out
            elif per == 1:
                outs[0][...] = out[: UNIT // 2]
                outs[1][...] = out[UNIT // 2 :]
            else:
                half = per // 2
                outs[i // half][(i % half) * UNIT : (i % half + 1) * UNIT, :] = out

    def left_in(given, start, i):
        rows = (given[0] if isinstance(given, tuple) else given).shape[1]
        return (
            given,
            (1, rows, UNIT),
            lambda u, j, t: (group.plane(j, t), 0, t[start + first + u * per + i]),
        )

    def right_in(given, count, at):
        return given, (1, count, tile), lambda u, j, t: at(j, t)

    def block(skip, rows=per * UNIT):
        return (rows, tile), lambda u, j, t: (skip + u, j)

    wide = group.tiles * tile
    rows = sum(count for _, count, _ in rights)
    if split:
        outs = [(sds((per * UNIT // 2, wide)),) + block(0, per * UNIT // 2)] * 2
    else:
        outs = [(sds((steps * per * UNIT, wide)),) + block(0)]
    out = line.launch(
        kernel,
        "weight_grad",
        [group.table],
        (steps, group.tiles),
        [left_in(a, start, i) for a, start in lefts for i in range(per)]
        + [right_in(*right) for right in rights]
        + [(a,) + block(skip) for a, skip in addends],
        outs,
        flops=2 * steps * per * UNIT * wide * rows,
    )
    return out if split else out[0]


class Devices:
    def __init__(self, size):
        self.size = size
        self.core = lax.axis_index("section")
        self.index = lax.axis_index("dp")

    def bits(self, core, line):
        near = [1, 2] if core == 0 else [2, 1]
        far = [1 << b for b in range(2, self.size.bit_length() - 1)]
        return near + far if line else far[:1] + near + far[1:]

    def swap(self, array, step, line=False):
        pairs = []
        for core in range(2):
            by = self.bits(core, line)[step]
            pairs += [(core * self.size + i, core * self.size + (i ^ by)) for i in range(self.size)]
        return lax.ppermute(array, ("section", "dp"), pairs)

    def cores(self, array):
        return lax.ppermute(array, "section", [(0, 1), (1, 0)])

    def order(self, line=False):
        orders = []
        for core in range(2):
            bits = self.bits(core, line)
            if line:
                bits = bits[:2] + bits[:1:-1]
            order = [
                sum(bit for i, bit in enumerate(bits) if (spot >> (len(bits) - 1 - i)) & 1)
                for spot in range(self.size)
            ]
            orders.append(jnp.array(order, jnp.int32))
        return jnp.where(self.core == 0, orders[0], orders[1]) ^ (
            self.index % 4 if line else self.index
        )

    def columns(self, count, line=False):
        block = count // self.size
        order = self.order(line)
        return (order[:, None] * block + jnp.arange(block, dtype=jnp.int32)).reshape(-1)

    def spots(self, count, line=False):
        at = self.columns(count, line)[None, :]
        return (lax.broadcasted_iota(jnp.int32, (count, count), 0) == at).astype(BF16)

    def along_z(self, array):
        depth = self.size // 4
        groups = [[4 * z + place for z in range(depth)] for place in range(4)]
        return lax.psum_scatter(
            array, "dp", scatter_dimension=0, axis_index_groups=groups, tiled=True
        )

    def table(self, *orders):
        parts = [self.core[None].astype(jnp.int32)] + [jnp.asarray(o, jnp.int32) for o in orders]
        return jnp.concatenate(parts)


class Sum:
    def __init__(self, devices, line, group, step=0, along_z=False):
        self.devices, self.line, self.group, self.step = devices, line, group, step
        self.one, self.along_z = None, along_z
        self.rider = None

    def grad(self, first, count, addends, split=False):
        group = self.group
        steps, per = (count, group.per) if group.per > 1 else (1, count)
        return weight_grad(self.line, group, first * group.per, steps, per, addends, split)

    def send(self, array):
        rows, columns = array.shape
        if self.rider is not None:
            shape, size = self.rider.shape, self.rider.size
            high = self.rider.astype(BF16)
            low = (self.rider - high.astype(F32)).astype(BF16)
            extra = jnp.concatenate([high, low]).reshape(-1, columns)
            extra = jnp.pad(extra, ((0, -extra.shape[0] % RIDER), (0, 0)))
            array = jnp.concatenate([array, extra])
        got = self.devices.swap(array, self.step, self.along_z)
        if self.rider is not None:
            extra = got[rows:].astype(F32).reshape(-1)
            self.rider = self.rider + (extra[:size] + extra[size : 2 * size]).reshape(shape)
        self.step += 1
        return got

    def first(self):
        self.one = self.send(self.grad(2, 2, []))

    def second(self):
        self.two = self.send(self.grad(1, 1, [] if self.one is None else [(self.one, 1)]))

    def third(self):
        addends = [(one, 0) for one in (self.one, self.two) if one is not None]
        if self.along_z:
            self.kept = self.devices.along_z(self.grad(0, 1, addends))
            return
        self.kept, sent = self.grad(0, 1, addends, split=True)
        self.got = self.send(sent)

    def rest(self):
        steps = self.devices.size.bit_length() - 1
        total = self.kept
        while self.step < steps:
            got = self.got
            half = total.shape[0] // 2
            sent = (total[half:].astype(F32) + got[half : 2 * half].astype(F32)).astype(BF16)
            total = total[:half].astype(F32) + got[:half].astype(F32)
            if self.step < steps - 1:
                total = total.astype(BF16)
            self.line.wait(sent)
            self.got = self.send(sent)
        self.kept = total

    def last(self):
        if self.along_z:
            return self.kept.astype(F32)
        return self.kept.astype(F32) + self.got[: self.kept.shape[0]].astype(F32)


PLAN = (
    "g_qkv",
    "g_attn",
    "g_mlp",
    "g_pack",
    "l_qkv",
    "l_attn",
    "l_mlp",
    "l_place",
    "l_down first",
    "l_mlp_back",
    "g_units",
    "l_attn_back",
    "wait l_down one",
    "l_down second",
    "g_place",
    "l_up first",
    "l_rest first",
    "wait l_placed_got",
    "l_down third",
    "l_qkv_back",
    "g_mlp_back",
    "wait active_got",
    "l_output",
    "g_attn_back",
    "wait placed_got",
    "g_qkv_back",
    "g_gains",
    "l_rest second",
    "g_up second",
    "wait l_up one",
    "l_up second",
    "g_rest second",
    "l_up third",
    "g_output",
    "wait l_down two",
    "g_up third",
    "l_rest third",
    "g_down second",
    "g_rest third",
    "g_down third",
    "g_down rest",
    "g_rest rest",
    "g_up rest",
    "down_out",
    "up_out",
    "rest_out",
)


def both_halves(line, here, devices, ours, theirs, parts):
    rows, wide = ours.kept.shape
    half = jax.ShapeDtypeStruct((rows, wide), BF16)

    def split(scalars, ins, outs, _):
        core = scalars[0][0]
        kept, got, other = [i[0][...].astype(F32) for i in ins]
        mine = kept + got[:rows]
        outs[0][...] = jnp.where(core == 0, other, mine).astype(BF16)
        outs[1][...] = jnp.where(core == 0, mine, other)

    sent, mine = line.launch(
        split,
        "split_halves",
        [here],
        (1,),
        [whole(ours.kept), whole(ours.got), whole(theirs.kept)],
        [full(half.shape), full(half.shape, F32)],
    )
    got = devices.cores(sent)

    def join(scalars, ins, outs, _):
        core = scalars[0][0]
        mine, got = ins[0][0][...], ins[1][0][...].astype(F32)
        joined = jnp.concatenate(
            [jnp.where(core == 0, mine, got), jnp.where(core == 0, got, mine)], axis=1
        )
        start = 0
        for out in outs:
            out[0] = joined[:, start : start + out.shape[2]]
            start += out.shape[2]

    return line.launch(
        join,
        "join_halves",
        [here],
        (1,),
        [whole(mine), whole(got)],
        [full((1, rows, 2 * wide * part // sum(parts)), F32) for part in parts],
    )


def local(codebook_embed, item_lengths, gain_attn, w_qkv, w_out, gain_mlp, w_up, w_down, cotangent):
    size = lax.axis_size("dp")
    micros, frames, books, features = codebook_embed.shape
    half_width = features // 2
    scale_in = books**-0.5
    devices, line = Devices(size), Line()
    core = devices.core
    first_core = core == 0
    here = core[None].astype(jnp.int32)

    def zero(core):
        return 0

    def same(core):
        return core

    gains = jnp.stack([gain_attn[0], gain_mlp[0]])
    own = [w_qkv[0], w_out[0], w_up[0], w_down[0]]
    gains_other = devices.cores(gains)
    other = [devices.cores(w) for w in own]
    w_qkv_g, w_out_g, w_up_g, w_down_g = zip(own, other)
    w_qkv_l, w_out_l, w_up_l, w_down_l = zip(other, own)
    gains_g = [(gains[i : i + 1], gains_other[i : i + 1]) for i in range(2)]
    gains_l = [(b, a) for a, b in gains_g]

    embed = codebook_embed.transpose(0, 2, 1, 3)
    upstream = cotangent.transpose(0, 2, 1, 3).reshape(micros, -1, features)

    def with_first(array):
        return array, devices.cores(array)

    columns = w_down.shape[1]
    unit_rows = columns // size == UNIT
    units = columns // UNIT
    near, far = range(units // 2), range(units // 2, units)
    placed_table = devices.table([0, 1, 2, 3], [0, 2, 1, 3])
    down_table = devices.table(devices.order() if unit_rows else range(units), range(units))
    spots, line_spots = devices.spots(features), devices.spots(features, True)
    line_table = devices.table(devices.order(True) if unit_rows else range(units))

    def by_units(array, line=False):
        if unit_rows:
            return array
        if isinstance(array, tuple):
            return tuple(by_units(a, line) for a in array)
        return jnp.take(array[:1], devices.columns(columns, line), axis=2)

    def down_group(table, lefts, rights):
        return Group(table, units, lefts, rights, half_width, 1, lambda j, t: 0)

    def up_group(lefts, rights):
        return Group(
            placed_table,
            4,
            lefts,
            [(a, count, lambda j, t, i=i: (0, i, j)) for a, count, i in rights],
            features,
            2,
            lambda j, t: 2,
        )

    def rest_group(lefts, rights):
        return Group(
            placed_table,
            4,
            lefts,
            [(a, count, lambda j, t, i=i: (j, i, 0)) for a, count, i in rights],
            features,
            2,
            lambda j, t: jnp.where(2 * t[0] + j == 3, 1, 0),
        )

    def my_half(array):
        return jnp.where(first_core, array[..., :half_width], array[..., half_width:])

    def other_half(array):
        return jnp.where(first_core, array[..., half_width:], array[..., :half_width])

    def halves(array):
        got = devices.cores(other_half(array).astype(BF16)).astype(array.dtype)
        mine = my_half(array)
        pair = jnp.where(first_core, jnp.stack([mine, got]), jnp.stack([got, mine]))
        return pair.transpose(0, 2, 1, 3)

    def both(mine, others):
        return [(mine, mine.shape[1], 0), (devices.cores(others), mine.shape[1], 0)]

    def all_rows(mine, others):
        rights = both(mine, others)
        far = devices.swap(jnp.concatenate([rights[0][0], rights[1][0]], axis=1), 0)
        return rights + [(far, frames, i) for i in range(micros)]

    at = types.SimpleNamespace()

    def g_qkv():
        def frame_rows(core, ins):
            (e_ref,) = ins[0]
            return [
                add_all([e_ref[m, b].astype(F32) for b in range(books)]) * scale_in
                for m in range(micros)
            ]

        at.rows, at.normed, at.packed = qkv_forward(
            line, here, (micros * frames, [whole(embed)]), frame_rows, gains[:1], own[0]
        )

    def g_attn():
        at.mixture = global_attn_forward(line, at.packed, item_lengths)

    def g_mlp():
        result, at.middle, at.normed_two, active = mlp_forward(
            line, here, at.rows, at.mixture, own[1], gains[1:], own[2], own[3], True
        )
        at.states, at.active = with_first(result), with_first(active)
        at.active_units = by_units(at.active)

    def g_pack():
        arrays = [at.normed, at.mixture, at.normed_two, at.packed, at.middle]
        at.kept = with_first(pack(line, here, arrays, features))

    def l_qkv():
        def local_rows(core, ins):
            (e_ref,), s_refs = ins
            state = read(core, s_refs).astype(F32)
            return [e_ref[0, b].astype(F32) + state for b in range(books)]

        parts = [
            (embed, (1, books, frames, features), lambda j, s: (s[0], 0, 0, 0)),
            (at.states, (frames, features), lambda j, s: (s[0], 0)),
        ]
        at.l_rows, at.l_normed, at.l_packed = qkv_forward(
            line, here, (books * frames, parts), local_rows, gains_l[0], w_qkv_l
        )

    def l_attn():
        at.l_mixture = local_attn(line, here, at.l_packed, books)

    def l_mlp():
        at.l_out, at.l_middle, at.l_normed_two, at.l_active, at.l_slope = mlp_forward(
            line, here, at.l_rows, at.l_mixture, w_out_l, gains_l[1], w_up_l, w_down_l, False
        )
        at.l_active_got = devices.cores(at.l_active)
        at.l_down = Sum(
            devices,
            line,
            down_group(
                line_table,
                [(by_units(at.l_active, True), 1), (by_units(at.l_active_got, True), 1)],
                [
                    (upstream, books * frames, lambda j, t: (t[0], 0, t[0])),
                    (upstream, books * frames, lambda j, t: (1 - t[0], 0, t[0])),
                ],
            ),
            along_z=True,
        )

    def g_units():
        at.active_got = devices.swap(
            place_units(line, down_table, at.active_units, micros * frames, (far.start, len(far))),
            0,
        )

    def g_place():
        at.placed, placed_far = place_columns(
            line, here, [(at.kept, i) for i in range(3)], micros * frames, spots, True
        )
        at.placed_got = devices.swap(placed_far, 0)

    def l_place():
        placed = place_columns(
            line, here, [at.l_normed, at.l_mixture, at.l_normed_two], books * frames, line_spots
        )
        at.l_placed_got = devices.cores(placed)
        at.l_lefts = [(placed, 1), (at.l_placed_got, 5)]

    def l_mlp_back():
        at.l_low, dz_own, dz_other, at.l_dm, at.l_do, at.l_gain_two = mlp_backward(
            line,
            here,
            (upstream, same, zero, books * frames),
            (at.l_slope, 0, zero),
            (at.l_middle[None], 0, zero),
            w_out_l,
            gains_l[1],
            w_up_l,
            w_down_l,
        )
        at.l_dz = both(dz_own, dz_other)

    def l_attn_back():
        grads = (at.l_do, at.l_low)
        at.l_dp = local_attn(line, here, at.l_packed, books, grads)
        at.l_rights = both(*at.l_dp)

    def l_qkv_back():
        at.local_grad, at.frame_grad, at.l_gain_one = qkv_backward(
            line, here, *at.l_dp, (at.l_rows, zero), at.l_dm, gains_l[0], w_qkv_l, books
        )
        at.g_frame = all_rows(at.frame_grad, at.frame_grad)

    def l_output():
        at.local_out = halves(at.l_out.reshape(books, frames, features))
        line.wait(at.local_out)

    def g_mlp_back():
        at.g_low, dz_own, dz_other, at.g_dm, at.g_do, at.g_gain_two = mlp_backward(
            line,
            here,
            (at.frame_grad, zero, zero, frames),
            (at.active, 1, same),
            (at.kept, 6, same),
            w_out_g,
            gains_g[1],
            w_up_g,
            w_down_g,
        )
        at.g_dz = all_rows(dz_own, dz_other)

    def g_attn_back():
        grads = (at.g_do, at.g_low)
        at.g_dp = global_attn_backward(line, here, at.kept, 3, item_lengths, grads)
        at.g_rights = all_rows(*at.g_dp)

    def g_qkv_back():
        at.global_grad, _, at.g_gain_one = qkv_backward(
            line, here, *at.g_dp, (at.rows, same), at.g_dm, gains_g[0], w_qkv_g, 1
        )

    def g_gains():
        gains = [at.g_gain_one, at.g_gain_two, at.l_gain_one, at.l_gain_two]
        gains = jnp.concatenate(gains)
        at.gains = gains + devices.swap(gains, 0)
        line.wait(at.gains)

    def g_output():
        at.embed_grad = halves(
            at.local_grad.reshape(books, frames, features) + (at.global_grad * scale_in)[None]
        )
        line.wait(at.embed_grad)

    def down_out():
        (at.down,) = both_halves(line, here, devices, at.g_down, at.l_down, (1,))

    def up_out():
        (at.up,) = both_halves(line, here, devices, at.g_up, at.l_up, (1,))

    def rest_out():
        at.qkv, at.out = both_halves(line, here, devices, at.g_rest, at.l_rest, (3, 1))

    def make(name):
        if not hasattr(at, name):
            if name == "l_up":
                one = Sum(devices, line, up_group(at.l_lefts, at.l_dz), along_z=True)
            elif name == "l_rest":
                one = Sum(devices, line, rest_group(at.l_lefts, at.l_rights), along_z=True)
            elif name == "g_down":
                lefts = [(at.active_units, 1), (at.active_got, 1 + units)]
                rights = [(a, count, lambda j, t, i=i: (0, i, t[0])) for a, count, i in at.g_frame]
                one = Sum(devices, line, down_group(down_table, lefts, rights), 1)
            else:
                lefts = [(at.placed, 1), (at.placed_got, 1)]
                if name == "g_up":
                    one = Sum(devices, line, up_group(lefts, at.g_dz), 1)
                    one.rider = at.gains
                else:
                    one = Sum(devices, line, rest_group(lefts, at.g_rights), 1)
            setattr(at, name, one)
        return getattr(at, name)

    steps = (g_qkv, g_attn, g_mlp, g_pack, l_qkv, l_attn, l_mlp, g_units, g_place, l_place)
    steps += (l_mlp_back, l_attn_back, l_qkv_back, l_output)
    steps += (g_mlp_back, g_attn_back, g_qkv_back, g_gains, g_output)
    steps += (down_out, up_out, rest_out)
    steps = {step.__name__: step for step in steps}
    for words in PLAN:
        name, *rest = words.split()
        if name in steps:
            steps[name]()
        elif name == "wait":
            one = getattr(at, rest[0])
            one = getattr(one, rest[1]) if rest[1:] not in ([], ["far"]) else one
            line.wait(one[2 if "far" in rest else 1][0] if isinstance(one, list) else one)
        else:
            getattr(make(name), rest[0])()
    gain_sums = at.g_up.rider
    gain_sums = gain_sums + devices.cores(gain_sums)
    gain_sums = jnp.where(first_core, gain_sums[:2], gain_sums[2:]).reshape(2, size, -1)
    gain_sums = lax.dynamic_index_in_dim(gain_sums, devices.index, 1, keepdims=False)

    return (
        at.local_out,
        at.embed_grad,
        gain_sums[:1],
        at.qkv,
        at.out,
        gain_sums[1:],
        at.up,
        at.down,
    )


def solution(mesh):
    in_specs = (
        P(None, "dp", None, None),
        P(None, "dp", None),
        P("section", None),
        P("section", None, None),
        P("section", None, None),
        P("section", None),
        P("section", None, None),
        P("section", None, None),
        P(None, "dp", None, None),
    )
    out_specs = (
        P(None, "dp", None, "section"),
        P(None, "dp", None, "section"),
        P("section", "dp"),
        P("section", "dp", None),
        P("section", "dp", None),
        P("section", "dp"),
        P("section", "dp", None),
        P("section", "dp", None),
    )
    return jax.shard_map(local, mesh=mesh, in_specs=in_specs, out_specs=out_specs, check_vma=False)
```

```python
import functools
import types

import jax
import jax.numpy as jnp
from jax import lax
from jax.experimental import pallas as pl
from jax.experimental.pallas import tpu as pltpu
from jax.sharding import PartitionSpec as P

HEADS = 16
EPSILON = 1e-05
BF16 = jnp.bfloat16
F32 = jnp.float32
VMEM_LIMIT = 48 * 1024 * 1024
CHUNK = 128
COST = 1.0
COST_SUMS = 1.0
LINE, NEAR, FAR = range(3)
DOWN_KIND = FAR
REST_KIND = NEAR
LOCAL_DOWN_KIND = LINE
LOCAL_REST_KIND = LINE
RIDER = 16
UNIT = 256


def dot(left, right):
    return jnp.dot(left, right, preferred_element_type=F32)


def dot_t(left, right):
    return lax.dot_general(left, right, (((1,), (1,)), ((), ())), preferred_element_type=F32)


def t_dot(left, right):
    return lax.dot_general(left, right, (((0,), (0,)), ((), ())), preferred_element_type=F32)


def add_all(terms):
    return functools.reduce(lambda s, t: s + t, terms)


def sds(shape, dtype=BF16):
    return jax.ShapeDtypeStruct(shape, dtype)


class Weight:
    def __init__(self, given, block, index, tiles):
        self.arrays = list(given) if isinstance(given, tuple) else [given]
        self.block, self.index, self.tiles = block, index, tiles
        self.slots = min(tiles, 2)


class Tiles:
    def __init__(self, weight, core, refs, held, sems):
        self.weight, self.core, self.refs, self.held, self.sems = weight, core, refs, held, sems

    def copy(self, place, j):
        block = self.weight.block
        at = zip(self.weight.index(j, self.core), block)
        at = tuple(pl.ds(pl.multiple_of(i * b, b), b) for i, b in at)
        slot = j % self.weight.slots
        return pltpu.make_async_copy(self.refs[place].at[at], self.held.at[slot], self.sems.at[slot])

    def start(self, j):
        for place in range(len(self.refs)):
            if len(self.refs) == 1:
                self.copy(place, j).start()
            else:

                @pl.when(self.core == place)
                def _():
                    self.copy(place, j).start()

    def get(self, j):
        self.copy(0, j).wait()
        return self.held[j % self.weight.slots]

    def ahead(self, j):
        @pl.when(j == 0)
        def _():
            self.start(0)

        if self.weight.tiles > 1:

            @pl.when(j + 1 < self.weight.tiles)
            def _():
                self.start(j + 1)


class Line:
    def __init__(self):
        self.behind = []

    def wait(self, *arrays):
        self.behind.extend(arrays)

    def launch(self, kernel, name, scalars, grid, ins, outs, scratch=(), flops=0):
        arrays, specs, counts, held = [], [], [], []
        for operand in ins:
            if isinstance(operand, Weight):
                specs.extend([pl.BlockSpec(memory_space=pl.ANY)] * len(operand.arrays))
                arrays.extend(operand.arrays)
                counts.append(operand)
                held.append(pltpu.VMEM((operand.slots,) + operand.block, operand.arrays[0].dtype))
                held.append(pltpu.SemaphoreType.DMA((operand.slots,)))
                continue
            given, block, index = operand
            if isinstance(given, tuple):
                for place in range(2):

                    def at(*args, place=place, index=index):
                        here = args[len(grid)][0] == place
                        return tuple(jnp.where(here, i, 0) for i in index(*args))

                    specs.append(pl.BlockSpec(block, at))
                arrays.extend(given)
                counts.append(2)
            else:
                specs.append(pl.BlockSpec(block, index))
                arrays.append(given)
                counts.append(1)
        skipped = len(self.behind)
        arrays.extend(self.behind)
        specs.extend([pl.BlockSpec(memory_space=pl.ANY)] * skipped)

        def body(*refs):
            scalar_refs, refs = refs[: len(scalars)], refs[len(scalars) :]
            groups, own = [], refs[len(refs) - len(held) :]
            for count in counts:
                if isinstance(count, Weight):
                    weight, count = count, len(count.arrays)
                    core = scalar_refs[0][0]
                    groups.append(Tiles(weight, core, list(refs[:count]), *own[:2]))
                    own = own[2:]
                else:
                    groups.append(list(refs[:count]))
                refs = refs[count:]
            refs = refs[skipped : len(refs) - len(held)]
            kernel(scalar_refs, groups, refs[: len(outs)], refs[len(outs) :])

        share = COST_SUMS if name == "weight_grad" else COST
        out = pl.pallas_call(
            body,
            grid_spec=pltpu.PrefetchScalarGridSpec(
                num_scalar_prefetch=len(scalars),
                grid=grid,
                in_specs=specs,
                out_specs=[pl.BlockSpec(block, index) for _, block, index in outs],
                scratch_shapes=list(scratch) + held,
            ),
            out_shape=[shape for shape, _, _ in outs],
            compiler_params=pltpu.CompilerParams(vmem_limit_bytes=VMEM_LIMIT),
            cost_estimate=pl.CostEstimate(
                flops=int(flops * share),
                bytes_accessed=int(share * sum(a.size * a.dtype.itemsize for a in arrays[: len(specs) - skipped])),
                transcendentals=0,
            ),
            name=name,
        )(*scalars, *arrays)
        self.behind = [out[0]]
        return out


def read(core, refs):
    if len(refs) == 1:
        return refs[0][...]
    return jnp.where(core == 0, refs[0][...], refs[1][...])


def origin(rank):
    return lambda *_: (0,) * rank


def whole(array):
    return array, array.shape, origin(array.ndim)


def full(shape, dtype=BF16):
    return sds(shape, dtype), shape, origin(len(shape))


def rstd(rows):
    return lax.rsqrt(jnp.mean(rows * rows, axis=-1, keepdims=True) + EPSILON)


def by_chunks(rows, step):
    def one(i, carry):
        step(pl.ds(pl.multiple_of(i * CHUNK, CHUNK), CHUNK))
        return carry

    lax.fori_loop(0, rows // CHUNK, one, 0)


def norm_backward(grad, rows, gain):
    scale = rstd(rows)
    plain = rows * scale
    grad_gain = jnp.sum(grad * plain, axis=0, keepdims=True)
    lead = grad * gain
    return scale * (lead - plain * jnp.mean(lead * plain, axis=-1, keepdims=True)), grad_gain


def gelu_parts(hidden):
    c = 0.7978845608028654
    square = hidden * hidden
    t = jnp.tanh(hidden * (c + (c * 0.044715) * square))
    half = 0.5 + 0.5 * t
    slope = half + (hidden * half) * ((1.0 - t) * (c + (3 * 0.044715 * c) * square))
    return (hidden * half).astype(BF16), slope.astype(BF16)


def qkv_forward(line, here, parts, make_rows, gain, w_qkv, tile=1024):
    features = gain[0].shape[1] if isinstance(gain, tuple) else gain.shape[1]
    count, wide = parts[0], 3 * features

    def kernel(scalars, ins, outs, _):
        core = scalars[0][0]
        gain_refs, w = ins[-2:]
        x_ref, h_ref, p_ref = outs
        j = pl.program_id(0)
        w.ahead(j)

        @pl.when(j == 0)
        def _():
            gain = read(core, gain_refs)
            for i, x in enumerate(make_rows(core, ins[:-2])):
                at = slice(i * CHUNK, (i + 1) * CHUNK)
                x_ref[at, :] = x
                h_ref[at, :] = (x * rstd(x) * gain).astype(BF16)

        p_ref[...] = dot(h_ref[...], w.get(j)).astype(BF16)

    return line.launch(
        kernel,
        "qkv_forward",
        [here],
        (wide // tile,),
        parts[1]
        + [
            (gain, (1, features), origin(2)),
            Weight(w_qkv, (features, tile), lambda j, core: (0, j), wide // tile),
        ],
        [
            full((count, features), F32),
            full((count, features)),
            (sds((count, wide)), (count, tile), lambda j, s: (0, j)),
        ],
        flops=2 * count * features * wide,
    )


def mlp_forward(line, here, rows, mixture, w_out, gain, w_up, w_down, joined, tile=1024):
    count, features = rows.shape
    wide = (w_up[0] if isinstance(w_up, tuple) else w_up).shape[1]

    def kernel(scalars, ins, outs, scratch):
        core = scalars[0][0]
        (x_ref,), (o_ref,), w_out, gain_refs, w_up, w_down = ins
        y_ref, m_ref, h_ref = outs[:3]
        (acc_ref,) = scratch
        j = pl.program_id(0)
        for w in (w_out, w_up, w_down):
            w.ahead(j)

        @pl.when(j == 0)
        def _():
            gain, wide_out = read(core, gain_refs), w_out.get(0)

            def step(at):
                m = x_ref[at, :] + dot(o_ref[at, :], wide_out)
                m_ref[at, :] = m
                acc_ref[at, :] = m
                h_ref[at, :] = (m * rstd(m) * gain).astype(BF16)

            by_chunks(count, step)

        g, slope = gelu_parts(dot(h_ref[...], w_up.get(j)))
        if joined:
            outs[3][0] = g
            outs[3][1] = slope
        else:
            outs[3][0] = g
            outs[4][0] = slope
        acc_ref[...] += dot(g, w_down.get(j))

        @pl.when(pl.program_id(0) == pl.num_programs(0) - 1)
        def _():
            y_ref[...] = acc_ref[...].astype(BF16)

    planes = 2 if joined else 1
    wide_out = (sds((planes, count, wide)), (planes, count, tile), lambda j, s: (0, 0, j))
    return line.launch(
        kernel,
        "mlp_forward",
        [here],
        (wide // tile,),
        [
            whole(rows),
            whole(mixture),
            Weight(w_out, (features, features), lambda j, core: (0, 0), 1),
            (gain, (1, features), origin(2)),
            Weight(w_up, (features, tile), lambda j, core: (0, j), wide // tile),
            Weight(w_down, (tile, features), lambda j, core: (j, 0), wide // tile),
        ],
        [full(rows.shape), full(rows.shape, F32), full(rows.shape)] + [wide_out] * (3 - planes),
        [pltpu.VMEM(rows.shape, F32)],
        flops=2 * count * features * (features + 2 * wide),
    )


def mlp_backward(line, here, low_out, slope, middle, w_out, gain, w_up, w_down, tile=1024):
    wide, features = w_down[0].shape
    count = low_out[3]
    tiles = wide // tile
    half = tiles // 2

    def kernel(scalars, ins, outs, scratch):
        core = scalars[0][0]
        (dy_ref,), s_refs, m_refs, gain_refs, w_down, w_up, w_out = ins
        low_ref, own_ref, other_ref, dm_ref, do_ref, gg_ref = outs
        (acc_ref,) = scratch
        j = pl.program_id(0)
        for w in (w_down, w_up, w_out):
            w.ahead(j)
        slope = read(core, s_refs)[0].astype(F32)
        dz = (slope * dot_t(dy_ref[0], w_down.get(j))).astype(BF16)

        @pl.when(j < half)
        def _():
            other_ref[0] = dz

        @pl.when(j >= half)
        def _():
            own_ref[0] = dz

        term = dot_t(dz, w_up.get(j))

        @pl.when(j == 0)
        def _():
            acc_ref[...] = term

        @pl.when(j > 0)
        def _():
            acc_ref[...] += term

        @pl.when(j == tiles - 1)
        def _():
            gg_ref[...] = jnp.zeros_like(gg_ref)
            gain, wide_out = read(core, gain_refs), w_out.get(0)

            def step(at):
                if len(m_refs) == 1:
                    m = m_refs[0][0, at, :].astype(F32)
                else:
                    m = jnp.where(core == 0, m_refs[0][0, at, :], m_refs[1][0, at, :]).astype(F32)
                dm, gg = norm_backward(acc_ref[at, :], m, gain)
                gg_ref[...] += gg
                dm = dm + dy_ref[0, at, :].astype(F32)
                dm_ref[at, :] = dm
                low = dm.astype(BF16)
                low_ref[at, :] = low
                do_ref[at, :] = dot_t(low, wide_out).astype(BF16)

            by_chunks(count, step)

    def at(j, core):
        return (j + (1 - core) * half) % tiles

    shape = (count, features)
    return line.launch(
        kernel,
        "mlp_backward",
        [here],
        (tiles,),
        [
            (low_out[0], (1,) + shape, lambda j, s: (low_out[1](s[0]), low_out[2](s[0]), 0)),
            (slope[0], (1, count, tile), lambda j, s: (slope[1], slope[2](s[0]), at(j, s[0]))),
            (middle[0], (1,) + shape, lambda j, s: (middle[1], middle[2](s[0]), 0)),
            (gain, (1, features), origin(2)),
            Weight(w_down, (tile, features), lambda j, core: (at(j, core), 0), tiles),
            Weight(w_up, (features, tile), lambda j, core: (0, at(j, core)), tiles),
            Weight(w_out, (features, features), lambda j, core: (0, 0), 1),
        ],
        [
            full(shape),
            (
                sds((1, count, wide // 2)),
                (1, count, tile),
                lambda j, s: (0, 0, jnp.maximum(j - half, 0)),
            ),
            (
                sds((1, count, wide // 2)),
                (1, count, tile),
                lambda j, s: (0, 0, jnp.minimum(j, half - 1)),
            ),
            full(shape, F32),
            full(shape),
            full((1, features), F32),
        ],
        [pltpu.VMEM(shape, F32)],
        flops=2 * count * features * (features + 2 * wide),
    )


def qkv_backward(line, here, own, other, rows, grad_middle, gain, w_qkv, books, tile=512):
    count, features = grad_middle.shape
    frames = count // books

    def kernel(scalars, ins, outs, scratch):
        core = scalars[0][0]
        (own_ref,), (other_ref,), (x_ref,), (dm_ref,), gain_refs, w_tiles = ins
        dx_ref, sum_ref, gg_ref = outs
        (acc_ref,) = scratch
        j = pl.program_id(0)
        w_tiles.ahead(j)
        w = w_tiles.get(j)
        terms = []
        for i in range(3):
            part = jnp.where(core == i // 2, own_ref[i % 2], other_ref[i % 2])
            terms.append(dot_t(part, w[:, i * features : (i + 1) * features]))
        acc_ref[:, pl.ds(pl.multiple_of(j * tile, tile), tile)] = add_all(terms)

        @pl.when(j == pl.num_programs(0) - 1)
        def _():
            gg_ref[...] = jnp.zeros_like(gg_ref)
            gain = read(core, gain_refs)
            total = 0.0
            for b in range(books):
                at = slice(b * frames, (b + 1) * frames)
                dx, gg = norm_backward(acc_ref[at, :], x_ref[at, :], gain)
                gg_ref[...] += gg
                dx = dx + dm_ref[at, :]
                dx_ref[at, :] = dx
                total = total + dx
            sum_ref[0] = total.astype(BF16)

    shape = (count, features)
    return line.launch(
        kernel,
        "qkv_backward",
        [here],
        (features // tile,),
        [
            whole(own),
            whole(other),
            (rows[0], shape, lambda j, s: (rows[1](s[0]), 0)),
            whole(grad_middle),
            (gain, (1, features), origin(2)),
            Weight(w_qkv, (tile, 3 * features), lambda j, core: (j, 0), features // tile),
        ],
        [full(shape, F32), full((1, frames, features)), full((1, features), F32)],
        [pltpu.VMEM(shape, F32)],
        flops=6 * count * features * features,
    )


def head_sum(product, reduce_mat):
    high = product.astype(BF16)
    low = (product - high.astype(F32)).astype(BF16)
    return dot(high, reduce_mat) + dot(low, reduce_mat)


def head_mats(lanes, width):
    row = lax.broadcasted_iota(jnp.int32, (lanes, 128), 0)
    col = lax.broadcasted_iota(jnp.int32, (lanes, 128), 1)
    reduce_mat = (row // width == col).astype(BF16)
    row = lax.broadcasted_iota(jnp.int32, (128, lanes), 0)
    col = lax.broadcasted_iota(jnp.int32, (128, lanes), 1)
    return reduce_mat, (col // width == row).astype(BF16)


def local_probs(q, k, reduce_mat, scale):
    probs = {}
    for a in range(len(q)):
        scores = [head_sum(q[a] * k[b], reduce_mat) * scale for b in range(a + 1)]
        peak = functools.reduce(jnp.maximum, scores)
        parts = [jnp.exp(s - peak) for s in scores]
        total = add_all(parts)
        for b in range(a + 1):
            probs[a, b] = parts[b] / total
    return probs


def local_attn_fwd_kernel(width, q_ref, k_ref, v_ref, o_ref):
    books, _, lanes = q_ref.shape
    reduce_mat, expand_mat = head_mats(lanes, width)
    q = [q_ref[a].astype(F32) for a in range(books)]
    k = [k_ref[a].astype(F32) for a in range(books)]
    v = [v_ref[a].astype(F32) for a in range(books)]
    probs = local_probs(q, k, reduce_mat, width**-0.5)
    for a in range(books):
        mixed = [dot(probs[a, b].astype(BF16), expand_mat) * v[b] for b in range(a + 1)]
        o_ref[a] = add_all(mixed).astype(BF16)


def by_half(core, parts, own_ref, other_ref):
    for c in range(2):

        @pl.when(core == c)
        def _():
            for i in range(2):
                own_ref[i] = parts[2 * c + i]
                other_ref[i] = parts[2 - 2 * c + i]


def local_attn_bwd_kernel(
    width, core, q_ref, k_ref, v_ref, g_ref, m_ref, own_ref, other_ref
):
    books, _, lanes = q_ref.shape
    scale = width**-0.5
    reduce_mat, expand_mat = head_mats(lanes, width)
    q = [q_ref[a].astype(F32) for a in range(books)]
    k = [k_ref[a].astype(F32) for a in range(books)]
    v = [v_ref[a].astype(F32) for a in range(books)]
    g = [g_ref[a].astype(F32) for a in range(books)]
    probs = local_probs(q, k, reduce_mat, scale)
    dq = [0.0] * books
    dk = [0.0] * books
    dv = [0.0] * books
    for a in range(books):
        dprobs = [head_sum(g[a] * v[b], reduce_mat) for b in range(a + 1)]
        inner = add_all([dprobs[b] * probs[a, b] for b in range(a + 1)])
        for b in range(a + 1):
            dscore = dot((probs[a, b] * (dprobs[b] - inner)).astype(BF16), expand_mat)
            dq[a] = dq[a] + dscore * k[b]
            dk[b] = dk[b] + dscore * q[a]
            dv[b] = dv[b] + dot(probs[a, b].astype(BF16), expand_mat) * g[a]
    parts = [
        jnp.stack([(one * by).astype(BF16) for one in ones])
        for ones, by in ((dq, scale), (dk, scale), (dv, 1.0))
    ]
    by_half(core, parts + [m_ref[...]], own_ref, other_ref)


def local_attn(line, here, packed, books, grads=None, lanes=512):
    count, wide = packed.shape
    features, frames = wide // 3, count // books
    width, groups = features // HEADS, features // lanes
    packed = packed.reshape(books, frames, wide)
    shape, block = (books, frames, features), (books, frames, lanes)

    def at(part):
        return lambda h, *_: (0, 0, part * groups + h)

    ins = [(packed, block, at(i)) for i in range(3)]
    if grads is None:

        def forward(scalars, ins, outs, _):
            local_attn_fwd_kernel(width, *[i[0] for i in ins], *outs)

        out = line.launch(
            forward,
            "local_attn_forward",
            [here],
            (groups,),
            ins,
            [(sds(shape), block, at(0))],
            flops=4000 * count * features,
        )
        return out[0].reshape(count, features)

    def backward(scalars, ins, outs, _):
        local_attn_bwd_kernel(width, scalars[0][0], *[i[0] for i in ins], *outs)

    ins += [(g.reshape(shape), block, at(0)) for g in grads]
    half = (sds((2,) + shape), (2,) + block, lambda h, *_: (0, 0, 0, h))
    out = line.launch(
        backward,
        "local_attn_backward",
        [here],
        (groups,),
        ins,
        [half] * 2,
        flops=10000 * count * features,
    )
    return [one.reshape(2, count, features) for one in out]


def item_mask(lengths_ref, micro, frames, items):
    row = lax.broadcasted_iota(jnp.int32, (frames, frames), 0)
    col = lax.broadcasted_iota(jnp.int32, (frames, frames), 1)
    row_item = jnp.zeros((frames, frames), jnp.int32)
    col_item = jnp.zeros((frames, frames), jnp.int32)
    end = 0
    for i in range(items):
        end = end + lengths_ref[micro, 0, i]
        row_item = row_item + (row >= end).astype(jnp.int32)
        col_item = col_item + (col >= end).astype(jnp.int32)
    return (row_item == col_item) & (row >= col)


def head_parts(block, width):
    per = 128 // width
    lane = lax.broadcasted_iota(jnp.int32, (block.shape[0], 128), 1)
    parts = []
    for h in range(block.shape[1] // width):
        tile = block[:, (h // per) * 128 : (h // per + 1) * 128]
        parts.append(jnp.where(lane // width == h % per, tile, jnp.zeros_like(tile)))
    return parts


def frame_probs(q, k, mask, scale):
    scores = jnp.where(mask, dot_t(q, k) * scale, -1e30)
    parts = jnp.exp(scores - jnp.max(scores, axis=-1, keepdims=True))
    return parts / jnp.sum(parts, axis=-1, keepdims=True)


def global_attn_fwd_kernel(width, items, lengths_ref, q_ref, k_ref, v_ref, o_ref):
    frames, lanes = q_ref.shape
    mask = item_mask(lengths_ref, pl.program_id(0), frames, items)
    per = 128 // width
    q = head_parts(q_ref[...], width)
    v = head_parts(v_ref[...], width)
    mixed = [0.0] * (lanes // 128)
    for h in range(lanes // width):
        tile = slice((h // per) * 128, (h // per + 1) * 128)
        probs = frame_probs(q[h], k_ref[:, tile], mask, width**-0.5)
        mixed[h // per] = mixed[h // per] + dot(probs.astype(BF16), v[h])
    for i, tile in enumerate(mixed):
        o_ref[:, i * 128 : (i + 1) * 128] = tile.astype(BF16)


def global_attn_bwd_kernel(
    width, items, core, lengths_ref, q, k, v, g_ref, m_ref, own_ref, other_ref
):
    frames, lanes = q.shape
    scale = width**-0.5
    mask = item_mask(lengths_ref, core, frames, items)
    per = 128 // width
    q = head_parts(q, width)
    wide_k, k = k, head_parts(k, width)
    g = head_parts(g_ref[...], width)
    tiles = lanes // 128
    dq, dk, dv = [0.0] * tiles, [0.0] * tiles, [0.0] * tiles
    for h in range(lanes // width):
        t = h // per
        tile = slice(t * 128, (t + 1) * 128)
        probs = frame_probs(q[h], wide_k[:, tile], mask, scale)
        dv[t] = dv[t] + t_dot(probs.astype(BF16), g[h])
        dprobs = dot_t(g[h], v[:, tile])
        inner = jnp.sum(dprobs * probs, axis=-1, keepdims=True)
        dscore = (probs * (dprobs - inner)).astype(BF16)
        dq[t] = dq[t] + dot(dscore, k[h])
        dk[t] = dk[t] + t_dot(dscore, q[h])
    parts = [
        jnp.concatenate([(one * by).astype(BF16) for one in ones], axis=1)
        for ones, by in ((dq, scale), (dk, scale), (dv, 1.0))
    ]
    by_half(core, parts + [m_ref[...]], own_ref, other_ref)


def global_attn_forward(line, packed, lengths, lanes=1024):
    micros, _, items = lengths.shape
    count, wide = packed.shape
    features, frames = wide // 3, count // micros
    width, groups = features // HEADS, features // lanes
    block = (frames, lanes)

    def at(part):
        return lambda m, h, _: (m, part * groups + h)

    def kernel(scalars, ins, outs, _):
        global_attn_fwd_kernel(width, items, scalars[0], *[i[0] for i in ins], *outs)

    return line.launch(
        kernel,
        "global_attn_forward",
        [lengths],
        (micros, groups),
        [(packed, block, at(i)) for i in range(3)],
        [(sds((count, features)), block, at(0))],
        flops=10000 * count * features,
    )[0]


def global_attn_backward(line, here, kept, first, lengths, grads, lanes=1024):
    micros, _, items = lengths.shape
    _, count, features = kept[0].shape
    frames = count // micros
    width, groups = features // HEADS, features // lanes
    block = (frames, lanes)

    def kernel(scalars, ins, outs, _):
        core = scalars[0][0]
        q, k, v = [read(core, i)[0] for i in ins[:3]]
        global_attn_bwd_kernel(
            width, items, core, scalars[1], q, k, v, ins[3][0], ins[4][0], *outs
        )

    half = (sds((2, frames, features)), (2,) + block, lambda h, *_: (0, 0, h))
    return line.launch(
        kernel,
        "global_attn_backward",
        [here, lengths],
        (groups,),
        [(kept, (1,) + block, lambda h, c, _, i=i: (first + i, c[0], h)) for i in range(3)]
        + [(g, block, lambda h, *_: (0, h)) for g in grads],
        [half] * 2,
        flops=30000 * frames * features,
    )


def place_columns(line, here, sources, rows, spots, cut=False):
    features = spots.shape[0]

    def kernel(scalars, ins, outs, _):
        for i, refs in enumerate(ins[1:]):
            block = read(scalars[0][0], refs).reshape(rows, features)
            placed = dot(block, ins[0][0][...]).astype(BF16)
            wide = features // len(outs)
            for k, out in enumerate(outs):
                out[i] = placed[:, k * wide : (k + 1) * wide]

    ins = [whole(spots)]
    for source in sources:
        if isinstance(source, tuple):
            ins.append((source[0], (1, rows, features), lambda _, s, plane=source[1]: (plane, 0, 0)))
        else:
            ins.append(whole(source))
    parts = 2 if cut else 1
    out = line.launch(
        kernel,
        "place_columns",
        [here],
        (1,),
        ins,
        [full((len(sources), rows, features // parts))] * parts,
        flops=2 * len(sources) * rows * features * features,
    )
    return out if cut else out[0]


def place_units(line, table, source, rows, units):
    per = 4

    def kernel(scalars, ins, outs, _):
        for i in range(per):
            outs[0][0, :, i * UNIT : (i + 1) * UNIT] = read(scalars[0][0], ins[i])[0]

    first, count = units

    def at(i):
        return lambda u, t: (0, 0, t[1 + first + u * per + i])

    return line.launch(
        kernel,
        "place_units",
        [table],
        (count // per,),
        [(source, (1, rows, UNIT), at(i)) for i in range(per)],
        [(sds((1, rows, count * UNIT)), (1, rows, per * UNIT), lambda u, t: (0, 0, u))],
    )[0]


def pack(line, here, arrays, features):
    count = arrays[0].shape[0]
    planes = [(i, c) for i, a in enumerate(arrays) for c in range(a.shape[1] // features)]

    def kernel(scalars, ins, outs, _):
        for plane, (i, c) in enumerate(planes):
            outs[0][plane] = ins[i][0][:, c * features : (c + 1) * features].astype(BF16)

    return line.launch(
        kernel,
        "pack",
        [here],
        (1,),
        [whole(a) for a in arrays],
        [full((len(planes), count, features))],
    )[0]


class Group:
    def __init__(self, table, units, lefts, rights, tile, tiles, plane):
        self.table, self.per = table, units // 4
        self.lefts, self.rights = lefts, rights
        self.tile, self.tiles, self.plane = tile, tiles, plane


def joined(core, blocks, ordered):
    if ordered:
        pairs = []
        for a, b in zip(blocks[::2], blocks[1::2]):
            pairs += [jnp.where(core == 0, a, b), jnp.where(core == 0, b, a)]
        blocks = pairs
    return blocks[0] if len(blocks) == 1 else jnp.concatenate(blocks, axis=0)


def weight_grad(line, group, first, steps, per, addends, split):
    lefts, rights, tile = group.lefts, group.rights, group.tile

    def kernel(scalars, ins, outs, _):
        core = scalars[0][0]
        left_refs = [ins[i * per : (i + 1) * per] for i in range(len(lefts))]
        ins = ins[len(lefts) * per :]
        right = joined(
            core, [r[0][0] for r in ins[: len(rights)]], len(rights) > len(lefts)
        )
        add_refs = [r[0] for r in ins[len(rights) :]]
        for i in range(per):
            at = slice(i * UNIT, (i + 1) * UNIT)
            left = joined(
                core, [read(core, r[i])[0] for r in left_refs], len(lefts) > len(rights)
            )
            out = add_all([t_dot(left, right)] + [r[at, :].astype(F32) for r in add_refs])
            out = out.astype(BF16)
            if not split:
                outs[0][at, :] = out
            elif per == 1:
                outs[0][...] = out[: UNIT // 2]
                outs[1][...] = out[UNIT // 2 :]
            else:
                half = per // 2
                outs[i // half][(i % half) * UNIT : (i % half + 1) * UNIT, :] = out

    def left_in(given, start, i):
        rows = (given[0] if isinstance(given, tuple) else given).shape[1]
        return (
            given,
            (1, rows, UNIT),
            lambda u, j, t: (group.plane(j, t), 0, t[start + first + u * per + i]),
        )

    def right_in(given, count, at):
        return given, (1, count, tile), lambda u, j, t: at(j, t)

    def block(skip, rows=per * UNIT):
        return (rows, tile), lambda u, j, t: (skip + u, j)

    wide = group.tiles * tile
    rows = sum(count for _, count, _ in rights)
    if split:
        outs = [(sds((per * UNIT // 2, wide)),) + block(0, per * UNIT // 2)] * 2
    else:
        outs = [(sds((steps * per * UNIT, wide)),) + block(0)]
    out = line.launch(
        kernel,
        "weight_grad",
        [group.table],
        (steps, group.tiles),
        [left_in(a, start, i) for a, start in lefts for i in range(per)]
        + [right_in(*right) for right in rights]
        + [(a,) + block(skip) for a, skip in addends],
        outs,
        flops=2 * steps * per * UNIT * wide * rows,
    )
    return out if split else out[0]


class Devices:
    def __init__(self, size):
        self.size = size
        self.core = lax.axis_index("section")
        self.index = lax.axis_index("dp")

    def bits(self, core, kind):
        near = [1, 2] if core == 0 else [2, 1]
        far = [1 << b for b in range(2, self.size.bit_length() - 1)]
        return far[:1] + near + far[1:] if kind == FAR else near + far

    def swap(self, array, step, kind):
        pairs = []
        for core in range(2):
            by = self.bits(core, kind)[step]
            pairs += [(core * self.size + i, core * self.size + (i ^ by)) for i in range(self.size)]
        return lax.ppermute(array, ("section", "dp"), pairs)

    def cores(self, array):
        return lax.ppermute(array, "section", [(0, 1), (1, 0)])

    def order(self, kind):
        orders = []
        for core in range(2):
            bits = self.bits(core, kind)
            if kind == LINE:
                bits = bits[:2] + bits[:1:-1]
            order = [
                sum(bit for i, bit in enumerate(bits) if (spot >> (len(bits) - 1 - i)) & 1)
                for spot in range(self.size)
            ]
            orders.append(jnp.array(order, jnp.int32))
        return jnp.where(self.core == 0, orders[0], orders[1]) ^ (
            self.index % 4 if kind == LINE else self.index
        )

    def columns(self, count, kind):
        block = count // self.size
        order = self.order(kind)
        return (order[:, None] * block + jnp.arange(block, dtype=jnp.int32)).reshape(-1)

    def spots(self, count, kind):
        at = self.columns(count, kind)[None, :]
        return (lax.broadcasted_iota(jnp.int32, (count, count), 0) == at).astype(BF16)

    def along_z(self, array):
        depth = self.size // 4
        groups = [[4 * z + place for z in range(depth)] for place in range(4)]
        return lax.psum_scatter(
            array, "dp", scatter_dimension=0, axis_index_groups=groups, tiled=True
        )

    def table(self, *orders):
        parts = [self.core[None].astype(jnp.int32)] + [jnp.asarray(o, jnp.int32) for o in orders]
        return jnp.concatenate(parts)


class Sum:
    def __init__(self, devices, line, group, step=0, kind=LINE):
        self.devices, self.line, self.group, self.step = devices, line, group, step
        self.one, self.kind = None, kind
        self.rider = None

    def grad(self, first, count, addends, split=False):
        group = self.group
        steps, per = (count, group.per) if group.per > 1 else (1, count)
        return weight_grad(self.line, group, first * group.per, steps, per, addends, split)

    def send(self, array):
        rows, columns = array.shape
        if self.rider is not None:
            shape, size = self.rider.shape, self.rider.size
            high = self.rider.astype(BF16)
            low = (self.rider - high.astype(F32)).astype(BF16)
            extra = jnp.concatenate([high, low]).reshape(-1, columns)
            extra = jnp.pad(extra, ((0, -extra.shape[0] % RIDER), (0, 0)))
            array = jnp.concatenate([array, extra])
        got = self.devices.swap(array, self.step, self.kind)
        if self.rider is not None:
            extra = got[rows:].astype(F32).reshape(-1)
            self.rider = self.rider + (extra[:size] + extra[size : 2 * size]).reshape(shape)
        self.step += 1
        return got

    def first(self):
        self.one = self.send(self.grad(2, 2, []))

    def second(self):
        self.two = self.send(self.grad(1, 1, [] if self.one is None else [(self.one, 1)]))

    def third(self):
        addends = [(one, 0) for one in (self.one, self.two) if one is not None]
        if self.kind == LINE:
            self.kept = self.devices.along_z(self.grad(0, 1, addends))
            return
        self.kept, sent = self.grad(0, 1, addends, split=True)
        self.got = self.send(sent)

    def rest(self):
        if self.kind == LINE:
            return
        steps = self.devices.size.bit_length() - 1
        total = self.kept
        while self.step < steps:
            got = self.got
            half = total.shape[0] // 2
            sent = (total[half:].astype(F32) + got[half : 2 * half].astype(F32)).astype(BF16)
            total = total[:half].astype(F32) + got[:half].astype(F32)
            if self.step < steps - 1:
                total = total.astype(BF16)
            self.line.wait(sent)
            self.got = self.send(sent)
        self.kept = total

    def last(self):
        return self.kept.astype(F32) + self.got[: self.kept.shape[0]].astype(F32)


PLAN = (
    "g_qkv",
    "g_attn",
    "g_mlp",
    "g_pack",
    "l_qkv",
    "l_attn",
    "l_mlp",
    "l_place",
    "l_down first",
    "l_mlp_back",
    "l_attn_back",
    "l_down second",
    "g_units",
    "g_place",
    "l_up first",
    "l_down third",
    "l_rest first",
    "l_down rest",
    "l_qkv_back",
    "wait l_down one",
    "l_output",
    "wait active_got",
    "g_mlp_back",
    "g_attn_back",
    "g_qkv_back",
    "wait placed_got",
    "g_gains",
    "l_rest second",
    "g_up second",
    "l_up second",
    "g_rest second",
    "l_up third",
    "g_output",
    "l_up rest",
    "g_up third",
    "g_down second",
    "l_rest third",
    "wait l_down kept",
    "g_rest third",
    "l_rest rest",
    "g_down third",
    "g_down rest",
    "g_rest rest",
    "g_up rest",
    "up_out",
    "rest_out",
    "wait g_dz far",
    "down_out",
)


def both_halves(line, here, devices, ours, theirs, parts):
    rows, wide = ours.kept.shape
    half = jax.ShapeDtypeStruct((rows, wide), BF16)
    operands = [[one.kept] if one.kind == LINE else [one.kept, one.got] for one in (ours, theirs)]
    count = len(operands[0])

    def split(scalars, ins, outs, _):
        core = scalars[0][0]
        terms = [i[0][:rows, :].astype(F32) for i in ins]
        mine, other = add_all(terms[:count]), add_all(terms[count:])
        outs[0][...] = jnp.where(core == 0, other, mine).astype(BF16)
        outs[1][...] = jnp.where(core == 0, mine, other)

    sent, mine = line.launch(
        split,
        "split_halves",
        [here],
        (1,),
        [whole(one) for one in operands[0] + operands[1]],
        [full(half.shape), full(half.shape, F32)],
    )
    got = devices.cores(sent)

    def join(scalars, ins, outs, _):
        core = scalars[0][0]
        mine, got = ins[0][0][...], ins[1][0][...].astype(F32)
        joined = jnp.concatenate(
            [jnp.where(core == 0, mine, got), jnp.where(core == 0, got, mine)], axis=1
        )
        start = 0
        for out in outs:
            out[0] = joined[:, start : start + out.shape[2]]
            start += out.shape[2]

    return line.launch(
        join,
        "join_halves",
        [here],
        (1,),
        [whole(mine), whole(got)],
        [full((1, rows, 2 * wide * part // sum(parts)), F32) for part in parts],
    )


def local(codebook_embed, item_lengths, gain_attn, w_qkv, w_out, gain_mlp, w_up, w_down, cotangent):
    size = lax.axis_size("dp")
    micros, frames, books, features = codebook_embed.shape
    half_width = features // 2
    scale_in = books**-0.5
    devices, line = Devices(size), Line()
    core = devices.core
    first_core = core == 0
    here = core[None].astype(jnp.int32)

    def zero(core):
        return 0

    def same(core):
        return core

    gains = jnp.stack([gain_attn[0], gain_mlp[0]])
    own = [w_qkv[0], w_out[0], w_up[0], w_down[0]]
    gains_other = devices.cores(gains)
    other = [devices.cores(w) for w in own]
    w_qkv_g, w_out_g, w_up_g, w_down_g = zip(own, other)
    w_qkv_l, w_out_l, w_up_l, w_down_l = zip(other, own)
    gains_g = [(gains[i : i + 1], gains_other[i : i + 1]) for i in range(2)]
    gains_l = [(b, a) for a, b in gains_g]

    embed = codebook_embed.transpose(0, 2, 1, 3)
    upstream = cotangent.transpose(0, 2, 1, 3).reshape(micros, -1, features)

    def with_first(array):
        return array, devices.cores(array)

    columns = w_down.shape[1]
    unit_rows = columns // size == UNIT
    units = columns // UNIT
    near, far = range(units // 2), range(units // 2, units)
    placed_table = devices.table([0, 1, 2, 3], [0, 2, 1, 3])
    down_order = devices.order(DOWN_KIND) if unit_rows else range(units)
    down_table = devices.table(down_order, range(units))
    local_table = devices.table(devices.order(LOCAL_DOWN_KIND) if unit_rows else range(units))
    spots = devices.spots(features, REST_KIND)
    local_spots = devices.spots(features, LOCAL_REST_KIND)

    def by_units(array, kind):
        if unit_rows:
            return array
        if isinstance(array, tuple):
            return tuple(by_units(a, kind) for a in array)
        return jnp.take(array[:1], devices.columns(columns, kind), axis=2)

    def down_group(table, lefts, rights):
        return Group(table, units, lefts, rights, half_width, 1, lambda j, t: 0)

    def up_group(lefts, rights):
        return Group(
            placed_table,
            4,
            lefts,
            [(a, count, lambda j, t, i=i: (0, i, j)) for a, count, i in rights],
            features,
            2,
            lambda j, t: 2,
        )

    def rest_group(lefts, rights):
        return Group(
            placed_table,
            4,
            lefts,
            [(a, count, lambda j, t, i=i: (j, i, 0)) for a, count, i in rights],
            features,
            2,
            lambda j, t: jnp.where(2 * t[0] + j == 3, 1, 0),
        )

    def my_half(array):
        return jnp.where(first_core, array[..., :half_width], array[..., half_width:])

    def other_half(array):
        return jnp.where(first_core, array[..., half_width:], array[..., :half_width])

    def halves(array):
        got = devices.cores(other_half(array).astype(BF16)).astype(array.dtype)
        mine = my_half(array)
        pair = jnp.where(first_core, jnp.stack([mine, got]), jnp.stack([got, mine]))
        return pair.transpose(0, 2, 1, 3)

    def both(mine, others):
        return [(mine, mine.shape[1], 0), (devices.cores(others), mine.shape[1], 0)]

    def all_rows(mine, others, kind):
        rights = both(mine, others)
        far = devices.swap(jnp.concatenate([rights[0][0], rights[1][0]], axis=1), 0, kind)
        return rights + [(far, frames, i) for i in range(micros)]

    at = types.SimpleNamespace()

    def g_qkv():
        def frame_rows(core, ins):
            (e_ref,) = ins[0]
            return [
                add_all([e_ref[m, b].astype(F32) for b in range(books)]) * scale_in
                for m in range(micros)
            ]

        at.rows, at.normed, at.packed = qkv_forward(
            line, here, (micros * frames, [whole(embed)]), frame_rows, gains[:1], own[0]
        )

    def g_attn():
        at.mixture = global_attn_forward(line, at.packed, item_lengths)

    def g_mlp():
        result, at.middle, at.normed_two, active = mlp_forward(
            line, here, at.rows, at.mixture, own[1], gains[1:], own[2], own[3], True
        )
        at.states, at.active = with_first(result), with_first(active)
        at.active_units = by_units(at.active, DOWN_KIND)

    def g_pack():
        arrays = [at.normed, at.mixture, at.normed_two, at.packed, at.middle]
        at.kept = with_first(pack(line, here, arrays, features))

    def l_qkv():
        def local_rows(core, ins):
            (e_ref,), s_refs = ins
            state = read(core, s_refs).astype(F32)
            return [e_ref[0, b].astype(F32) + state for b in range(books)]

        parts = [
            (embed, (1, books, frames, features), lambda j, s: (s[0], 0, 0, 0)),
            (at.states, (frames, features), lambda j, s: (s[0], 0)),
        ]
        at.l_rows, at.l_normed, at.l_packed = qkv_forward(
            line, here, (books * frames, parts), local_rows, gains_l[0], w_qkv_l
        )

    def l_attn():
        at.l_mixture = local_attn(line, here, at.l_packed, books)

    def l_mlp():
        at.l_out, at.l_middle, at.l_normed_two, at.l_active, at.l_slope = mlp_forward(
            line, here, at.l_rows, at.l_mixture, w_out_l, gains_l[1], w_up_l, w_down_l, False
        )
        at.l_active_got = devices.cores(at.l_active)
        at.l_down = Sum(
            devices,
            line,
            down_group(
                local_table,
                [
                    (by_units(at.l_active, LOCAL_DOWN_KIND), 1),
                    (by_units(at.l_active_got, LOCAL_DOWN_KIND), 1),
                ],
                [
                    (upstream, books * frames, lambda j, t: (t[0], 0, t[0])),
                    (upstream, books * frames, lambda j, t: (1 - t[0], 0, t[0])),
                ],
            ),
            kind=LOCAL_DOWN_KIND,
        )

    def g_units():
        at.active_got = devices.swap(
            place_units(line, down_table, at.active_units, micros * frames, (far.start, len(far))),
            0,
            DOWN_KIND,
        )

    def g_place():
        at.placed, placed_far = place_columns(
            line, here, [(at.kept, i) for i in range(3)], micros * frames, spots, True
        )
        at.placed_got = devices.swap(placed_far, 0, REST_KIND)

    def l_place():
        placed = place_columns(
            line, here, [at.l_normed, at.l_mixture, at.l_normed_two], books * frames, local_spots
        )
        at.l_placed_got = devices.cores(placed)
        at.l_lefts = [(placed, 1), (at.l_placed_got, 5)]

    def l_mlp_back():
        at.l_low, dz_own, dz_other, at.l_dm, at.l_do, at.l_gain_two = mlp_backward(
            line,
            here,
            (upstream, same, zero, books * frames),
            (at.l_slope, 0, zero),
            (at.l_middle[None], 0, zero),
            w_out_l,
            gains_l[1],
            w_up_l,
            w_down_l,
        )
        at.l_dz = both(dz_own, dz_other)

    def l_attn_back():
        grads = (at.l_do, at.l_low)
        at.l_dp = local_attn(line, here, at.l_packed, books, grads)
        at.l_rights = both(*at.l_dp)

    def l_qkv_back():
        at.local_grad, at.frame_grad, at.l_gain_one = qkv_backward(
            line, here, *at.l_dp, (at.l_rows, zero), at.l_dm, gains_l[0], w_qkv_l, books
        )
        at.g_frame = all_rows(at.frame_grad, at.frame_grad, DOWN_KIND)

    def l_output():
        at.local_out = halves(at.l_out.reshape(books, frames, features))
        line.wait(at.local_out)

    def g_mlp_back():
        at.g_low, dz_own, dz_other, at.g_dm, at.g_do, at.g_gain_two = mlp_backward(
            line,
            here,
            (at.frame_grad, zero, zero, frames),
            (at.active, 1, same),
            (at.kept, 6, same),
            w_out_g,
            gains_g[1],
            w_up_g,
            w_down_g,
        )
        at.g_dz = all_rows(dz_own, dz_other, REST_KIND)

    def g_attn_back():
        grads = (at.g_do, at.g_low)
        at.g_dp = global_attn_backward(line, here, at.kept, 3, item_lengths, grads)
        at.g_rights = all_rows(*at.g_dp, REST_KIND)

    def g_qkv_back():
        at.global_grad, _, at.g_gain_one = qkv_backward(
            line, here, *at.g_dp, (at.rows, same), at.g_dm, gains_g[0], w_qkv_g, 1
        )

    def g_gains():
        gains = [at.g_gain_one, at.g_gain_two, at.l_gain_one, at.l_gain_two]
        gains = jnp.concatenate(gains)
        at.gains = gains + devices.swap(gains, 0, REST_KIND)
        line.wait(at.gains)

    def g_output():
        at.embed_grad = halves(
            at.local_grad.reshape(books, frames, features) + (at.global_grad * scale_in)[None]
        )
        line.wait(at.embed_grad)

    def down_out():
        (at.down,) = both_halves(line, here, devices, at.g_down, at.l_down, (1,))

    def up_out():
        (at.up,) = both_halves(line, here, devices, at.g_up, at.l_up, (1,))

    def rest_out():
        at.qkv, at.out = both_halves(line, here, devices, at.g_rest, at.l_rest, (3, 1))

    def make(name):
        if not hasattr(at, name):
            if name == "l_up":
                one = Sum(devices, line, up_group(at.l_lefts, at.l_dz), kind=LOCAL_REST_KIND)
            elif name == "l_rest":
                one = Sum(devices, line, rest_group(at.l_lefts, at.l_rights), kind=LOCAL_REST_KIND)
            elif name == "g_down":
                lefts = [(at.active_units, 1), (at.active_got, 1 + units)]
                rights = [(a, count, lambda j, t, i=i: (0, i, t[0])) for a, count, i in at.g_frame]
                one = Sum(devices, line, down_group(down_table, lefts, rights), 1, DOWN_KIND)
            else:
                lefts = [(at.placed, 1), (at.placed_got, 1)]
                if name == "g_up":
                    one = Sum(devices, line, up_group(lefts, at.g_dz), 1, REST_KIND)
                    one.rider = at.gains
                else:
                    one = Sum(devices, line, rest_group(lefts, at.g_rights), 1, REST_KIND)
            setattr(at, name, one)
        return getattr(at, name)

    steps = (g_qkv, g_attn, g_mlp, g_pack, l_qkv, l_attn, l_mlp, g_units, g_place, l_place)
    steps += (l_mlp_back, l_attn_back, l_qkv_back, l_output)
    steps += (g_mlp_back, g_attn_back, g_qkv_back, g_gains, g_output)
    steps += (down_out, up_out, rest_out)
    steps = {step.__name__: step for step in steps}
    for words in PLAN:
        name, *rest = words.split()
        if name in steps:
            steps[name]()
        elif name == "wait":
            one = getattr(at, rest[0])
            one = getattr(one, rest[1]) if rest[1:] not in ([], ["far"]) else one
            line.wait(one[2 if "far" in rest else 1][0] if isinstance(one, list) else one)
        else:
            getattr(make(name), rest[0])()
    gain_sums = at.g_up.rider
    gain_sums = gain_sums + devices.cores(gain_sums)
    gain_sums = jnp.where(first_core, gain_sums[:2], gain_sums[2:]).reshape(2, size, -1)
    gain_sums = lax.dynamic_index_in_dim(gain_sums, devices.index, 1, keepdims=False)

    return (
        at.local_out,
        at.embed_grad,
        gain_sums[:1],
        at.qkv,
        at.out,
        gain_sums[1:],
        at.up,
        at.down,
    )


def solution(mesh):
    in_specs = (
        P(None, "dp", None, None),
        P(None, "dp", None),
        P("section", None),
        P("section", None, None),
        P("section", None, None),
        P("section", None),
        P("section", None, None),
        P("section", None, None),
        P(None, "dp", None, None),
    )
    out_specs = (
        P(None, "dp", None, "section"),
        P(None, "dp", None, "section"),
        P("section", "dp"),
        P("section", "dp", None),
        P("section", "dp", None),
        P("section", "dp"),
        P("section", "dp", None),
        P("section", "dp", None),
    )
    return jax.shard_map(local, mesh=mesh, in_specs=in_specs, out_specs=out_specs, check_vma=False)
```

```python
import functools
import types

import jax
import jax.numpy as jnp
from jax import lax
from jax.experimental import pallas as pl
from jax.experimental.pallas import tpu as pltpu
from jax.sharding import PartitionSpec as P

HEADS = 16
EPSILON = 1e-05
BF16 = jnp.bfloat16
F32 = jnp.float32
VMEM_LIMIT = 48 * 1024 * 1024
CHUNK = 128
COST = 1.0
COST_SUMS = 1.0
LINE, NEAR, FAR = range(3)
DOWN_KIND = FAR
REST_KIND = NEAR
LOCAL_DOWN_KIND = LINE
LOCAL_REST_KIND = LINE
RIDER = 16
UNIT = 256


def dot(left, right):
    return jnp.dot(left, right, preferred_element_type=F32)


def dot_t(left, right):
    return lax.dot_general(left, right, (((1,), (1,)), ((), ())), preferred_element_type=F32)


def t_dot(left, right):
    return lax.dot_general(left, right, (((0,), (0,)), ((), ())), preferred_element_type=F32)


def add_all(terms):
    return functools.reduce(lambda s, t: s + t, terms)


def sds(shape, dtype=BF16):
    return jax.ShapeDtypeStruct(shape, dtype)


class Weight:
    def __init__(self, given, block, index, tiles):
        self.arrays = list(given) if isinstance(given, tuple) else [given]
        self.block, self.index, self.tiles = block, index, tiles
        self.slots = min(tiles, 2)


class Tiles:
    def __init__(self, weight, core, refs, held, sems):
        self.weight, self.core, self.refs, self.held, self.sems = weight, core, refs, held, sems

    def copy(self, place, j):
        block = self.weight.block
        at = zip(self.weight.index(j, self.core), block)
        at = tuple(pl.ds(pl.multiple_of(i * b, b), b) for i, b in at)
        slot = j % self.weight.slots
        return pltpu.make_async_copy(self.refs[place].at[at], self.held.at[slot], self.sems.at[slot])

    def start(self, j):
        for place in range(len(self.refs)):
            if len(self.refs) == 1:
                self.copy(place, j).start()
            else:

                @pl.when(self.core == place)
                def _():
                    self.copy(place, j).start()

    def get(self, j):
        self.copy(0, j).wait()
        return self.held[j % self.weight.slots]

    def ahead(self, j):
        @pl.when(j == 0)
        def _():
            self.start(0)

        if self.weight.tiles > 1:

            @pl.when(j + 1 < self.weight.tiles)
            def _():
                self.start(j + 1)


class Line:
    def __init__(self):
        self.behind = []

    def wait(self, *arrays):
        self.behind.extend(arrays)

    def launch(self, kernel, name, scalars, grid, ins, outs, scratch=(), flops=0):
        arrays, specs, counts, held = [], [], [], []
        for operand in ins:
            if isinstance(operand, Weight):
                specs.extend([pl.BlockSpec(memory_space=pl.ANY)] * len(operand.arrays))
                arrays.extend(operand.arrays)
                counts.append(operand)
                held.append(pltpu.VMEM((operand.slots,) + operand.block, operand.arrays[0].dtype))
                held.append(pltpu.SemaphoreType.DMA((operand.slots,)))
                continue
            given, block, index = operand
            if isinstance(given, tuple):
                for place in range(2):

                    def at(*args, place=place, index=index):
                        here = args[len(grid)][0] == place
                        return tuple(jnp.where(here, i, 0) for i in index(*args))

                    specs.append(pl.BlockSpec(block, at))
                arrays.extend(given)
                counts.append(2)
            else:
                specs.append(pl.BlockSpec(block, index))
                arrays.append(given)
                counts.append(1)
        skipped = len(self.behind)
        arrays.extend(self.behind)
        specs.extend([pl.BlockSpec(memory_space=pl.ANY)] * skipped)

        def body(*refs):
            scalar_refs, refs = refs[: len(scalars)], refs[len(scalars) :]
            groups, own = [], refs[len(refs) - len(held) :]
            for count in counts:
                if isinstance(count, Weight):
                    weight, count = count, len(count.arrays)
                    core = scalar_refs[0][0]
                    groups.append(Tiles(weight, core, list(refs[:count]), *own[:2]))
                    own = own[2:]
                else:
                    groups.append(list(refs[:count]))
                refs = refs[count:]
            refs = refs[skipped : len(refs) - len(held)]
            kernel(scalar_refs, groups, refs[: len(outs)], refs[len(outs) :])

        share = COST_SUMS if name == "weight_grad" else COST
        out = pl.pallas_call(
            body,
            grid_spec=pltpu.PrefetchScalarGridSpec(
                num_scalar_prefetch=len(scalars),
                grid=grid,
                in_specs=specs,
                out_specs=[pl.BlockSpec(block, index) for _, block, index in outs],
                scratch_shapes=list(scratch) + held,
            ),
            out_shape=[shape for shape, _, _ in outs],
            compiler_params=pltpu.CompilerParams(vmem_limit_bytes=VMEM_LIMIT),
            cost_estimate=pl.CostEstimate(
                flops=int(flops * share),
                bytes_accessed=int(share * sum(a.size * a.dtype.itemsize for a in arrays[: len(specs) - skipped])),
                transcendentals=0,
            ),
            name=name,
        )(*scalars, *arrays)
        self.behind = [out[0]]
        return out


def read(core, refs):
    if len(refs) == 1:
        return refs[0][...]
    return jnp.where(core == 0, refs[0][...], refs[1][...])


def origin(rank):
    return lambda *_: (0,) * rank


def whole(array):
    return array, array.shape, origin(array.ndim)


def full(shape, dtype=BF16):
    return sds(shape, dtype), shape, origin(len(shape))


def rstd(rows):
    return lax.rsqrt(jnp.mean(rows * rows, axis=-1, keepdims=True) + EPSILON)


def by_chunks(rows, step):
    def one(i, carry):
        step(pl.ds(pl.multiple_of(i * CHUNK, CHUNK), CHUNK))
        return carry

    lax.fori_loop(0, rows // CHUNK, one, 0)


def norm_backward(grad, rows, gain):
    scale = rstd(rows)
    plain = rows * scale
    grad_gain = jnp.sum(grad * plain, axis=0, keepdims=True)
    lead = grad * gain
    return scale * (lead - plain * jnp.mean(lead * plain, axis=-1, keepdims=True)), grad_gain


def gelu_parts(hidden):
    c = 0.7978845608028654
    square = hidden * hidden
    t = jnp.tanh(hidden * (c + (c * 0.044715) * square))
    half = 0.5 + 0.5 * t
    slope = half + (hidden * half) * ((1.0 - t) * (c + (3 * 0.044715 * c) * square))
    return (hidden * half).astype(BF16), slope.astype(BF16)


def qkv_forward(line, here, parts, make_rows, gain, w_qkv, tile=1024):
    features = gain[0].shape[1] if isinstance(gain, tuple) else gain.shape[1]
    count, wide = parts[0], 3 * features

    def kernel(scalars, ins, outs, _):
        core = scalars[0][0]
        gain_refs, w = ins[-2:]
        x_ref, h_ref, p_ref = outs
        j = pl.program_id(0)
        w.ahead(j)

        @pl.when(j == 0)
        def _():
            gain = read(core, gain_refs)
            for i, x in enumerate(make_rows(core, ins[:-2])):
                at = slice(i * CHUNK, (i + 1) * CHUNK)
                x_ref[at, :] = x
                h_ref[at, :] = (x * rstd(x) * gain).astype(BF16)

        p_ref[...] = dot(h_ref[...], w.get(j)).astype(BF16)

    return line.launch(
        kernel,
        "qkv_forward",
        [here],
        (wide // tile,),
        parts[1]
        + [
            (gain, (1, features), origin(2)),
            Weight(w_qkv, (features, tile), lambda j, core: (0, j), wide // tile),
        ],
        [
            full((count, features), F32),
            full((count, features)),
            (sds((count, wide)), (count, tile), lambda j, s: (0, j)),
        ],
        flops=2 * count * features * wide,
    )


def mlp_forward(line, here, rows, mixture, w_out, gain, w_up, w_down, joined, tile=1024):
    count, features = rows.shape
    wide = (w_up[0] if isinstance(w_up, tuple) else w_up).shape[1]

    def kernel(scalars, ins, outs, scratch):
        core = scalars[0][0]
        (x_ref,), (o_ref,), w_out, gain_refs, w_up, w_down = ins
        y_ref, m_ref, h_ref = outs[:3]
        (acc_ref,) = scratch
        j = pl.program_id(0)
        for w in (w_out, w_up, w_down):
            w.ahead(j)

        @pl.when(j == 0)
        def _():
            gain, wide_out = read(core, gain_refs), w_out.get(0)

            def step(at):
                m = x_ref[at, :] + dot(o_ref[at, :], wide_out)
                m_ref[at, :] = m
                acc_ref[at, :] = m
                h_ref[at, :] = (m * rstd(m) * gain).astype(BF16)

            by_chunks(count, step)

        g, slope = gelu_parts(dot(h_ref[...], w_up.get(j)))
        if joined:
            outs[3][0] = g
            outs[3][1] = slope
        else:
            outs[3][0] = g
            outs[4][0] = slope
        acc_ref[...] += dot(g, w_down.get(j))

        @pl.when(pl.program_id(0) == pl.num_programs(0) - 1)
        def _():
            y_ref[...] = acc_ref[...].astype(BF16)

    planes = 2 if joined else 1
    wide_out = (sds((planes, count, wide)), (planes, count, tile), lambda j, s: (0, 0, j))
    return line.launch(
        kernel,
        "mlp_forward",
        [here],
        (wide // tile,),
        [
            whole(rows),
            whole(mixture),
            Weight(w_out, (features, features), lambda j, core: (0, 0), 1),
            (gain, (1, features), origin(2)),
            Weight(w_up, (features, tile), lambda j, core: (0, j), wide // tile),
            Weight(w_down, (tile, features), lambda j, core: (j, 0), wide // tile),
        ],
        [full(rows.shape), full(rows.shape, F32), full(rows.shape)] + [wide_out] * (3 - planes),
        [pltpu.VMEM(rows.shape, F32)],
        flops=2 * count * features * (features + 2 * wide),
    )


def mlp_backward(line, here, low_out, slope, middle, w_out, gain, w_up, w_down, tile=1024):
    wide, features = w_down[0].shape
    count = low_out[3]
    tiles = wide // tile
    half = tiles // 2

    def kernel(scalars, ins, outs, scratch):
        core = scalars[0][0]
        (dy_ref,), s_refs, m_refs, gain_refs, w_down, w_up, w_out = ins
        low_ref, own_ref, other_ref, dm_ref, do_ref, gg_ref = outs
        (acc_ref,) = scratch
        j = pl.program_id(0)
        for w in (w_down, w_up, w_out):
            w.ahead(j)
        slope = read(core, s_refs)[0].astype(F32)
        dz = (slope * dot_t(dy_ref[0], w_down.get(j))).astype(BF16)

        @pl.when(j < half)
        def _():
            other_ref[0] = dz

        @pl.when(j >= half)
        def _():
            own_ref[0] = dz

        term = dot_t(dz, w_up.get(j))

        @pl.when(j == 0)
        def _():
            acc_ref[...] = term

        @pl.when(j > 0)
        def _():
            acc_ref[...] += term

        @pl.when(j == tiles - 1)
        def _():
            gg_ref[...] = jnp.zeros_like(gg_ref)
            gain, wide_out = read(core, gain_refs), w_out.get(0)

            def step(at):
                if len(m_refs) == 1:
                    m = m_refs[0][0, at, :].astype(F32)
                else:
                    m = jnp.where(core == 0, m_refs[0][0, at, :], m_refs[1][0, at, :]).astype(F32)
                dm, gg = norm_backward(acc_ref[at, :], m, gain)
                gg_ref[...] += gg
                dm = dm + dy_ref[0, at, :].astype(F32)
                dm_ref[at, :] = dm
                low = dm.astype(BF16)
                low_ref[at, :] = low
                do_ref[at, :] = dot_t(low, wide_out).astype(BF16)

            by_chunks(count, step)

    def at(j, core):
        return (j + (1 - core) * half) % tiles

    shape = (count, features)
    return line.launch(
        kernel,
        "mlp_backward",
        [here],
        (tiles,),
        [
            (low_out[0], (1,) + shape, lambda j, s: (low_out[1](s[0]), low_out[2](s[0]), 0)),
            (slope[0], (1, count, tile), lambda j, s: (slope[1], slope[2](s[0]), at(j, s[0]))),
            (middle[0], (1,) + shape, lambda j, s: (middle[1], middle[2](s[0]), 0)),
            (gain, (1, features), origin(2)),
            Weight(w_down, (tile, features), lambda j, core: (at(j, core), 0), tiles),
            Weight(w_up, (features, tile), lambda j, core: (0, at(j, core)), tiles),
            Weight(w_out, (features, features), lambda j, core: (0, 0), 1),
        ],
        [
            full(shape),
            (
                sds((1, count, wide // 2)),
                (1, count, tile),
                lambda j, s: (0, 0, jnp.maximum(j - half, 0)),
            ),
            (
                sds((1, count, wide // 2)),
                (1, count, tile),
                lambda j, s: (0, 0, jnp.minimum(j, half - 1)),
            ),
            full(shape, F32),
            full(shape),
            full((1, features), F32),
        ],
        [pltpu.VMEM(shape, F32)],
        flops=2 * count * features * (features + 2 * wide),
    )


def qkv_backward(line, here, own, other, rows, grad_middle, gain, w_qkv, books, tile=512):
    count, features = grad_middle.shape
    frames = count // books

    def kernel(scalars, ins, outs, scratch):
        core = scalars[0][0]
        (own_ref,), (other_ref,), (x_ref,), (dm_ref,), gain_refs, w_tiles = ins
        dx_ref, sum_ref, gg_ref = outs
        (acc_ref,) = scratch
        j = pl.program_id(0)
        w_tiles.ahead(j)
        w = w_tiles.get(j)
        terms = []
        for i in range(3):
            part = jnp.where(core == i // 2, own_ref[i % 2], other_ref[i % 2])
            terms.append(dot_t(part, w[:, i * features : (i + 1) * features]))
        acc_ref[:, pl.ds(pl.multiple_of(j * tile, tile), tile)] = add_all(terms)

        @pl.when(j == pl.num_programs(0) - 1)
        def _():
            gg_ref[...] = jnp.zeros_like(gg_ref)
            gain = read(core, gain_refs)
            total = 0.0
            for b in range(books):
                at = slice(b * frames, (b + 1) * frames)
                dx, gg = norm_backward(acc_ref[at, :], x_ref[at, :], gain)
                gg_ref[...] += gg
                dx = dx + dm_ref[at, :]
                dx_ref[at, :] = dx
                total = total + dx
            sum_ref[0] = total.astype(BF16)

    shape = (count, features)
    return line.launch(
        kernel,
        "qkv_backward",
        [here],
        (features // tile,),
        [
            whole(own),
            whole(other),
            (rows[0], shape, lambda j, s: (rows[1](s[0]), 0)),
            whole(grad_middle),
            (gain, (1, features), origin(2)),
            Weight(w_qkv, (tile, 3 * features), lambda j, core: (j, 0), features // tile),
        ],
        [full(shape, F32), full((1, frames, features)), full((1, features), F32)],
        [pltpu.VMEM(shape, F32)],
        flops=6 * count * features * features,
    )


def head_sum(product, reduce_mat):
    high = product.astype(BF16)
    low = (product - high.astype(F32)).astype(BF16)
    return dot(high, reduce_mat) + dot(low, reduce_mat)


def head_mats(lanes, width):
    row = lax.broadcasted_iota(jnp.int32, (lanes, 128), 0)
    col = lax.broadcasted_iota(jnp.int32, (lanes, 128), 1)
    reduce_mat = (row // width == col).astype(BF16)
    row = lax.broadcasted_iota(jnp.int32, (128, lanes), 0)
    col = lax.broadcasted_iota(jnp.int32, (128, lanes), 1)
    return reduce_mat, (col // width == row).astype(BF16)


def local_probs(q, k, reduce_mat, scale):
    probs = {}
    for a in range(len(q)):
        scores = [head_sum(q[a] * k[b], reduce_mat) * scale for b in range(a + 1)]
        peak = functools.reduce(jnp.maximum, scores)
        parts = [jnp.exp(s - peak) for s in scores]
        total = add_all(parts)
        for b in range(a + 1):
            probs[a, b] = parts[b] / total
    return probs


def local_attn_fwd_kernel(width, q_ref, k_ref, v_ref, o_ref):
    books, _, lanes = q_ref.shape
    reduce_mat, expand_mat = head_mats(lanes, width)
    q = [q_ref[a].astype(F32) for a in range(books)]
    k = [k_ref[a].astype(F32) for a in range(books)]
    v = [v_ref[a].astype(F32) for a in range(books)]
    probs = local_probs(q, k, reduce_mat, width**-0.5)
    for a in range(books):
        mixed = [dot(probs[a, b].astype(BF16), expand_mat) * v[b] for b in range(a + 1)]
        o_ref[a] = add_all(mixed).astype(BF16)


def by_half(core, parts, own_ref, other_ref):
    for c in range(2):

        @pl.when(core == c)
        def _():
            for i in range(2):
                own_ref[i] = parts[2 * c + i]
                other_ref[i] = parts[2 - 2 * c + i]


def local_attn_bwd_kernel(
    width, core, q_ref, k_ref, v_ref, g_ref, m_ref, own_ref, other_ref
):
    books, _, lanes = q_ref.shape
    scale = width**-0.5
    reduce_mat, expand_mat = head_mats(lanes, width)
    q = [q_ref[a].astype(F32) for a in range(books)]
    k = [k_ref[a].astype(F32) for a in range(books)]
    v = [v_ref[a].astype(F32) for a in range(books)]
    g = [g_ref[a].astype(F32) for a in range(books)]
    probs = local_probs(q, k, reduce_mat, scale)
    dq = [0.0] * books
    dk = [0.0] * books
    dv = [0.0] * books
    for a in range(books):
        dprobs = [head_sum(g[a] * v[b], reduce_mat) for b in range(a + 1)]
        inner = add_all([dprobs[b] * probs[a, b] for b in range(a + 1)])
        for b in range(a + 1):
            dscore = dot((probs[a, b] * (dprobs[b] - inner)).astype(BF16), expand_mat)
            dq[a] = dq[a] + dscore * k[b]
            dk[b] = dk[b] + dscore * q[a]
            dv[b] = dv[b] + dot(probs[a, b].astype(BF16), expand_mat) * g[a]
    parts = [
        jnp.stack([(one * by).astype(BF16) for one in ones])
        for ones, by in ((dq, scale), (dk, scale), (dv, 1.0))
    ]
    by_half(core, parts + [m_ref[...]], own_ref, other_ref)


def local_attn(line, here, packed, books, grads=None, lanes=512):
    count, wide = packed.shape
    features, frames = wide // 3, count // books
    width, groups = features // HEADS, features // lanes
    packed = packed.reshape(books, frames, wide)
    shape, block = (books, frames, features), (books, frames, lanes)

    def at(part):
        return lambda h, *_: (0, 0, part * groups + h)

    ins = [(packed, block, at(i)) for i in range(3)]
    if grads is None:

        def forward(scalars, ins, outs, _):
            local_attn_fwd_kernel(width, *[i[0] for i in ins], *outs)

        out = line.launch(
            forward,
            "local_attn_forward",
            [here],
            (groups,),
            ins,
            [(sds(shape), block, at(0))],
            flops=4000 * count * features,
        )
        return out[0].reshape(count, features)

    def backward(scalars, ins, outs, _):
        local_attn_bwd_kernel(width, scalars[0][0], *[i[0] for i in ins], *outs)

    ins += [(g.reshape(shape), block, at(0)) for g in grads]
    half = (sds((2,) + shape), (2,) + block, lambda h, *_: (0, 0, 0, h))
    out = line.launch(
        backward,
        "local_attn_backward",
        [here],
        (groups,),
        ins,
        [half] * 2,
        flops=10000 * count * features,
    )
    return [one.reshape(2, count, features) for one in out]


def item_mask(lengths_ref, micro, frames, items):
    row = lax.broadcasted_iota(jnp.int32, (frames, frames), 0)
    col = lax.broadcasted_iota(jnp.int32, (frames, frames), 1)
    row_item = jnp.zeros((frames, frames), jnp.int32)
    col_item = jnp.zeros((frames, frames), jnp.int32)
    end = 0
    for i in range(items):
        end = end + lengths_ref[micro, 0, i]
        row_item = row_item + (row >= end).astype(jnp.int32)
        col_item = col_item + (col >= end).astype(jnp.int32)
    return (row_item == col_item) & (row >= col)


def head_parts(block, width):
    per = 128 // width
    lane = lax.broadcasted_iota(jnp.int32, (block.shape[0], 128), 1)
    parts = []
    for h in range(block.shape[1] // width):
        tile = block[:, (h // per) * 128 : (h // per + 1) * 128]
        parts.append(jnp.where(lane // width == h % per, tile, jnp.zeros_like(tile)))
    return parts


def frame_probs(q, k, mask, scale):
    scores = jnp.where(mask, dot_t(q, k) * scale, -1e30)
    parts = jnp.exp(scores - jnp.max(scores, axis=-1, keepdims=True))
    return parts / jnp.sum(parts, axis=-1, keepdims=True)


def global_attn_fwd_kernel(width, items, lengths_ref, q_ref, k_ref, v_ref, o_ref):
    frames, lanes = q_ref.shape
    mask = item_mask(lengths_ref, pl.program_id(0), frames, items)
    per = 128 // width
    q = head_parts(q_ref[...], width)
    v = head_parts(v_ref[...], width)
    mixed = [0.0] * (lanes // 128)
    for h in range(lanes // width):
        tile = slice((h // per) * 128, (h // per + 1) * 128)
        probs = frame_probs(q[h], k_ref[:, tile], mask, width**-0.5)
        mixed[h // per] = mixed[h // per] + dot(probs.astype(BF16), v[h])
    for i, tile in enumerate(mixed):
        o_ref[:, i * 128 : (i + 1) * 128] = tile.astype(BF16)


def global_attn_bwd_kernel(
    width, items, core, lengths_ref, q, k, v, g_ref, m_ref, own_ref, other_ref
):
    frames, lanes = q.shape
    scale = width**-0.5
    mask = item_mask(lengths_ref, core, frames, items)
    per = 128 // width
    q = head_parts(q, width)
    wide_k, k = k, head_parts(k, width)
    g = head_parts(g_ref[...], width)
    tiles = lanes // 128
    dq, dk, dv = [0.0] * tiles, [0.0] * tiles, [0.0] * tiles
    for h in range(lanes // width):
        t = h // per
        tile = slice(t * 128, (t + 1) * 128)
        probs = frame_probs(q[h], wide_k[:, tile], mask, scale)
        dv[t] = dv[t] + t_dot(probs.astype(BF16), g[h])
        dprobs = dot_t(g[h], v[:, tile])
        inner = jnp.sum(dprobs * probs, axis=-1, keepdims=True)
        dscore = (probs * (dprobs - inner)).astype(BF16)
        dq[t] = dq[t] + dot(dscore, k[h])
        dk[t] = dk[t] + t_dot(dscore, q[h])
    parts = [
        jnp.concatenate([(one * by).astype(BF16) for one in ones], axis=1)
        for ones, by in ((dq, scale), (dk, scale), (dv, 1.0))
    ]
    by_half(core, parts + [m_ref[...]], own_ref, other_ref)


def global_attn_forward(line, packed, lengths, lanes=1024):
    micros, _, items = lengths.shape
    count, wide = packed.shape
    features, frames = wide // 3, count // micros
    width, groups = features // HEADS, features // lanes
    block = (frames, lanes)

    def at(part):
        return lambda m, h, _: (m, part * groups + h)

    def kernel(scalars, ins, outs, _):
        global_attn_fwd_kernel(width, items, scalars[0], *[i[0] for i in ins], *outs)

    return line.launch(
        kernel,
        "global_attn_forward",
        [lengths],
        (micros, groups),
        [(packed, block, at(i)) for i in range(3)],
        [(sds((count, features)), block, at(0))],
        flops=10000 * count * features,
    )[0]


def global_attn_backward(line, here, kept, first, lengths, grads, lanes=1024):
    micros, _, items = lengths.shape
    _, count, features = kept[0].shape
    frames = count // micros
    width, groups = features // HEADS, features // lanes
    block = (frames, lanes)

    def kernel(scalars, ins, outs, _):
        core = scalars[0][0]
        q, k, v = [read(core, i)[0] for i in ins[:3]]
        global_attn_bwd_kernel(
            width, items, core, scalars[1], q, k, v, ins[3][0], ins[4][0], *outs
        )

    half = (sds((2, frames, features)), (2,) + block, lambda h, *_: (0, 0, h))
    return line.launch(
        kernel,
        "global_attn_backward",
        [here, lengths],
        (groups,),
        [(kept, (1,) + block, lambda h, c, _, i=i: (first + i, c[0], h)) for i in range(3)]
        + [(g, block, lambda h, *_: (0, h)) for g in grads],
        [half] * 2,
        flops=30000 * frames * features,
    )


def place_columns(line, here, sources, rows, spots, cut=False):
    features = spots.shape[0]

    def kernel(scalars, ins, outs, _):
        for i, refs in enumerate(ins[1:]):
            block = read(scalars[0][0], refs).reshape(rows, features)
            placed = dot(block, ins[0][0][...]).astype(BF16)
            wide = features // len(outs)
            for k, out in enumerate(outs):
                out[i] = placed[:, k * wide : (k + 1) * wide]

    ins = [whole(spots)]
    for source in sources:
        if isinstance(source, tuple):
            ins.append((source[0], (1, rows, features), lambda _, s, plane=source[1]: (plane, 0, 0)))
        else:
            ins.append(whole(source))
    parts = 2 if cut else 1
    out = line.launch(
        kernel,
        "place_columns",
        [here],
        (1,),
        ins,
        [full((len(sources), rows, features // parts))] * parts,
        flops=2 * len(sources) * rows * features * features,
    )
    return out if cut else out[0]


def place_units(line, table, source, rows, units):
    per = 4

    def kernel(scalars, ins, outs, _):
        for i in range(per):
            outs[0][0, :, i * UNIT : (i + 1) * UNIT] = read(scalars[0][0], ins[i])[0]

    first, count = units

    def at(i):
        return lambda u, t: (0, 0, t[1 + first + u * per + i])

    return line.launch(
        kernel,
        "place_units",
        [table],
        (count // per,),
        [(source, (1, rows, UNIT), at(i)) for i in range(per)],
        [(sds((1, rows, count * UNIT)), (1, rows, per * UNIT), lambda u, t: (0, 0, u))],
    )[0]


def pack(line, here, arrays, features):
    count = arrays[0].shape[0]
    planes = [(i, c) for i, a in enumerate(arrays) for c in range(a.shape[1] // features)]

    def kernel(scalars, ins, outs, _):
        for plane, (i, c) in enumerate(planes):
            outs[0][plane] = ins[i][0][:, c * features : (c + 1) * features].astype(BF16)

    return line.launch(
        kernel,
        "pack",
        [here],
        (1,),
        [whole(a) for a in arrays],
        [full((len(planes), count, features))],
    )[0]


class Group:
    def __init__(self, table, units, lefts, rights, tile, tiles, plane):
        self.table, self.per = table, units // 4
        self.lefts, self.rights = lefts, rights
        self.tile, self.tiles, self.plane = tile, tiles, plane


def joined(core, blocks, ordered):
    if ordered:
        pairs = []
        for a, b in zip(blocks[::2], blocks[1::2]):
            pairs += [jnp.where(core == 0, a, b), jnp.where(core == 0, b, a)]
        blocks = pairs
    return blocks[0] if len(blocks) == 1 else jnp.concatenate(blocks, axis=0)


def weight_grad(line, group, first, steps, per, addends, split):
    lefts, rights, tile = group.lefts, group.rights, group.tile

    def kernel(scalars, ins, outs, _):
        core = scalars[0][0]
        left_refs = [ins[i * per : (i + 1) * per] for i in range(len(lefts))]
        ins = ins[len(lefts) * per :]
        right = joined(
            core, [r[0][0] for r in ins[: len(rights)]], len(rights) > len(lefts)
        )
        add_refs = [r[0] for r in ins[len(rights) :]]
        for i in range(per):
            at = slice(i * UNIT, (i + 1) * UNIT)
            left = joined(
                core, [read(core, r[i])[0] for r in left_refs], len(lefts) > len(rights)
            )
            out = add_all([t_dot(left, right)] + [r[at, :].astype(F32) for r in add_refs])
            out = out.astype(BF16)
            if not split:
                outs[0][at, :] = out
            elif per == 1:
                outs[0][...] = out[: UNIT // 2]
                outs[1][...] = out[UNIT // 2 :]
            else:
                half = per // 2
                outs[i // half][(i % half) * UNIT : (i % half + 1) * UNIT, :] = out

    def left_in(given, start, i):
        rows = (given[0] if isinstance(given, tuple) else given).shape[1]
        return (
            given,
            (1, rows, UNIT),
            lambda u, j, t: (group.plane(j, t), 0, t[start + first + u * per + i]),
        )

    def right_in(given, count, at):
        return given, (1, count, tile), lambda u, j, t: at(j, t)

    def block(skip, rows=per * UNIT):
        return (rows, tile), lambda u, j, t: (skip + u, j)

    wide = group.tiles * tile
    rows = sum(count for _, count, _ in rights)
    if split:
        outs = [(sds((per * UNIT // 2, wide)),) + block(0, per * UNIT // 2)] * 2
    else:
        outs = [(sds((steps * per * UNIT, wide)),) + block(0)]
    out = line.launch(
        kernel,
        "weight_grad",
        [group.table],
        (steps, group.tiles),
        [left_in(a, start, i) for a, start in lefts for i in range(per)]
        + [right_in(*right) for right in rights]
        + [(a,) + block(skip) for a, skip in addends],
        outs,
        flops=2 * steps * per * UNIT * wide * rows,
    )
    return out if split else out[0]


class Devices:
    def __init__(self, size):
        self.size = size
        self.core = lax.axis_index("section")
        self.index = lax.axis_index("dp")

    def bits(self, core, kind):
        near = [1, 2] if core == 0 else [2, 1]
        far = [1 << b for b in range(2, self.size.bit_length() - 1)]
        return far[:1] + near + far[1:] if kind == FAR else near + far

    def swap(self, array, step, kind):
        pairs = []
        for core in range(2):
            by = self.bits(core, kind)[step]
            pairs += [(core * self.size + i, core * self.size + (i ^ by)) for i in range(self.size)]
        return lax.ppermute(array, ("section", "dp"), pairs)

    def cores(self, array):
        return lax.ppermute(array, "section", [(0, 1), (1, 0)])

    def order(self, kind):
        orders = []
        for core in range(2):
            bits = self.bits(core, kind)
            if kind == LINE:
                bits = bits[:2] + bits[:1:-1]
            order = [
                sum(bit for i, bit in enumerate(bits) if (spot >> (len(bits) - 1 - i)) & 1)
                for spot in range(self.size)
            ]
            orders.append(jnp.array(order, jnp.int32))
        return jnp.where(self.core == 0, orders[0], orders[1]) ^ (
            self.index % 4 if kind == LINE else self.index
        )

    def columns(self, count, kind):
        block = count // self.size
        order = self.order(kind)
        return (order[:, None] * block + jnp.arange(block, dtype=jnp.int32)).reshape(-1)

    def spots(self, count, kind):
        at = self.columns(count, kind)[None, :]
        return (lax.broadcasted_iota(jnp.int32, (count, count), 0) == at).astype(BF16)

    def along_z(self, array):
        depth = self.size // 4
        groups = [[4 * z + place for z in range(depth)] for place in range(4)]
        return lax.psum_scatter(
            array, "dp", scatter_dimension=0, axis_index_groups=groups, tiled=True
        )

    def table(self, *orders):
        parts = [self.core[None].astype(jnp.int32)] + [jnp.asarray(o, jnp.int32) for o in orders]
        return jnp.concatenate(parts)


class Sum:
    def __init__(self, devices, line, group, step=0, kind=LINE):
        self.devices, self.line, self.group, self.step = devices, line, group, step
        self.one, self.kind = None, kind
        self.rider = None

    def grad(self, first, count, addends, split=False):
        group = self.group
        steps, per = (count, group.per) if group.per > 1 else (1, count)
        return weight_grad(self.line, group, first * group.per, steps, per, addends, split)

    def send(self, array):
        rows, columns = array.shape
        if self.rider is not None:
            shape, size = self.rider.shape, self.rider.size
            high = self.rider.astype(BF16)
            low = (self.rider - high.astype(F32)).astype(BF16)
            extra = jnp.concatenate([high, low]).reshape(-1, columns)
            extra = jnp.pad(extra, ((0, -extra.shape[0] % RIDER), (0, 0)))
            array = jnp.concatenate([array, extra])
        got = self.devices.swap(array, self.step, self.kind)
        if self.rider is not None:
            extra = got[rows:].astype(F32).reshape(-1)
            self.rider = self.rider + (extra[:size] + extra[size : 2 * size]).reshape(shape)
        self.step += 1
        return got

    def first(self):
        self.one = self.send(self.grad(2, 2, []))

    def second(self):
        self.two = self.send(self.grad(1, 1, [] if self.one is None else [(self.one, 1)]))

    def third(self):
        addends = [(one, 0) for one in (self.one, self.two) if one is not None]
        if self.kind == LINE:
            self.kept = self.devices.along_z(self.grad(0, 1, addends))
            return
        self.kept, sent = self.grad(0, 1, addends, split=True)
        self.got = self.send(sent)

    def rest(self):
        if self.kind == LINE:
            return
        steps = self.devices.size.bit_length() - 1
        total = self.kept
        while self.step < steps:
            got = self.got
            half = total.shape[0] // 2
            sent = (total[half:].astype(F32) + got[half : 2 * half].astype(F32)).astype(BF16)
            total = total[:half].astype(F32) + got[:half].astype(F32)
            if self.step < steps - 1:
                total = total.astype(BF16)
            self.line.wait(sent)
            self.got = self.send(sent)
        self.kept = total

    def last(self):
        return self.kept.astype(F32) + self.got[: self.kept.shape[0]].astype(F32)


PLAN = (
    "g_qkv",
    "g_attn",
    "g_mlp",
    "g_pack",
    "l_qkv",
    "l_attn",
    "l_mlp",
    "l_place",
    "l_down first",
    "l_mlp_back",
    "l_attn_back",
    "l_down second",
    "g_units",
    "g_place",
    "l_up first",
    "l_down third",
    "l_rest first",
    "l_down rest",
    "l_qkv_back",
    "wait l_down one",
    "l_output",
    "wait active_got",
    "g_mlp_back",
    "g_attn_back",
    "g_qkv_back",
    "wait placed_got",
    "g_gains",
    "l_rest second",
    "g_up second",
    "l_up second",
    "g_rest second",
    "l_up third",
    "g_output",
    "l_up rest",
    "g_up third",
    "g_down second",
    "l_rest third",
    "wait l_down kept",
    "g_rest third",
    "l_rest rest",
    "g_down third",
    "g_down rest",
    "g_rest rest",
    "g_up rest",
    "up_out",
    "rest_out",
    "wait g_dz far",
    "down_out",
)


def both_halves(line, here, devices, ours, theirs, parts):
    rows, wide = ours.kept.shape
    half = jax.ShapeDtypeStruct((rows, wide), BF16)
    operands = [[one.kept] if one.kind == LINE else [one.kept, one.got] for one in (ours, theirs)]
    count = len(operands[0])

    def split(scalars, ins, outs, _):
        core = scalars[0][0]
        terms = [i[0][:rows, :].astype(F32) for i in ins]
        mine, other = add_all(terms[:count]), add_all(terms[count:])
        outs[0][...] = jnp.where(core == 0, other, mine).astype(BF16)
        outs[1][...] = jnp.where(core == 0, mine, other)

    sent, mine = line.launch(
        split,
        "split_halves",
        [here],
        (1,),
        [whole(one) for one in operands[0] + operands[1]],
        [full(half.shape), full(half.shape, F32)],
    )
    got = devices.cores(sent)

    def join(scalars, ins, outs, _):
        core = scalars[0][0]
        mine, got = ins[0][0][...], ins[1][0][...].astype(F32)
        joined = jnp.concatenate(
            [jnp.where(core == 0, mine, got), jnp.where(core == 0, got, mine)], axis=1
        )
        start = 0
        for out in outs:
            out[0] = joined[:, start : start + out.shape[2]]
            start += out.shape[2]

    return line.launch(
        join,
        "join_halves",
        [here],
        (1,),
        [whole(mine), whole(got)],
        [full((1, rows, 2 * wide * part // sum(parts)), F32) for part in parts],
    )


def local(codebook_embed, item_lengths, gain_attn, w_qkv, w_out, gain_mlp, w_up, w_down, cotangent):
    size = lax.axis_size("dp")
    micros, frames, books, features = codebook_embed.shape
    half_width = features // 2
    scale_in = books**-0.5
    devices, line = Devices(size), Line()
    core = devices.core
    first_core = core == 0
    here = core[None].astype(jnp.int32)

    def zero(core):
        return 0

    def same(core):
        return core

    gains = jnp.stack([gain_attn[0], gain_mlp[0]])
    own = [w_qkv[0], w_out[0], w_up[0], w_down[0]]
    gains_other = devices.cores(gains)
    other = [devices.cores(w) for w in own]
    w_qkv_g, w_out_g, w_up_g, w_down_g = zip(own, other)
    w_qkv_l, w_out_l, w_up_l, w_down_l = zip(other, own)
    gains_g = [(gains[i : i + 1], gains_other[i : i + 1]) for i in range(2)]
    gains_l = [(b, a) for a, b in gains_g]

    embed = codebook_embed.transpose(0, 2, 1, 3)
    upstream = cotangent.transpose(0, 2, 1, 3).reshape(micros, -1, features)

    def with_first(array):
        return array, devices.cores(array)

    columns = w_down.shape[1]
    unit_rows = columns // size == UNIT
    units = columns // UNIT
    near, far = range(units // 2), range(units // 2, units)
    placed_table = devices.table([0, 1, 2, 3], [0, 2, 1, 3])
    down_order = devices.order(DOWN_KIND) if unit_rows else range(units)
    down_table = devices.table(down_order, range(units))
    local_table = devices.table(devices.order(LOCAL_DOWN_KIND) if unit_rows else range(units))
    spots = devices.spots(features, REST_KIND)
    local_spots = devices.spots(features, LOCAL_REST_KIND)

    def by_units(array, kind):
        if unit_rows:
            return array
        if isinstance(array, tuple):
            return tuple(by_units(a, kind) for a in array)
        return jnp.take(array[:1], devices.columns(columns, kind), axis=2)

    def down_group(table, lefts, rights):
        return Group(table, units, lefts, rights, half_width, 1, lambda j, t: 0)

    def up_group(lefts, rights):
        return Group(
            placed_table,
            4,
            lefts,
            [(a, count, lambda j, t, i=i: (0, i, j)) for a, count, i in rights],
            features,
            2,
            lambda j, t: 2,
        )

    def rest_group(lefts, rights):
        return Group(
            placed_table,
            4,
            lefts,
            [(a, count, lambda j, t, i=i: (j, i, 0)) for a, count, i in rights],
            features,
            2,
            lambda j, t: jnp.where(2 * t[0] + j == 3, 1, 0),
        )

    def my_half(array):
        return jnp.where(first_core, array[..., :half_width], array[..., half_width:])

    def other_half(array):
        return jnp.where(first_core, array[..., half_width:], array[..., :half_width])

    def halves(array):
        got = devices.cores(other_half(array).astype(BF16)).astype(array.dtype)
        mine = my_half(array)
        return jnp.where(first_core, jnp.stack([mine, got]), jnp.stack([got, mine]))

    def both(mine, others):
        return [(mine, mine.shape[1], 0), (devices.cores(others), mine.shape[1], 0)]

    def all_rows(mine, others, kind):
        rights = both(mine, others)
        far = devices.swap(jnp.concatenate([rights[0][0], rights[1][0]], axis=1), 0, kind)
        return rights + [(far, frames, i) for i in range(micros)]

    at = types.SimpleNamespace()

    def g_qkv():
        def frame_rows(core, ins):
            (e_ref,) = ins[0]
            return [
                add_all([e_ref[m, b].astype(F32) for b in range(books)]) * scale_in
                for m in range(micros)
            ]

        at.rows, at.normed, at.packed = qkv_forward(
            line, here, (micros * frames, [whole(embed)]), frame_rows, gains[:1], own[0]
        )

    def g_attn():
        at.mixture = global_attn_forward(line, at.packed, item_lengths)

    def g_mlp():
        result, at.middle, at.normed_two, active = mlp_forward(
            line, here, at.rows, at.mixture, own[1], gains[1:], own[2], own[3], True
        )
        at.states, at.active = with_first(result), with_first(active)
        at.active_units = by_units(at.active, DOWN_KIND)

    def g_pack():
        arrays = [at.normed, at.mixture, at.normed_two, at.packed, at.middle]
        at.kept = with_first(pack(line, here, arrays, features))

    def l_qkv():
        def local_rows(core, ins):
            (e_ref,), s_refs = ins
            state = read(core, s_refs).astype(F32)
            return [e_ref[0, b].astype(F32) + state for b in range(books)]

        parts = [
            (embed, (1, books, frames, features), lambda j, s: (s[0], 0, 0, 0)),
            (at.states, (frames, features), lambda j, s: (s[0], 0)),
        ]
        at.l_rows, at.l_normed, at.l_packed = qkv_forward(
            line, here, (books * frames, parts), local_rows, gains_l[0], w_qkv_l
        )

    def l_attn():
        at.l_mixture = local_attn(line, here, at.l_packed, books)

    def l_mlp():
        at.l_out, at.l_middle, at.l_normed_two, at.l_active, at.l_slope = mlp_forward(
            line, here, at.l_rows, at.l_mixture, w_out_l, gains_l[1], w_up_l, w_down_l, False
        )
        at.l_active_got = devices.cores(at.l_active)
        at.l_down = Sum(
            devices,
            line,
            down_group(
                local_table,
                [
                    (by_units(at.l_active, LOCAL_DOWN_KIND), 1),
                    (by_units(at.l_active_got, LOCAL_DOWN_KIND), 1),
                ],
                [
                    (upstream, books * frames, lambda j, t: (t[0], 0, t[0])),
                    (upstream, books * frames, lambda j, t: (1 - t[0], 0, t[0])),
                ],
            ),
            kind=LOCAL_DOWN_KIND,
        )

    def g_units():
        at.active_got = devices.swap(
            place_units(line, down_table, at.active_units, micros * frames, (far.start, len(far))),
            0,
            DOWN_KIND,
        )

    def g_place():
        at.placed, placed_far = place_columns(
            line, here, [(at.kept, i) for i in range(3)], micros * frames, spots, True
        )
        at.placed_got = devices.swap(placed_far, 0, REST_KIND)

    def l_place():
        placed = place_columns(
            line, here, [at.l_normed, at.l_mixture, at.l_normed_two], books * frames, local_spots
        )
        at.l_placed_got = devices.cores(placed)
        at.l_lefts = [(placed, 1), (at.l_placed_got, 5)]

    def l_mlp_back():
        at.l_low, dz_own, dz_other, at.l_dm, at.l_do, at.l_gain_two = mlp_backward(
            line,
            here,
            (upstream, same, zero, books * frames),
            (at.l_slope, 0, zero),
            (at.l_middle[None], 0, zero),
            w_out_l,
            gains_l[1],
            w_up_l,
            w_down_l,
        )
        at.l_dz = both(dz_own, dz_other)

    def l_attn_back():
        grads = (at.l_do, at.l_low)
        at.l_dp = local_attn(line, here, at.l_packed, books, grads)
        at.l_rights = both(*at.l_dp)

    def l_qkv_back():
        at.local_grad, at.frame_grad, at.l_gain_one = qkv_backward(
            line, here, *at.l_dp, (at.l_rows, zero), at.l_dm, gains_l[0], w_qkv_l, books
        )
        at.g_frame = all_rows(at.frame_grad, at.frame_grad, DOWN_KIND)

    def l_output():
        at.local_out = halves(at.l_out.reshape(books, frames, features))
        line.wait(at.local_out)

    def g_mlp_back():
        at.g_low, dz_own, dz_other, at.g_dm, at.g_do, at.g_gain_two = mlp_backward(
            line,
            here,
            (at.frame_grad, zero, zero, frames),
            (at.active, 1, same),
            (at.kept, 6, same),
            w_out_g,
            gains_g[1],
            w_up_g,
            w_down_g,
        )
        at.g_dz = all_rows(dz_own, dz_other, REST_KIND)

    def g_attn_back():
        grads = (at.g_do, at.g_low)
        at.g_dp = global_attn_backward(line, here, at.kept, 3, item_lengths, grads)
        at.g_rights = all_rows(*at.g_dp, REST_KIND)

    def g_qkv_back():
        at.global_grad, _, at.g_gain_one = qkv_backward(
            line, here, *at.g_dp, (at.rows, same), at.g_dm, gains_g[0], w_qkv_g, 1
        )

    def g_gains():
        gains = [at.g_gain_one, at.g_gain_two, at.l_gain_one, at.l_gain_two]
        gains = jnp.concatenate(gains)
        at.gains = gains + devices.swap(gains, 0, REST_KIND)
        line.wait(at.gains)

    def g_output():
        at.embed_grad = halves(
            at.local_grad.reshape(books, frames, features) + (at.global_grad * scale_in)[None]
        )
        line.wait(at.embed_grad)

    def down_out():
        (at.down,) = both_halves(line, here, devices, at.g_down, at.l_down, (1,))

    def up_out():
        (at.up,) = both_halves(line, here, devices, at.g_up, at.l_up, (1,))

    def rest_out():
        at.qkv, at.out = both_halves(line, here, devices, at.g_rest, at.l_rest, (3, 1))

    def make(name):
        if not hasattr(at, name):
            if name == "l_up":
                one = Sum(devices, line, up_group(at.l_lefts, at.l_dz), kind=LOCAL_REST_KIND)
            elif name == "l_rest":
                one = Sum(devices, line, rest_group(at.l_lefts, at.l_rights), kind=LOCAL_REST_KIND)
            elif name == "g_down":
                lefts = [(at.active_units, 1), (at.active_got, 1 + units)]
                rights = [(a, count, lambda j, t, i=i: (0, i, t[0])) for a, count, i in at.g_frame]
                one = Sum(devices, line, down_group(down_table, lefts, rights), 1, DOWN_KIND)
            else:
                lefts = [(at.placed, 1), (at.placed_got, 1)]
                if name == "g_up":
                    one = Sum(devices, line, up_group(lefts, at.g_dz), 1, REST_KIND)
                    one.rider = at.gains
                else:
                    one = Sum(devices, line, rest_group(lefts, at.g_rights), 1, REST_KIND)
            setattr(at, name, one)
        return getattr(at, name)

    steps = (g_qkv, g_attn, g_mlp, g_pack, l_qkv, l_attn, l_mlp, g_units, g_place, l_place)
    steps += (l_mlp_back, l_attn_back, l_qkv_back, l_output)
    steps += (g_mlp_back, g_attn_back, g_qkv_back, g_gains, g_output)
    steps += (down_out, up_out, rest_out)
    steps = {step.__name__: step for step in steps}
    for words in PLAN:
        name, *rest = words.split()
        if name in steps:
            steps[name]()
        elif name == "wait":
            one = getattr(at, rest[0])
            one = getattr(one, rest[1]) if rest[1:] not in ([], ["far"]) else one
            line.wait(one[2 if "far" in rest else 1][0] if isinstance(one, list) else one)
        else:
            getattr(make(name), rest[0])()
    gain_sums = at.g_up.rider
    gain_sums = gain_sums + devices.cores(gain_sums)
    gain_sums = jnp.where(first_core, gain_sums[:2], gain_sums[2:]).reshape(2, size, -1)
    gain_sums = lax.dynamic_index_in_dim(gain_sums, devices.index, 1, keepdims=False)

    return (
        at.local_out.transpose(0, 2, 1, 3),
        at.embed_grad.transpose(0, 2, 1, 3),
        gain_sums[:1],
        at.qkv,
        at.out,
        gain_sums[1:],
        at.up,
        at.down,
    )


def solution(mesh):
    in_specs = (
        P(None, "dp", None, None),
        P(None, "dp", None),
        P("section", None),
        P("section", None, None),
        P("section", None, None),
        P("section", None),
        P("section", None, None),
        P("section", None, None),
        P(None, "dp", None, None),
    )
    out_specs = (
        P(None, "dp", None, "section"),
        P(None, "dp", None, "section"),
        P("section", "dp"),
        P("section", "dp", None),
        P("section", "dp", None),
        P("section", "dp"),
        P("section", "dp", None),
        P("section", "dp", None),
    )
    return jax.shard_map(local, mesh=mesh, in_specs=in_specs, out_specs=out_specs, check_vma=False)
```

```python
import functools
import types

import jax
import jax.numpy as jnp
from jax import lax
from jax.experimental import pallas as pl
from jax.experimental.pallas import tpu as pltpu
from jax.sharding import PartitionSpec as P

HEADS = 16
EPSILON = 1e-05
BF16 = jnp.bfloat16
F32 = jnp.float32
VMEM_LIMIT = 48 * 1024 * 1024
CHUNK = 128
COST = 1.0
COST_SUMS = 1.0
LINE, NEAR, FAR = range(3)
DOWN_KIND = FAR
REST_KIND = FAR
LOCAL_DOWN_KIND = LINE
LOCAL_REST_KIND = LINE
RIDER = 16
UNIT = 256


def dot(left, right):
    return jnp.dot(left, right, preferred_element_type=F32)


def dot_t(left, right):
    return lax.dot_general(left, right, (((1,), (1,)), ((), ())), preferred_element_type=F32)


def t_dot(left, right):
    return lax.dot_general(left, right, (((0,), (0,)), ((), ())), preferred_element_type=F32)


def add_all(terms):
    return functools.reduce(lambda s, t: s + t, terms)


def sds(shape, dtype=BF16):
    return jax.ShapeDtypeStruct(shape, dtype)


class Weight:
    def __init__(self, given, block, index, tiles):
        self.arrays = list(given) if isinstance(given, tuple) else [given]
        self.block, self.index, self.tiles = block, index, tiles
        self.slots = min(tiles, 2)


class Tiles:
    def __init__(self, weight, core, refs, held, sems):
        self.weight, self.core, self.refs, self.held, self.sems = weight, core, refs, held, sems

    def copy(self, place, j):
        block = self.weight.block
        at = zip(self.weight.index(j, self.core), block)
        at = tuple(pl.ds(pl.multiple_of(i * b, b), b) for i, b in at)
        slot = j % self.weight.slots
        return pltpu.make_async_copy(self.refs[place].at[at], self.held.at[slot], self.sems.at[slot])

    def start(self, j):
        for place in range(len(self.refs)):
            if len(self.refs) == 1:
                self.copy(place, j).start()
            else:

                @pl.when(self.core == place)
                def _():
                    self.copy(place, j).start()

    def get(self, j):
        self.copy(0, j).wait()
        return self.held[j % self.weight.slots]

    def ahead(self, j):
        @pl.when(j == 0)
        def _():
            self.start(0)

        if self.weight.tiles > 1:

            @pl.when(j + 1 < self.weight.tiles)
            def _():
                self.start(j + 1)


class Line:
    def __init__(self):
        self.behind = []

    def wait(self, *arrays):
        self.behind.extend(arrays)

    def launch(self, kernel, name, scalars, grid, ins, outs, scratch=(), flops=0):
        arrays, specs, counts, held = [], [], [], []
        for operand in ins:
            if isinstance(operand, Weight):
                specs.extend([pl.BlockSpec(memory_space=pl.ANY)] * len(operand.arrays))
                arrays.extend(operand.arrays)
                counts.append(operand)
                held.append(pltpu.VMEM((operand.slots,) + operand.block, operand.arrays[0].dtype))
                held.append(pltpu.SemaphoreType.DMA((operand.slots,)))
                continue
            given, block, index = operand
            if isinstance(given, tuple):
                for place in range(2):

                    def at(*args, place=place, index=index):
                        here = args[len(grid)][0] == place
                        return tuple(jnp.where(here, i, 0) for i in index(*args))

                    specs.append(pl.BlockSpec(block, at))
                arrays.extend(given)
                counts.append(2)
            else:
                specs.append(pl.BlockSpec(block, index))
                arrays.append(given)
                counts.append(1)
        skipped = len(self.behind)
        arrays.extend(self.behind)
        specs.extend([pl.BlockSpec(memory_space=pl.ANY)] * skipped)

        def body(*refs):
            scalar_refs, refs = refs[: len(scalars)], refs[len(scalars) :]
            groups, own = [], refs[len(refs) - len(held) :]
            for count in counts:
                if isinstance(count, Weight):
                    weight, count = count, len(count.arrays)
                    core = scalar_refs[0][0]
                    groups.append(Tiles(weight, core, list(refs[:count]), *own[:2]))
                    own = own[2:]
                else:
                    groups.append(list(refs[:count]))
                refs = refs[count:]
            refs = refs[skipped : len(refs) - len(held)]
            kernel(scalar_refs, groups, refs[: len(outs)], refs[len(outs) :])

        share = COST_SUMS if name == "weight_grad" else COST
        out = pl.pallas_call(
            body,
            grid_spec=pltpu.PrefetchScalarGridSpec(
                num_scalar_prefetch=len(scalars),
                grid=grid,
                in_specs=specs,
                out_specs=[pl.BlockSpec(block, index) for _, block, index in outs],
                scratch_shapes=list(scratch) + held,
            ),
            out_shape=[shape for shape, _, _ in outs],
            compiler_params=pltpu.CompilerParams(vmem_limit_bytes=VMEM_LIMIT),
            cost_estimate=pl.CostEstimate(
                flops=int(flops * share),
                bytes_accessed=int(share * sum(a.size * a.dtype.itemsize for a in arrays[: len(specs) - skipped])),
                transcendentals=0,
            ),
            name=name,
        )(*scalars, *arrays)
        self.behind = [out[0]]
        return out


def read(core, refs):
    if len(refs) == 1:
        return refs[0][...]
    return jnp.where(core == 0, refs[0][...], refs[1][...])


def origin(rank):
    return lambda *_: (0,) * rank


def whole(array):
    return array, array.shape, origin(array.ndim)


def full(shape, dtype=BF16):
    return sds(shape, dtype), shape, origin(len(shape))


def rstd(rows):
    return lax.rsqrt(jnp.mean(rows * rows, axis=-1, keepdims=True) + EPSILON)


def by_chunks(rows, step):
    def one(i, carry):
        step(pl.ds(pl.multiple_of(i * CHUNK, CHUNK), CHUNK))
        return carry

    lax.fori_loop(0, rows // CHUNK, one, 0)


def norm_backward(grad, rows, gain):
    scale = rstd(rows)
    plain = rows * scale
    grad_gain = jnp.sum(grad * plain, axis=0, keepdims=True)
    lead = grad * gain
    return scale * (lead - plain * jnp.mean(lead * plain, axis=-1, keepdims=True)), grad_gain


def gelu_parts(hidden):
    c = 0.7978845608028654
    square = hidden * hidden
    t = jnp.tanh(hidden * (c + (c * 0.044715) * square))
    half = 0.5 + 0.5 * t
    slope = half + (hidden * half) * ((1.0 - t) * (c + (3 * 0.044715 * c) * square))
    return (hidden * half).astype(BF16), slope.astype(BF16)


def qkv_forward(line, here, parts, make_rows, gain, w_qkv, tile=1024):
    features = gain[0].shape[1] if isinstance(gain, tuple) else gain.shape[1]
    count, wide = parts[0], 3 * features

    def kernel(scalars, ins, outs, _):
        core = scalars[0][0]
        gain_refs, w = ins[-2:]
        x_ref, h_ref, p_ref = outs
        j = pl.program_id(0)
        w.ahead(j)

        @pl.when(j == 0)
        def _():
            gain = read(core, gain_refs)
            for i, x in enumerate(make_rows(core, ins[:-2])):
                at = slice(i * CHUNK, (i + 1) * CHUNK)
                x_ref[at, :] = x
                h_ref[at, :] = (x * rstd(x) * gain).astype(BF16)

        p_ref[...] = dot(h_ref[...], w.get(j)).astype(BF16)

    return line.launch(
        kernel,
        "qkv_forward",
        [here],
        (wide // tile,),
        parts[1]
        + [
            (gain, (1, features), origin(2)),
            Weight(w_qkv, (features, tile), lambda j, core: (0, j), wide // tile),
        ],
        [
            full((count, features), F32),
            full((count, features)),
            (sds((count, wide)), (count, tile), lambda j, s: (0, j)),
        ],
        flops=2 * count * features * wide,
    )


def mlp_forward(line, here, rows, mixture, w_out, gain, w_up, w_down, joined, tile=1024):
    count, features = rows.shape
    wide = (w_up[0] if isinstance(w_up, tuple) else w_up).shape[1]

    def kernel(scalars, ins, outs, scratch):
        core = scalars[0][0]
        (x_ref,), (o_ref,), w_out, gain_refs, w_up, w_down = ins
        y_ref, m_ref, h_ref = outs[:3]
        (acc_ref,) = scratch
        j = pl.program_id(0)
        for w in (w_out, w_up, w_down):
            w.ahead(j)

        @pl.when(j == 0)
        def _():
            gain, wide_out = read(core, gain_refs), w_out.get(0)

            def step(at):
                m = x_ref[at, :] + dot(o_ref[at, :], wide_out)
                m_ref[at, :] = m
                acc_ref[at, :] = m
                h_ref[at, :] = (m * rstd(m) * gain).astype(BF16)

            by_chunks(count, step)

        g, slope = gelu_parts(dot(h_ref[...], w_up.get(j)))
        if joined:
            outs[3][0] = g
            outs[3][1] = slope
        else:
            outs[3][0] = g
            outs[4][0] = slope
        acc_ref[...] += dot(g, w_down.get(j))

        @pl.when(pl.program_id(0) == pl.num_programs(0) - 1)
        def _():
            y_ref[...] = acc_ref[...].astype(BF16)

    planes = 2 if joined else 1
    wide_out = (sds((planes, count, wide)), (planes, count, tile), lambda j, s: (0, 0, j))
    return line.launch(
        kernel,
        "mlp_forward",
        [here],
        (wide // tile,),
        [
            whole(rows),
            whole(mixture),
            Weight(w_out, (features, features), lambda j, core: (0, 0), 1),
            (gain, (1, features), origin(2)),
            Weight(w_up, (features, tile), lambda j, core: (0, j), wide // tile),
            Weight(w_down, (tile, features), lambda j, core: (j, 0), wide // tile),
        ],
        [full(rows.shape), full(rows.shape, F32), full(rows.shape)] + [wide_out] * (3 - planes),
        [pltpu.VMEM(rows.shape, F32)],
        flops=2 * count * features * (features + 2 * wide),
    )


def mlp_backward(line, here, low_out, slope, middle, w_out, gain, w_up, w_down, tile=1024):
    wide, features = w_down[0].shape
    count = low_out[3]
    tiles = wide // tile
    half = tiles // 2

    def kernel(scalars, ins, outs, scratch):
        core = scalars[0][0]
        (dy_ref,), s_refs, m_refs, gain_refs, w_down, w_up, w_out = ins
        low_ref, own_ref, other_ref, dm_ref, do_ref, gg_ref = outs
        (acc_ref,) = scratch
        j = pl.program_id(0)
        for w in (w_down, w_up, w_out):
            w.ahead(j)
        slope = read(core, s_refs)[0].astype(F32)
        dz = (slope * dot_t(dy_ref[0], w_down.get(j))).astype(BF16)

        @pl.when(j < half)
        def _():
            other_ref[0] = dz

        @pl.when(j >= half)
        def _():
            own_ref[0] = dz

        term = dot_t(dz, w_up.get(j))

        @pl.when(j == 0)
        def _():
            acc_ref[...] = term

        @pl.when(j > 0)
        def _():
            acc_ref[...] += term

        @pl.when(j == tiles - 1)
        def _():
            gg_ref[...] = jnp.zeros_like(gg_ref)
            gain, wide_out = read(core, gain_refs), w_out.get(0)

            def step(at):
                if len(m_refs) == 1:
                    m = m_refs[0][0, at, :].astype(F32)
                else:
                    m = jnp.where(core == 0, m_refs[0][0, at, :], m_refs[1][0, at, :]).astype(F32)
                dm, gg = norm_backward(acc_ref[at, :], m, gain)
                gg_ref[...] += gg
                dm = dm + dy_ref[0, at, :].astype(F32)
                dm_ref[at, :] = dm
                low = dm.astype(BF16)
                low_ref[at, :] = low
                do_ref[at, :] = dot_t(low, wide_out).astype(BF16)

            by_chunks(count, step)

    def at(j, core):
        return (j + (1 - core) * half) % tiles

    shape = (count, features)
    return line.launch(
        kernel,
        "mlp_backward",
        [here],
        (tiles,),
        [
            (low_out[0], (1,) + shape, lambda j, s: (low_out[1](s[0]), low_out[2](s[0]), 0)),
            (slope[0], (1, count, tile), lambda j, s: (slope[1], slope[2](s[0]), at(j, s[0]))),
            (middle[0], (1,) + shape, lambda j, s: (middle[1], middle[2](s[0]), 0)),
            (gain, (1, features), origin(2)),
            Weight(w_down, (tile, features), lambda j, core: (at(j, core), 0), tiles),
            Weight(w_up, (features, tile), lambda j, core: (0, at(j, core)), tiles),
            Weight(w_out, (features, features), lambda j, core: (0, 0), 1),
        ],
        [
            full(shape),
            (
                sds((1, count, wide // 2)),
                (1, count, tile),
                lambda j, s: (0, 0, jnp.maximum(j - half, 0)),
            ),
            (
                sds((1, count, wide // 2)),
                (1, count, tile),
                lambda j, s: (0, 0, jnp.minimum(j, half - 1)),
            ),
            full(shape, F32),
            full(shape),
            full((1, features), F32),
        ],
        [pltpu.VMEM(shape, F32)],
        flops=2 * count * features * (features + 2 * wide),
    )


def qkv_backward(line, here, own, other, rows, grad_middle, gain, w_qkv, books, tile=512):
    count, features = grad_middle.shape
    frames = count // books

    def kernel(scalars, ins, outs, scratch):
        core = scalars[0][0]
        (own_ref,), (other_ref,), (x_ref,), (dm_ref,), gain_refs, w_tiles = ins
        dx_ref, sum_ref, gg_ref = outs
        (acc_ref,) = scratch
        j = pl.program_id(0)
        w_tiles.ahead(j)
        w = w_tiles.get(j)
        terms = []
        for i in range(3):
            part = jnp.where(core == i // 2, own_ref[i % 2], other_ref[i % 2])
            terms.append(dot_t(part, w[:, i * features : (i + 1) * features]))
        acc_ref[:, pl.ds(pl.multiple_of(j * tile, tile), tile)] = add_all(terms)

        @pl.when(j == pl.num_programs(0) - 1)
        def _():
            gg_ref[...] = jnp.zeros_like(gg_ref)
            gain = read(core, gain_refs)
            total = 0.0
            for b in range(books):
                at = slice(b * frames, (b + 1) * frames)
                dx, gg = norm_backward(acc_ref[at, :], x_ref[at, :], gain)
                gg_ref[...] += gg
                dx = dx + dm_ref[at, :]
                dx_ref[at, :] = dx
                total = total + dx
            sum_ref[0] = total.astype(BF16)

    shape = (count, features)
    return line.launch(
        kernel,
        "qkv_backward",
        [here],
        (features // tile,),
        [
            whole(own),
            whole(other),
            (rows[0], shape, lambda j, s: (rows[1](s[0]), 0)),
            whole(grad_middle),
            (gain, (1, features), origin(2)),
            Weight(w_qkv, (tile, 3 * features), lambda j, core: (j, 0), features // tile),
        ],
        [full(shape, F32), full((1, frames, features)), full((1, features), F32)],
        [pltpu.VMEM(shape, F32)],
        flops=6 * count * features * features,
    )


def head_sum(product, reduce_mat):
    high = product.astype(BF16)
    low = (product - high.astype(F32)).astype(BF16)
    return dot(high, reduce_mat) + dot(low, reduce_mat)


def head_mats(lanes, width):
    row = lax.broadcasted_iota(jnp.int32, (lanes, 128), 0)
    col = lax.broadcasted_iota(jnp.int32, (lanes, 128), 1)
    reduce_mat = (row // width == col).astype(BF16)
    row = lax.broadcasted_iota(jnp.int32, (128, lanes), 0)
    col = lax.broadcasted_iota(jnp.int32, (128, lanes), 1)
    return reduce_mat, (col // width == row).astype(BF16)


def local_probs(q, k, reduce_mat, scale):
    probs = {}
    for a in range(len(q)):
        scores = [head_sum(q[a] * k[b], reduce_mat) * scale for b in range(a + 1)]
        peak = functools.reduce(jnp.maximum, scores)
        parts = [jnp.exp(s - peak) for s in scores]
        total = add_all(parts)
        for b in range(a + 1):
            probs[a, b] = parts[b] / total
    return probs


def local_attn_fwd_kernel(width, q_ref, k_ref, v_ref, o_ref):
    books, _, lanes = q_ref.shape
    reduce_mat, expand_mat = head_mats(lanes, width)
    q = [q_ref[a].astype(F32) for a in range(books)]
    k = [k_ref[a].astype(F32) for a in range(books)]
    v = [v_ref[a].astype(F32) for a in range(books)]
    probs = local_probs(q, k, reduce_mat, width**-0.5)
    for a in range(books):
        mixed = [dot(probs[a, b].astype(BF16), expand_mat) * v[b] for b in range(a + 1)]
        o_ref[a] = add_all(mixed).astype(BF16)


def by_half(core, parts, own_ref, other_ref):
    for c in range(2):

        @pl.when(core == c)
        def _():
            for i in range(2):
                own_ref[i] = parts[2 * c + i]
                other_ref[i] = parts[2 - 2 * c + i]


def local_attn_bwd_kernel(
    width, core, q_ref, k_ref, v_ref, g_ref, m_ref, own_ref, other_ref
):
    books, _, lanes = q_ref.shape
    scale = width**-0.5
    reduce_mat, expand_mat = head_mats(lanes, width)
    q = [q_ref[a].astype(F32) for a in range(books)]
    k = [k_ref[a].astype(F32) for a in range(books)]
    v = [v_ref[a].astype(F32) for a in range(books)]
    g = [g_ref[a].astype(F32) for a in range(books)]
    probs = local_probs(q, k, reduce_mat, scale)
    dq = [0.0] * books
    dk = [0.0] * books
    dv = [0.0] * books
    for a in range(books):
        dprobs = [head_sum(g[a] * v[b], reduce_mat) for b in range(a + 1)]
        inner = add_all([dprobs[b] * probs[a, b] for b in range(a + 1)])
        for b in range(a + 1):
            dscore = dot((probs[a, b] * (dprobs[b] - inner)).astype(BF16), expand_mat)
            dq[a] = dq[a] + dscore * k[b]
            dk[b] = dk[b] + dscore * q[a]
            dv[b] = dv[b] + dot(probs[a, b].astype(BF16), expand_mat) * g[a]
    parts = [
        jnp.stack([(one * by).astype(BF16) for one in ones])
        for ones, by in ((dq, scale), (dk, scale), (dv, 1.0))
    ]
    by_half(core, parts + [m_ref[...]], own_ref, other_ref)


def local_attn(line, here, packed, books, grads=None, lanes=512):
    count, wide = packed.shape
    features, frames = wide // 3, count // books
    width, groups = features // HEADS, features // lanes
    packed = packed.reshape(books, frames, wide)
    shape, block = (books, frames, features), (books, frames, lanes)

    def at(part):
        return lambda h, *_: (0, 0, part * groups + h)

    ins = [(packed, block, at(i)) for i in range(3)]
    if grads is None:

        def forward(scalars, ins, outs, _):
            local_attn_fwd_kernel(width, *[i[0] for i in ins], *outs)

        out = line.launch(
            forward,
            "local_attn_forward",
            [here],
            (groups,),
            ins,
            [(sds(shape), block, at(0))],
            flops=4000 * count * features,
        )
        return out[0].reshape(count, features)

    def backward(scalars, ins, outs, _):
        local_attn_bwd_kernel(width, scalars[0][0], *[i[0] for i in ins], *outs)

    ins += [(g.reshape(shape), block, at(0)) for g in grads]
    half = (sds((2,) + shape), (2,) + block, lambda h, *_: (0, 0, 0, h))
    out = line.launch(
        backward,
        "local_attn_backward",
        [here],
        (groups,),
        ins,
        [half] * 2,
        flops=10000 * count * features,
    )
    return [one.reshape(2, count, features) for one in out]


def item_mask(lengths_ref, micro, frames, items):
    row = lax.broadcasted_iota(jnp.int32, (frames, frames), 0)
    col = lax.broadcasted_iota(jnp.int32, (frames, frames), 1)
    row_item = jnp.zeros((frames, frames), jnp.int32)
    col_item = jnp.zeros((frames, frames), jnp.int32)
    end = 0
    for i in range(items):
        end = end + lengths_ref[micro, 0, i]
        row_item = row_item + (row >= end).astype(jnp.int32)
        col_item = col_item + (col >= end).astype(jnp.int32)
    return (row_item == col_item) & (row >= col)


def head_parts(block, width):
    per = 128 // width
    lane = lax.broadcasted_iota(jnp.int32, (block.shape[0], 128), 1)
    parts = []
    for h in range(block.shape[1] // width):
        tile = block[:, (h // per) * 128 : (h // per + 1) * 128]
        parts.append(jnp.where(lane // width == h % per, tile, jnp.zeros_like(tile)))
    return parts


def frame_probs(q, k, mask, scale):
    scores = jnp.where(mask, dot_t(q, k) * scale, -1e30)
    parts = jnp.exp(scores - jnp.max(scores, axis=-1, keepdims=True))
    return parts / jnp.sum(parts, axis=-1, keepdims=True)


def global_attn_fwd_kernel(width, items, lengths_ref, q_ref, k_ref, v_ref, o_ref):
    frames, lanes = q_ref.shape
    mask = item_mask(lengths_ref, pl.program_id(0), frames, items)
    per = 128 // width
    q = head_parts(q_ref[...], width)
    v = head_parts(v_ref[...], width)
    mixed = [0.0] * (lanes // 128)
    for h in range(lanes // width):
        tile = slice((h // per) * 128, (h // per + 1) * 128)
        probs = frame_probs(q[h], k_ref[:, tile], mask, width**-0.5)
        mixed[h // per] = mixed[h // per] + dot(probs.astype(BF16), v[h])
    for i, tile in enumerate(mixed):
        o_ref[:, i * 128 : (i + 1) * 128] = tile.astype(BF16)


def global_attn_bwd_kernel(
    width, items, core, lengths_ref, q, k, v, g_ref, m_ref, own_ref, other_ref
):
    frames, lanes = q.shape
    scale = width**-0.5
    mask = item_mask(lengths_ref, core, frames, items)
    per = 128 // width
    q = head_parts(q, width)
    wide_k, k = k, head_parts(k, width)
    g = head_parts(g_ref[...], width)
    tiles = lanes // 128
    dq, dk, dv = [0.0] * tiles, [0.0] * tiles, [0.0] * tiles
    for h in range(lanes // width):
        t = h // per
        tile = slice(t * 128, (t + 1) * 128)
        probs = frame_probs(q[h], wide_k[:, tile], mask, scale)
        dv[t] = dv[t] + t_dot(probs.astype(BF16), g[h])
        dprobs = dot_t(g[h], v[:, tile])
        inner = jnp.sum(dprobs * probs, axis=-1, keepdims=True)
        dscore = (probs * (dprobs - inner)).astype(BF16)
        dq[t] = dq[t] + dot(dscore, k[h])
        dk[t] = dk[t] + t_dot(dscore, q[h])
    parts = [
        jnp.concatenate([(one * by).astype(BF16) for one in ones], axis=1)
        for ones, by in ((dq, scale), (dk, scale), (dv, 1.0))
    ]
    by_half(core, parts + [m_ref[...]], own_ref, other_ref)


def global_attn_forward(line, packed, lengths, lanes=1024):
    micros, _, items = lengths.shape
    count, wide = packed.shape
    features, frames = wide // 3, count // micros
    width, groups = features // HEADS, features // lanes
    block = (frames, lanes)

    def at(part):
        return lambda m, h, _: (m, part * groups + h)

    def kernel(scalars, ins, outs, _):
        global_attn_fwd_kernel(width, items, scalars[0], *[i[0] for i in ins], *outs)

    return line.launch(
        kernel,
        "global_attn_forward",
        [lengths],
        (micros, groups),
        [(packed, block, at(i)) for i in range(3)],
        [(sds((count, features)), block, at(0))],
        flops=10000 * count * features,
    )[0]


def global_attn_backward(line, here, kept, first, lengths, grads, lanes=1024):
    micros, _, items = lengths.shape
    _, count, features = kept[0].shape
    frames = count // micros
    width, groups = features // HEADS, features // lanes
    block = (frames, lanes)

    def kernel(scalars, ins, outs, _):
        core = scalars[0][0]
        q, k, v = [read(core, i)[0] for i in ins[:3]]
        global_attn_bwd_kernel(
            width, items, core, scalars[1], q, k, v, ins[3][0], ins[4][0], *outs
        )

    half = (sds((2, frames, features)), (2,) + block, lambda h, *_: (0, 0, h))
    return line.launch(
        kernel,
        "global_attn_backward",
        [here, lengths],
        (groups,),
        [(kept, (1,) + block, lambda h, c, _, i=i: (first + i, c[0], h)) for i in range(3)]
        + [(g, block, lambda h, *_: (0, h)) for g in grads],
        [half] * 2,
        flops=30000 * frames * features,
    )


def place_columns(line, here, sources, rows, spots, cut=False):
    features = spots.shape[0]

    def kernel(scalars, ins, outs, _):
        for i, refs in enumerate(ins[1:]):
            block = read(scalars[0][0], refs).reshape(rows, features)
            placed = dot(block, ins[0][0][...]).astype(BF16)
            wide = features // len(outs)
            for k, out in enumerate(outs):
                out[i] = placed[:, k * wide : (k + 1) * wide]

    ins = [whole(spots)]
    for source in sources:
        if isinstance(source, tuple):
            ins.append((source[0], (1, rows, features), lambda _, s, plane=source[1]: (plane, 0, 0)))
        else:
            ins.append(whole(source))
    parts = 2 if cut else 1
    out = line.launch(
        kernel,
        "place_columns",
        [here],
        (1,),
        ins,
        [full((len(sources), rows, features // parts))] * parts,
        flops=2 * len(sources) * rows * features * features,
    )
    return out if cut else out[0]


def place_units(line, table, source, rows, units):
    per = 4

    def kernel(scalars, ins, outs, _):
        for i in range(per):
            outs[0][0, :, i * UNIT : (i + 1) * UNIT] = read(scalars[0][0], ins[i])[0]

    first, count = units

    def at(i):
        return lambda u, t: (0, 0, t[1 + first + u * per + i])

    return line.launch(
        kernel,
        "place_units",
        [table],
        (count // per,),
        [(source, (1, rows, UNIT), at(i)) for i in range(per)],
        [(sds((1, rows, count * UNIT)), (1, rows, per * UNIT), lambda u, t: (0, 0, u))],
    )[0]


def pack(line, here, arrays, features):
    count = arrays[0].shape[0]
    planes = [(i, c) for i, a in enumerate(arrays) for c in range(a.shape[1] // features)]

    def kernel(scalars, ins, outs, _):
        for plane, (i, c) in enumerate(planes):
            outs[0][plane] = ins[i][0][:, c * features : (c + 1) * features].astype(BF16)

    return line.launch(
        kernel,
        "pack",
        [here],
        (1,),
        [whole(a) for a in arrays],
        [full((len(planes), count, features))],
    )[0]


class Group:
    def __init__(self, table, units, lefts, rights, tile, tiles, plane):
        self.table, self.per = table, units // 4
        self.lefts, self.rights = lefts, rights
        self.tile, self.tiles, self.plane = tile, tiles, plane


def joined(core, blocks, ordered):
    if ordered:
        pairs = []
        for a, b in zip(blocks[::2], blocks[1::2]):
            pairs += [jnp.where(core == 0, a, b), jnp.where(core == 0, b, a)]
        blocks = pairs
    return blocks[0] if len(blocks) == 1 else jnp.concatenate(blocks, axis=0)


def weight_grad(line, group, first, steps, per, addends, split):
    lefts, rights, tile = group.lefts, group.rights, group.tile

    def kernel(scalars, ins, outs, _):
        core = scalars[0][0]
        left_refs = [ins[i * per : (i + 1) * per] for i in range(len(lefts))]
        ins = ins[len(lefts) * per :]
        right = joined(
            core, [r[0][0] for r in ins[: len(rights)]], len(rights) > len(lefts)
        )
        add_refs = [r[0] for r in ins[len(rights) :]]
        for i in range(per):
            at = slice(i * UNIT, (i + 1) * UNIT)
            left = joined(
                core, [read(core, r[i])[0] for r in left_refs], len(lefts) > len(rights)
            )
            out = add_all([t_dot(left, right)] + [r[at, :].astype(F32) for r in add_refs])
            out = out.astype(BF16)
            if not split:
                outs[0][at, :] = out
            elif per == 1:
                outs[0][...] = out[: UNIT // 2]
                outs[1][...] = out[UNIT // 2 :]
            else:
                half = per // 2
                outs[i // half][(i % half) * UNIT : (i % half + 1) * UNIT, :] = out

    def left_in(given, start, i):
        rows = (given[0] if isinstance(given, tuple) else given).shape[1]
        return (
            given,
            (1, rows, UNIT),
            lambda u, j, t: (group.plane(j, t), 0, t[start + first + u * per + i]),
        )

    def right_in(given, count, at):
        return given, (1, count, tile), lambda u, j, t: at(j, t)

    def block(skip, rows=per * UNIT):
        return (rows, tile), lambda u, j, t: (skip + u, j)

    wide = group.tiles * tile
    rows = sum(count for _, count, _ in rights)
    if split:
        outs = [(sds((per * UNIT // 2, wide)),) + block(0, per * UNIT // 2)] * 2
    else:
        outs = [(sds((steps * per * UNIT, wide)),) + block(0)]
    out = line.launch(
        kernel,
        "weight_grad",
        [group.table],
        (steps, group.tiles),
        [left_in(a, start, i) for a, start in lefts for i in range(per)]
        + [right_in(*right) for right in rights]
        + [(a,) + block(skip) for a, skip in addends],
        outs,
        flops=2 * steps * per * UNIT * wide * rows,
    )
    return out if split else out[0]


class Devices:
    def __init__(self, size):
        self.size = size
        self.core = lax.axis_index("section")
        self.index = lax.axis_index("dp")

    def bits(self, core, kind):
        near = [1, 2] if core == 0 else [2, 1]
        far = [1 << b for b in range(2, self.size.bit_length() - 1)]
        return far[:1] + near + far[1:] if kind == FAR else near + far

    def swap(self, array, step, kind):
        pairs = []
        for core in range(2):
            by = self.bits(core, kind)[step]
            pairs += [(core * self.size + i, core * self.size + (i ^ by)) for i in range(self.size)]
        return lax.ppermute(array, ("section", "dp"), pairs)

    def cores(self, array):
        return lax.ppermute(array, "section", [(0, 1), (1, 0)])

    def order(self, kind):
        orders = []
        for core in range(2):
            bits = self.bits(core, kind)
            if kind == LINE:
                bits = bits[:2] + bits[:1:-1]
            order = [
                sum(bit for i, bit in enumerate(bits) if (spot >> (len(bits) - 1 - i)) & 1)
                for spot in range(self.size)
            ]
            orders.append(jnp.array(order, jnp.int32))
        return jnp.where(self.core == 0, orders[0], orders[1]) ^ (
            self.index % 4 if kind == LINE else self.index
        )

    def columns(self, count, kind):
        block = count // self.size
        order = self.order(kind)
        return (order[:, None] * block + jnp.arange(block, dtype=jnp.int32)).reshape(-1)

    def spots(self, count, kind):
        at = self.columns(count, kind)[None, :]
        return (lax.broadcasted_iota(jnp.int32, (count, count), 0) == at).astype(BF16)

    def along_z(self, array):
        depth = self.size // 4
        groups = [[4 * z + place for z in range(depth)] for place in range(4)]
        return lax.psum_scatter(
            array, "dp", scatter_dimension=0, axis_index_groups=groups, tiled=True
        )

    def table(self, *orders):
        parts = [self.core[None].astype(jnp.int32)] + [jnp.asarray(o, jnp.int32) for o in orders]
        return jnp.concatenate(parts)


class Sum:
    def __init__(self, devices, line, group, step=0, kind=LINE):
        self.devices, self.line, self.group, self.step = devices, line, group, step
        self.one, self.kind = None, kind
        self.rider = None

    def grad(self, first, count, addends, split=False):
        group = self.group
        steps, per = (count, group.per) if group.per > 1 else (1, count)
        return weight_grad(self.line, group, first * group.per, steps, per, addends, split)

    def send(self, array):
        rows, columns = array.shape
        if self.rider is not None:
            shape, size = self.rider.shape, self.rider.size
            high = self.rider.astype(BF16)
            low = (self.rider - high.astype(F32)).astype(BF16)
            extra = jnp.concatenate([high, low]).reshape(-1, columns)
            extra = jnp.pad(extra, ((0, -extra.shape[0] % RIDER), (0, 0)))
            array = jnp.concatenate([array, extra])
        got = self.devices.swap(array, self.step, self.kind)
        if self.rider is not None:
            extra = got[rows:].astype(F32).reshape(-1)
            self.rider = self.rider + (extra[:size] + extra[size : 2 * size]).reshape(shape)
        self.step += 1
        return got

    def first(self):
        self.one = self.send(self.grad(2, 2, []))

    def second(self):
        self.two = self.send(self.grad(1, 1, [] if self.one is None else [(self.one, 1)]))

    def third(self):
        addends = [(one, 0) for one in (self.one, self.two) if one is not None]
        if self.kind == LINE:
            self.kept = self.devices.along_z(self.grad(0, 1, addends))
            return
        self.kept, sent = self.grad(0, 1, addends, split=True)
        self.got = self.send(sent)

    def rest(self):
        if self.kind == LINE:
            return
        steps = self.devices.size.bit_length() - 1
        total = self.kept
        while self.step < steps:
            got = self.got
            half = total.shape[0] // 2
            sent = (total[half:].astype(F32) + got[half : 2 * half].astype(F32)).astype(BF16)
            total = total[:half].astype(F32) + got[:half].astype(F32)
            if self.step < steps - 1:
                total = total.astype(BF16)
            self.line.wait(sent)
            self.got = self.send(sent)
        self.kept = total

    def last(self):
        return self.kept.astype(F32) + self.got[: self.kept.shape[0]].astype(F32)


PLAN = (
    "g_qkv",
    "g_attn",
    "g_mlp",
    "g_pack",
    "l_qkv",
    "l_attn",
    "l_mlp",
    "l_place",
    "l_down first",
    "l_mlp_back",
    "l_attn_back",
    "l_down second",
    "g_units",
    "g_place",
    "l_up first",
    "l_down third",
    "l_rest first",
    "l_down rest",
    "l_qkv_back",
    "g_mlp_back",
    "wait l_down one",
    "wait active_got",
    "g_attn_back",
    "g_qkv_back",
    "wait placed_got",
    "g_gains",
    "l_rest second",
    "l_up second",
    "g_up second",
    "l_output",
    "l_up third",
    "g_output",
    "wait l_rest two",
    "l_up rest",
    "g_rest second",
    "g_up third",
    "g_down second",
    "l_rest third",
    "wait l_down kept",
    "wait l_dz",
    "g_rest third",
    "l_rest rest",
    "g_down third",
    "g_down rest",
    "g_rest rest",
    "g_up rest",
    "up_out",
    "rest_out",
    "down_out",
)


def both_halves(line, here, devices, ours, theirs, parts):
    rows, wide = ours.kept.shape
    half = jax.ShapeDtypeStruct((rows, wide), BF16)
    operands = [[one.kept] if one.kind == LINE else [one.kept, one.got] for one in (ours, theirs)]
    count = len(operands[0])

    def split(scalars, ins, outs, _):
        core = scalars[0][0]
        terms = [i[0][:rows, :].astype(F32) for i in ins]
        mine, other = add_all(terms[:count]), add_all(terms[count:])
        outs[0][...] = jnp.where(core == 0, other, mine).astype(BF16)
        outs[1][...] = jnp.where(core == 0, mine, other)

    sent, mine = line.launch(
        split,
        "split_halves",
        [here],
        (1,),
        [whole(one) for one in operands[0] + operands[1]],
        [full(half.shape), full(half.shape, F32)],
    )
    got = devices.cores(sent)

    def join(scalars, ins, outs, _):
        core = scalars[0][0]
        mine, got = ins[0][0][...], ins[1][0][...].astype(F32)
        joined = jnp.concatenate(
            [jnp.where(core == 0, mine, got), jnp.where(core == 0, got, mine)], axis=1
        )
        start = 0
        for out in outs:
            out[0] = joined[:, start : start + out.shape[2]]
            start += out.shape[2]

    return line.launch(
        join,
        "join_halves",
        [here],
        (1,),
        [whole(mine), whole(got)],
        [full((1, rows, 2 * wide * part // sum(parts)), F32) for part in parts],
    )


def local(codebook_embed, item_lengths, gain_attn, w_qkv, w_out, gain_mlp, w_up, w_down, cotangent):
    size = lax.axis_size("dp")
    micros, frames, books, features = codebook_embed.shape
    half_width = features // 2
    scale_in = books**-0.5
    devices, line = Devices(size), Line()
    core = devices.core
    first_core = core == 0
    here = core[None].astype(jnp.int32)

    def zero(core):
        return 0

    def same(core):
        return core

    gains = jnp.stack([gain_attn[0], gain_mlp[0]])
    own = [w_qkv[0], w_out[0], w_up[0], w_down[0]]
    gains_other = devices.cores(gains)
    other = [devices.cores(w) for w in own]
    w_qkv_g, w_out_g, w_up_g, w_down_g = zip(own, other)
    w_qkv_l, w_out_l, w_up_l, w_down_l = zip(other, own)
    gains_g = [(gains[i : i + 1], gains_other[i : i + 1]) for i in range(2)]
    gains_l = [(b, a) for a, b in gains_g]

    embed = codebook_embed.transpose(0, 2, 1, 3)
    upstream = cotangent.transpose(0, 2, 1, 3).reshape(micros, -1, features)

    def with_first(array):
        return array, devices.cores(array)

    columns = w_down.shape[1]
    unit_rows = columns // size == UNIT
    units = columns // UNIT
    near, far = range(units // 2), range(units // 2, units)
    placed_table = devices.table([0, 1, 2, 3], [0, 2, 1, 3])
    down_order = devices.order(DOWN_KIND) if unit_rows else range(units)
    down_table = devices.table(down_order, range(units))
    local_table = devices.table(devices.order(LOCAL_DOWN_KIND) if unit_rows else range(units))
    spots = devices.spots(features, REST_KIND)
    local_spots = devices.spots(features, LOCAL_REST_KIND)

    def by_units(array, kind):
        if unit_rows:
            return array
        if isinstance(array, tuple):
            return tuple(by_units(a, kind) for a in array)
        return jnp.take(array[:1], devices.columns(columns, kind), axis=2)

    def down_group(table, lefts, rights):
        return Group(table, units, lefts, rights, half_width, 1, lambda j, t: 0)

    def up_group(lefts, rights):
        return Group(
            placed_table,
            4,
            lefts,
            [(a, count, lambda j, t, i=i: (0, i, j)) for a, count, i in rights],
            features,
            2,
            lambda j, t: 2,
        )

    def rest_group(lefts, rights):
        return Group(
            placed_table,
            4,
            lefts,
            [(a, count, lambda j, t, i=i: (j, i, 0)) for a, count, i in rights],
            features,
            2,
            lambda j, t: jnp.where(2 * t[0] + j == 3, 1, 0),
        )

    def my_half(array):
        return jnp.where(first_core, array[..., :half_width], array[..., half_width:])

    def other_half(array):
        return jnp.where(first_core, array[..., half_width:], array[..., :half_width])

    def halves(array):
        got = devices.cores(other_half(array).astype(BF16)).astype(array.dtype)
        mine = my_half(array)
        return jnp.where(first_core, jnp.stack([mine, got]), jnp.stack([got, mine]))

    def both(mine, others):
        return [(mine, mine.shape[1], 0), (devices.cores(others), mine.shape[1], 0)]

    def all_rows(mine, others, kind):
        rights = both(mine, others)
        far = devices.swap(jnp.concatenate([rights[0][0], rights[1][0]], axis=1), 0, kind)
        return rights + [(far, frames, i) for i in range(micros)]

    at = types.SimpleNamespace()

    def g_qkv():
        def frame_rows(core, ins):
            (e_ref,) = ins[0]
            return [
                add_all([e_ref[m, b].astype(F32) for b in range(books)]) * scale_in
                for m in range(micros)
            ]

        at.rows, at.normed, at.packed = qkv_forward(
            line, here, (micros * frames, [whole(embed)]), frame_rows, gains[:1], own[0]
        )

    def g_attn():
        at.mixture = global_attn_forward(line, at.packed, item_lengths)

    def g_mlp():
        result, at.middle, at.normed_two, active = mlp_forward(
            line, here, at.rows, at.mixture, own[1], gains[1:], own[2], own[3], True
        )
        at.states, at.active = with_first(result), with_first(active)
        at.active_units = by_units(at.active, DOWN_KIND)

    def g_pack():
        arrays = [at.normed, at.mixture, at.normed_two, at.packed, at.middle]
        at.kept = with_first(pack(line, here, arrays, features))

    def l_qkv():
        def local_rows(core, ins):
            (e_ref,), s_refs = ins
            state = read(core, s_refs).astype(F32)
            return [e_ref[0, b].astype(F32) + state for b in range(books)]

        parts = [
            (embed, (1, books, frames, features), lambda j, s: (s[0], 0, 0, 0)),
            (at.states, (frames, features), lambda j, s: (s[0], 0)),
        ]
        at.l_rows, at.l_normed, at.l_packed = qkv_forward(
            line, here, (books * frames, parts), local_rows, gains_l[0], w_qkv_l
        )

    def l_attn():
        at.l_mixture = local_attn(line, here, at.l_packed, books)

    def l_mlp():
        at.l_out, at.l_middle, at.l_normed_two, at.l_active, at.l_slope = mlp_forward(
            line, here, at.l_rows, at.l_mixture, w_out_l, gains_l[1], w_up_l, w_down_l, False
        )
        at.l_active_got = devices.cores(at.l_active)
        at.l_down = Sum(
            devices,
            line,
            down_group(
                local_table,
                [
                    (by_units(at.l_active, LOCAL_DOWN_KIND), 1),
                    (by_units(at.l_active_got, LOCAL_DOWN_KIND), 1),
                ],
                [
                    (upstream, books * frames, lambda j, t: (t[0], 0, t[0])),
                    (upstream, books * frames, lambda j, t: (1 - t[0], 0, t[0])),
                ],
            ),
            kind=LOCAL_DOWN_KIND,
        )

    def g_units():
        at.active_got = devices.swap(
            place_units(line, down_table, at.active_units, micros * frames, (far.start, len(far))),
            0,
            DOWN_KIND,
        )

    def g_place():
        at.placed, placed_far = place_columns(
            line, here, [(at.kept, i) for i in range(3)], micros * frames, spots, True
        )
        at.placed_got = devices.swap(placed_far, 0, REST_KIND)

    def l_place():
        placed = place_columns(
            line, here, [at.l_normed, at.l_mixture, at.l_normed_two], books * frames, local_spots
        )
        at.l_placed_got = devices.cores(placed)
        at.l_lefts = [(placed, 1), (at.l_placed_got, 5)]

    def l_mlp_back():
        at.l_low, dz_own, dz_other, at.l_dm, at.l_do, at.l_gain_two = mlp_backward(
            line,
            here,
            (upstream, same, zero, books * frames),
            (at.l_slope, 0, zero),
            (at.l_middle[None], 0, zero),
            w_out_l,
            gains_l[1],
            w_up_l,
            w_down_l,
        )
        at.l_dz = both(dz_own, dz_other)

    def l_attn_back():
        grads = (at.l_do, at.l_low)
        at.l_dp = local_attn(line, here, at.l_packed, books, grads)
        at.l_rights = both(*at.l_dp)

    def l_qkv_back():
        at.local_grad, at.frame_grad, at.l_gain_one = qkv_backward(
            line, here, *at.l_dp, (at.l_rows, zero), at.l_dm, gains_l[0], w_qkv_l, books
        )
        at.g_frame = all_rows(at.frame_grad, at.frame_grad, DOWN_KIND)

    def l_output():
        at.local_out = halves(at.l_out.reshape(books, frames, features))
        line.wait(at.local_out)

    def g_mlp_back():
        at.g_low, dz_own, dz_other, at.g_dm, at.g_do, at.g_gain_two = mlp_backward(
            line,
            here,
            (at.frame_grad, zero, zero, frames),
            (at.active, 1, same),
            (at.kept, 6, same),
            w_out_g,
            gains_g[1],
            w_up_g,
            w_down_g,
        )
        at.g_dz = all_rows(dz_own, dz_other, REST_KIND)

    def g_attn_back():
        grads = (at.g_do, at.g_low)
        at.g_dp = global_attn_backward(line, here, at.kept, 3, item_lengths, grads)
        at.g_rights = all_rows(*at.g_dp, REST_KIND)

    def g_qkv_back():
        at.global_grad, _, at.g_gain_one = qkv_backward(
            line, here, *at.g_dp, (at.rows, same), at.g_dm, gains_g[0], w_qkv_g, 1
        )

    def g_gains():
        gains = [at.g_gain_one, at.g_gain_two, at.l_gain_one, at.l_gain_two]
        gains = jnp.concatenate(gains)
        at.gains = gains + devices.swap(gains, 0, REST_KIND)
        line.wait(at.gains)

    def g_output():
        at.embed_grad = halves(
            at.local_grad.reshape(books, frames, features) + (at.global_grad * scale_in)[None]
        )
        line.wait(at.embed_grad)

    def down_out():
        (at.down,) = both_halves(line, here, devices, at.g_down, at.l_down, (1,))

    def up_out():
        (at.up,) = both_halves(line, here, devices, at.g_up, at.l_up, (1,))

    def rest_out():
        at.qkv, at.out = both_halves(line, here, devices, at.g_rest, at.l_rest, (3, 1))

    def make(name):
        if not hasattr(at, name):
            if name == "l_up":
                one = Sum(devices, line, up_group(at.l_lefts, at.l_dz), kind=LOCAL_REST_KIND)
            elif name == "l_rest":
                one = Sum(devices, line, rest_group(at.l_lefts, at.l_rights), kind=LOCAL_REST_KIND)
            elif name == "g_down":
                lefts = [(at.active_units, 1), (at.active_got, 1 + units)]
                rights = [(a, count, lambda j, t, i=i: (0, i, t[0])) for a, count, i in at.g_frame]
                one = Sum(devices, line, down_group(down_table, lefts, rights), 1, DOWN_KIND)
            else:
                lefts = [(at.placed, 1), (at.placed_got, 1)]
                if name == "g_up":
                    one = Sum(devices, line, up_group(lefts, at.g_dz), 1, REST_KIND)
                    one.rider = at.gains
                else:
                    one = Sum(devices, line, rest_group(lefts, at.g_rights), 1, REST_KIND)
            setattr(at, name, one)
        return getattr(at, name)

    steps = (g_qkv, g_attn, g_mlp, g_pack, l_qkv, l_attn, l_mlp, g_units, g_place, l_place)
    steps += (l_mlp_back, l_attn_back, l_qkv_back, l_output)
    steps += (g_mlp_back, g_attn_back, g_qkv_back, g_gains, g_output)
    steps += (down_out, up_out, rest_out)
    steps = {step.__name__: step for step in steps}
    for words in PLAN:
        name, *rest = words.split()
        if name in steps:
            steps[name]()
        elif name == "wait":
            one = getattr(at, rest[0])
            one = getattr(one, rest[1]) if rest[1:] not in ([], ["far"]) else one
            line.wait(one[2 if "far" in rest else 1][0] if isinstance(one, list) else one)
        else:
            getattr(make(name), rest[0])()
    gain_sums = at.g_up.rider
    gain_sums = gain_sums + devices.cores(gain_sums)
    gain_sums = jnp.where(first_core, gain_sums[:2], gain_sums[2:]).reshape(2, size, -1)
    gain_sums = lax.dynamic_index_in_dim(gain_sums, devices.index, 1, keepdims=False)

    return (
        at.local_out.transpose(0, 2, 1, 3),
        at.embed_grad.transpose(0, 2, 1, 3),
        gain_sums[:1],
        at.qkv,
        at.out,
        gain_sums[1:],
        at.up,
        at.down,
    )


def solution(mesh):
    in_specs = (
        P(None, "dp", None, None),
        P(None, "dp", None),
        P("section", None),
        P("section", None, None),
        P("section", None, None),
        P("section", None),
        P("section", None, None),
        P("section", None, None),
        P(None, "dp", None, None),
    )
    out_specs = (
        P(None, "dp", None, "section"),
        P(None, "dp", None, "section"),
        P("section", "dp"),
        P("section", "dp", None),
        P("section", "dp", None),
        P("section", "dp"),
        P("section", "dp", None),
        P("section", "dp", None),
    )
    return jax.shard_map(local, mesh=mesh, in_specs=in_specs, out_specs=out_specs, check_vma=False)
```

```python
import functools
import types

import jax
import jax.numpy as jnp
from jax import lax
from jax.experimental import pallas as pl
from jax.experimental.pallas import tpu as pltpu
from jax.sharding import PartitionSpec as P

HEADS = 16
EPSILON = 1e-05
BF16 = jnp.bfloat16
F32 = jnp.float32
VMEM_LIMIT = 48 * 1024 * 1024
CHUNK = 128
COST = 1.0
COST_SUMS = 1.0
LINE, NEAR, FAR = range(3)
DOWN_KIND = FAR
REST_KIND = FAR
LOCAL_DOWN_KIND = LINE
LOCAL_REST_KIND = LINE
RIDER = 16
UNIT = 256


def dot(left, right):
    return jnp.dot(left, right, preferred_element_type=F32)


def dot_t(left, right):
    return lax.dot_general(left, right, (((1,), (1,)), ((), ())), preferred_element_type=F32)


def t_dot(left, right):
    return lax.dot_general(left, right, (((0,), (0,)), ((), ())), preferred_element_type=F32)


def add_all(terms):
    return functools.reduce(lambda s, t: s + t, terms)


def sds(shape, dtype=BF16):
    return jax.ShapeDtypeStruct(shape, dtype)


class Weight:
    def __init__(self, given, block, index, tiles):
        self.arrays = list(given) if isinstance(given, tuple) else [given]
        self.block, self.index, self.tiles = block, index, tiles
        self.slots = min(tiles, 2)


class Tiles:
    def __init__(self, weight, core, refs, held, sems):
        self.weight, self.core, self.refs, self.held, self.sems = weight, core, refs, held, sems

    def copy(self, place, j):
        block = self.weight.block
        at = zip(self.weight.index(j, self.core), block)
        at = tuple(pl.ds(pl.multiple_of(i * b, b), b) for i, b in at)
        slot = j % self.weight.slots
        return pltpu.make_async_copy(self.refs[place].at[at], self.held.at[slot], self.sems.at[slot])

    def start(self, j):
        for place in range(len(self.refs)):
            if len(self.refs) == 1:
                self.copy(place, j).start()
            else:

                @pl.when(self.core == place)
                def _():
                    self.copy(place, j).start()

    def get(self, j):
        self.copy(0, j).wait()
        return self.held[j % self.weight.slots]

    def ahead(self, j):
        @pl.when(j == 0)
        def _():
            self.start(0)

        if self.weight.tiles > 1:

            @pl.when(j + 1 < self.weight.tiles)
            def _():
                self.start(j + 1)


class Line:
    def __init__(self):
        self.behind = []

    def wait(self, *arrays):
        self.behind.extend(arrays)

    def launch(self, kernel, name, scalars, grid, ins, outs, scratch=(), flops=0):
        arrays, specs, counts, held = [], [], [], []
        for operand in ins:
            if isinstance(operand, Weight):
                specs.extend([pl.BlockSpec(memory_space=pl.ANY)] * len(operand.arrays))
                arrays.extend(operand.arrays)
                counts.append(operand)
                held.append(pltpu.VMEM((operand.slots,) + operand.block, operand.arrays[0].dtype))
                held.append(pltpu.SemaphoreType.DMA((operand.slots,)))
                continue
            given, block, index = operand
            if isinstance(given, tuple):
                for place in range(2):

                    def at(*args, place=place, index=index):
                        here = args[len(grid)][0] == place
                        return tuple(jnp.where(here, i, 0) for i in index(*args))

                    specs.append(pl.BlockSpec(block, at))
                arrays.extend(given)
                counts.append(2)
            else:
                specs.append(pl.BlockSpec(block, index))
                arrays.append(given)
                counts.append(1)
        skipped = len(self.behind)
        arrays.extend(self.behind)
        specs.extend([pl.BlockSpec(memory_space=pl.ANY)] * skipped)

        def body(*refs):
            scalar_refs, refs = refs[: len(scalars)], refs[len(scalars) :]
            groups, own = [], refs[len(refs) - len(held) :]
            for count in counts:
                if isinstance(count, Weight):
                    weight, count = count, len(count.arrays)
                    core = scalar_refs[0][0]
                    groups.append(Tiles(weight, core, list(refs[:count]), *own[:2]))
                    own = own[2:]
                else:
                    groups.append(list(refs[:count]))
                refs = refs[count:]
            refs = refs[skipped : len(refs) - len(held)]
            kernel(scalar_refs, groups, refs[: len(outs)], refs[len(outs) :])

        share = COST_SUMS if name == "weight_grad" else COST
        out = pl.pallas_call(
            body,
            grid_spec=pltpu.PrefetchScalarGridSpec(
                num_scalar_prefetch=len(scalars),
                grid=grid,
                in_specs=specs,
                out_specs=[pl.BlockSpec(block, index) for _, block, index in outs],
                scratch_shapes=list(scratch) + held,
            ),
            out_shape=[shape for shape, _, _ in outs],
            compiler_params=pltpu.CompilerParams(vmem_limit_bytes=VMEM_LIMIT),
            cost_estimate=pl.CostEstimate(
                flops=int(flops * share),
                bytes_accessed=int(share * sum(a.size * a.dtype.itemsize for a in arrays[: len(specs) - skipped])),
                transcendentals=0,
            ),
            name=name,
        )(*scalars, *arrays)
        self.behind = [out[0]]
        return out


def read(core, refs):
    if len(refs) == 1:
        return refs[0][...]
    return jnp.where(core == 0, refs[0][...], refs[1][...])


def origin(rank):
    return lambda *_: (0,) * rank


def whole(array):
    return array, array.shape, origin(array.ndim)


def full(shape, dtype=BF16):
    return sds(shape, dtype), shape, origin(len(shape))


def rstd(rows):
    return lax.rsqrt(jnp.mean(rows * rows, axis=-1, keepdims=True) + EPSILON)


def by_chunks(rows, step):
    def one(i, carry):
        step(pl.ds(pl.multiple_of(i * CHUNK, CHUNK), CHUNK))
        return carry

    lax.fori_loop(0, rows // CHUNK, one, 0)


def norm_backward(grad, rows, gain):
    scale = rstd(rows)
    plain = rows * scale
    grad_gain = jnp.sum(grad * plain, axis=0, keepdims=True)
    lead = grad * gain
    return scale * (lead - plain * jnp.mean(lead * plain, axis=-1, keepdims=True)), grad_gain


def gelu_parts(hidden):
    c = 0.7978845608028654
    square = hidden * hidden
    t = jnp.tanh(hidden * (c + (c * 0.044715) * square))
    half = 0.5 + 0.5 * t
    slope = half + (hidden * half) * ((1.0 - t) * (c + (3 * 0.044715 * c) * square))
    return (hidden * half).astype(BF16), slope.astype(BF16)


def qkv_forward(line, here, parts, make_rows, gain, w_qkv, tile=1536):
    features = gain[0].shape[1] if isinstance(gain, tuple) else gain.shape[1]
    count, wide = parts[0], 3 * features

    def kernel(scalars, ins, outs, _):
        core = scalars[0][0]
        gain_refs, w = ins[-2:]
        x_ref, h_ref, p_ref = outs
        j = pl.program_id(0)
        w.ahead(j)

        @pl.when(j == 0)
        def _():
            gain = read(core, gain_refs)
            for i, x in enumerate(make_rows(core, ins[:-2])):
                at = slice(i * CHUNK, (i + 1) * CHUNK)
                x_ref[at, :] = x
                h_ref[at, :] = (x * rstd(x) * gain).astype(BF16)

        p_ref[...] = dot(h_ref[...], w.get(j)).astype(BF16)

    return line.launch(
        kernel,
        "qkv_forward",
        [here],
        (wide // tile,),
        parts[1]
        + [
            (gain, (1, features), origin(2)),
            Weight(w_qkv, (features, tile), lambda j, core: (0, j), wide // tile),
        ],
        [
            full((count, features), F32),
            full((count, features)),
            (sds((count, wide)), (count, tile), lambda j, s: (0, j)),
        ],
        flops=2 * count * features * wide,
    )


def mlp_forward(line, here, rows, mixture, w_out, gain, w_up, w_down, joined, tile=1024):
    count, features = rows.shape
    wide = (w_up[0] if isinstance(w_up, tuple) else w_up).shape[1]

    def kernel(scalars, ins, outs, scratch):
        core = scalars[0][0]
        (x_ref,), (o_ref,), w_out, gain_refs, w_up, w_down = ins
        y_ref, m_ref, h_ref = outs[:3]
        (acc_ref,) = scratch
        j = pl.program_id(0)
        for w in (w_out, w_up, w_down):
            w.ahead(j)

        @pl.when(j == 0)
        def _():
            gain, wide_out = read(core, gain_refs), w_out.get(0)

            def step(at):
                m = x_ref[at, :] + dot(o_ref[at, :], wide_out)
                m_ref[at, :] = m
                acc_ref[at, :] = m
                h_ref[at, :] = (m * rstd(m) * gain).astype(BF16)

            by_chunks(count, step)

        g, slope = gelu_parts(dot(h_ref[...], w_up.get(j)))
        if joined:
            outs[3][0] = g
            outs[3][1] = slope
        else:
            outs[3][0] = g
            outs[4][0] = slope
        acc_ref[...] += dot(g, w_down.get(j))

        @pl.when(pl.program_id(0) == pl.num_programs(0) - 1)
        def _():
            y_ref[...] = acc_ref[...].astype(BF16)

    planes = 2 if joined else 1
    wide_out = (sds((planes, count, wide)), (planes, count, tile), lambda j, s: (0, 0, j))
    return line.launch(
        kernel,
        "mlp_forward",
        [here],
        (wide // tile,),
        [
            whole(rows),
            whole(mixture),
            Weight(w_out, (features, features), lambda j, core: (0, 0), 1),
            (gain, (1, features), origin(2)),
            Weight(w_up, (features, tile), lambda j, core: (0, j), wide // tile),
            Weight(w_down, (tile, features), lambda j, core: (j, 0), wide // tile),
        ],
        [full(rows.shape), full(rows.shape, F32), full(rows.shape)] + [wide_out] * (3 - planes),
        [pltpu.VMEM(rows.shape, F32)],
        flops=2 * count * features * (features + 2 * wide),
    )


def mlp_backward(line, here, low_out, slope, middle, w_out, gain, w_up, w_down, tile=1024):
    wide, features = w_down[0].shape
    count = low_out[3]
    tiles = wide // tile
    half = tiles // 2

    def kernel(scalars, ins, outs, scratch):
        core = scalars[0][0]
        (dy_ref,), s_refs, m_refs, gain_refs, w_down, w_up, w_out = ins
        low_ref, own_ref, other_ref, dm_ref, do_ref, gg_ref = outs
        (acc_ref,) = scratch
        j = pl.program_id(0)
        for w in (w_down, w_up, w_out):
            w.ahead(j)
        slope = read(core, s_refs)[0].astype(F32)
        dz = (slope * dot_t(dy_ref[0], w_down.get(j))).astype(BF16)

        @pl.when(j < half)
        def _():
            other_ref[0] = dz

        @pl.when(j >= half)
        def _():
            own_ref[0] = dz

        term = dot_t(dz, w_up.get(j))

        @pl.when(j == 0)
        def _():
            acc_ref[...] = term

        @pl.when(j > 0)
        def _():
            acc_ref[...] += term

        @pl.when(j == tiles - 1)
        def _():
            gg_ref[...] = jnp.zeros_like(gg_ref)
            gain, wide_out = read(core, gain_refs), w_out.get(0)

            def step(at):
                if len(m_refs) == 1:
                    m = m_refs[0][0, at, :].astype(F32)
                else:
                    m = jnp.where(core == 0, m_refs[0][0, at, :], m_refs[1][0, at, :]).astype(F32)
                dm, gg = norm_backward(acc_ref[at, :], m, gain)
                gg_ref[...] += gg
                dm = dm + dy_ref[0, at, :].astype(F32)
                dm_ref[at, :] = dm
                low = dm.astype(BF16)
                low_ref[at, :] = low
                do_ref[at, :] = dot_t(low, wide_out).astype(BF16)

            by_chunks(count, step)

    def at(j, core):
        return (j + (1 - core) * half) % tiles

    shape = (count, features)
    return line.launch(
        kernel,
        "mlp_backward",
        [here],
        (tiles,),
        [
            (low_out[0], (1,) + shape, lambda j, s: (low_out[1](s[0]), low_out[2](s[0]), 0)),
            (slope[0], (1, count, tile), lambda j, s: (slope[1], slope[2](s[0]), at(j, s[0]))),
            (middle[0], (1,) + shape, lambda j, s: (middle[1], middle[2](s[0]), 0)),
            (gain, (1, features), origin(2)),
            Weight(w_down, (tile, features), lambda j, core: (at(j, core), 0), tiles),
            Weight(w_up, (features, tile), lambda j, core: (0, at(j, core)), tiles),
            Weight(w_out, (features, features), lambda j, core: (0, 0), 1),
        ],
        [
            full(shape),
            (
                sds((1, count, wide // 2)),
                (1, count, tile),
                lambda j, s: (0, 0, jnp.maximum(j - half, 0)),
            ),
            (
                sds((1, count, wide // 2)),
                (1, count, tile),
                lambda j, s: (0, 0, jnp.minimum(j, half - 1)),
            ),
            full(shape, F32),
            full(shape),
            full((1, features), F32),
        ],
        [pltpu.VMEM(shape, F32)],
        flops=2 * count * features * (features + 2 * wide),
    )


def qkv_backward(line, here, own, other, rows, grad_middle, gain, w_qkv, books, tile=512):
    count, features = grad_middle.shape
    frames = count // books

    def kernel(scalars, ins, outs, scratch):
        core = scalars[0][0]
        (own_ref,), (other_ref,), (x_ref,), (dm_ref,), gain_refs, w_tiles = ins
        dx_ref, sum_ref, gg_ref = outs
        (acc_ref,) = scratch
        j = pl.program_id(0)
        w_tiles.ahead(j)
        w = w_tiles.get(j)
        terms = []
        for i in range(3):
            part = jnp.where(core == i // 2, own_ref[i % 2], other_ref[i % 2])
            terms.append(dot_t(part, w[:, i * features : (i + 1) * features]))
        acc_ref[:, pl.ds(pl.multiple_of(j * tile, tile), tile)] = add_all(terms)

        @pl.when(j == pl.num_programs(0) - 1)
        def _():
            gg_ref[...] = jnp.zeros_like(gg_ref)
            gain = read(core, gain_refs)
            total = 0.0
            for b in range(books):
                at = slice(b * frames, (b + 1) * frames)
                dx, gg = norm_backward(acc_ref[at, :], x_ref[at, :], gain)
                gg_ref[...] += gg
                dx = dx + dm_ref[at, :]
                dx_ref[at, :] = dx
                total = total + dx
            sum_ref[0] = total.astype(BF16)

    shape = (count, features)
    return line.launch(
        kernel,
        "qkv_backward",
        [here],
        (features // tile,),
        [
            whole(own),
            whole(other),
            (rows[0], shape, lambda j, s: (rows[1](s[0]), 0)),
            whole(grad_middle),
            (gain, (1, features), origin(2)),
            Weight(w_qkv, (tile, 3 * features), lambda j, core: (j, 0), features // tile),
        ],
        [full(shape, F32), full((1, frames, features)), full((1, features), F32)],
        [pltpu.VMEM(shape, F32)],
        flops=6 * count * features * features,
    )


def head_sum(product, reduce_mat):
    high = product.astype(BF16)
    low = (product - high.astype(F32)).astype(BF16)
    return dot(high, reduce_mat) + dot(low, reduce_mat)


def head_mats(lanes, width):
    row = lax.broadcasted_iota(jnp.int32, (lanes, 128), 0)
    col = lax.broadcasted_iota(jnp.int32, (lanes, 128), 1)
    reduce_mat = (row // width == col).astype(BF16)
    row = lax.broadcasted_iota(jnp.int32, (128, lanes), 0)
    col = lax.broadcasted_iota(jnp.int32, (128, lanes), 1)
    return reduce_mat, (col // width == row).astype(BF16)


def local_probs(q, k, reduce_mat, scale):
    probs = {}
    for a in range(len(q)):
        scores = [head_sum(q[a] * k[b], reduce_mat) * scale for b in range(a + 1)]
        peak = functools.reduce(jnp.maximum, scores)
        parts = [jnp.exp(s - peak) for s in scores]
        total = add_all(parts)
        for b in range(a + 1):
            probs[a, b] = parts[b] / total
    return probs


def local_attn_fwd_kernel(width, q_ref, k_ref, v_ref, o_ref):
    books, _, lanes = q_ref.shape
    reduce_mat, expand_mat = head_mats(lanes, width)
    q = [q_ref[a].astype(F32) for a in range(books)]
    k = [k_ref[a].astype(F32) for a in range(books)]
    v = [v_ref[a].astype(F32) for a in range(books)]
    probs = local_probs(q, k, reduce_mat, width**-0.5)
    for a in range(books):
        mixed = [dot(probs[a, b].astype(BF16), expand_mat) * v[b] for b in range(a + 1)]
        o_ref[a] = add_all(mixed).astype(BF16)


def by_half(core, parts, own_ref, other_ref):
    for c in range(2):

        @pl.when(core == c)
        def _():
            for i in range(2):
                own_ref[i] = parts[2 * c + i]
                other_ref[i] = parts[2 - 2 * c + i]


def local_attn_bwd_kernel(
    width, core, q_ref, k_ref, v_ref, g_ref, m_ref, own_ref, other_ref
):
    books, _, lanes = q_ref.shape
    scale = width**-0.5
    reduce_mat, expand_mat = head_mats(lanes, width)
    q = [q_ref[a].astype(F32) for a in range(books)]
    k = [k_ref[a].astype(F32) for a in range(books)]
    v = [v_ref[a].astype(F32) for a in range(books)]
    g = [g_ref[a].astype(F32) for a in range(books)]
    probs = local_probs(q, k, reduce_mat, scale)
    dq = [0.0] * books
    dk = [0.0] * books
    dv = [0.0] * books
    for a in range(books):
        dprobs = [head_sum(g[a] * v[b], reduce_mat) for b in range(a + 1)]
        inner = add_all([dprobs[b] * probs[a, b] for b in range(a + 1)])
        for b in range(a + 1):
            dscore = dot((probs[a, b] * (dprobs[b] - inner)).astype(BF16), expand_mat)
            dq[a] = dq[a] + dscore * k[b]
            dk[b] = dk[b] + dscore * q[a]
            dv[b] = dv[b] + dot(probs[a, b].astype(BF16), expand_mat) * g[a]
    parts = [
        jnp.stack([(one * by).astype(BF16) for one in ones])
        for ones, by in ((dq, scale), (dk, scale), (dv, 1.0))
    ]
    by_half(core, parts + [m_ref[...]], own_ref, other_ref)


def local_attn(line, here, packed, books, grads=None, lanes=512):
    count, wide = packed.shape
    features, frames = wide // 3, count // books
    width, groups = features // HEADS, features // lanes
    packed = packed.reshape(books, frames, wide)
    shape, block = (books, frames, features), (books, frames, lanes)

    def at(part):
        return lambda h, *_: (0, 0, part * groups + h)

    ins = [(packed, block, at(i)) for i in range(3)]
    if grads is None:

        def forward(scalars, ins, outs, _):
            local_attn_fwd_kernel(width, *[i[0] for i in ins], *outs)

        out = line.launch(
            forward,
            "local_attn_forward",
            [here],
            (groups,),
            ins,
            [(sds(shape), block, at(0))],
            flops=4000 * count * features,
        )
        return out[0].reshape(count, features)

    def backward(scalars, ins, outs, _):
        local_attn_bwd_kernel(width, scalars[0][0], *[i[0] for i in ins], *outs)

    ins += [(g.reshape(shape), block, at(0)) for g in grads]
    half = (sds((2,) + shape), (2,) + block, lambda h, *_: (0, 0, 0, h))
    out = line.launch(
        backward,
        "local_attn_backward",
        [here],
        (groups,),
        ins,
        [half] * 2,
        flops=10000 * count * features,
    )
    return [one.reshape(2, count, features) for one in out]


def item_mask(lengths_ref, micro, frames, items):
    row = lax.broadcasted_iota(jnp.int32, (frames, frames), 0)
    col = lax.broadcasted_iota(jnp.int32, (frames, frames), 1)
    row_item = jnp.zeros((frames, frames), jnp.int32)
    col_item = jnp.zeros((frames, frames), jnp.int32)
    end = 0
    for i in range(items):
        end = end + lengths_ref[micro, 0, i]
        row_item = row_item + (row >= end).astype(jnp.int32)
        col_item = col_item + (col >= end).astype(jnp.int32)
    return (row_item == col_item) & (row >= col)


def head_parts(block, width):
    per = 128 // width
    lane = lax.broadcasted_iota(jnp.int32, (block.shape[0], 128), 1)
    parts = []
    for h in range(block.shape[1] // width):
        tile = block[:, (h // per) * 128 : (h // per + 1) * 128]
        parts.append(jnp.where(lane // width == h % per, tile, jnp.zeros_like(tile)))
    return parts


def frame_probs(q, k, mask, scale):
    scores = jnp.where(mask, dot_t(q, k) * scale, -1e30)
    parts = jnp.exp(scores - jnp.max(scores, axis=-1, keepdims=True))
    return parts / jnp.sum(parts, axis=-1, keepdims=True)


def global_attn_fwd_kernel(width, items, lengths_ref, q_ref, k_ref, v_ref, o_ref):
    frames, lanes = q_ref.shape
    mask = item_mask(lengths_ref, pl.program_id(0), frames, items)
    per = 128 // width
    q = head_parts(q_ref[...], width)
    v = head_parts(v_ref[...], width)
    mixed = [0.0] * (lanes // 128)
    for h in range(lanes // width):
        tile = slice((h // per) * 128, (h // per + 1) * 128)
        probs = frame_probs(q[h], k_ref[:, tile], mask, width**-0.5)
        mixed[h // per] = mixed[h // per] + dot(probs.astype(BF16), v[h])
    for i, tile in enumerate(mixed):
        o_ref[:, i * 128 : (i + 1) * 128] = tile.astype(BF16)


def global_attn_bwd_kernel(
    width, items, core, lengths_ref, q, k, v, g_ref, m_ref, own_ref, other_ref
):
    frames, lanes = q.shape
    scale = width**-0.5
    mask = item_mask(lengths_ref, core, frames, items)
    per = 128 // width
    q = head_parts(q, width)
    wide_k, k = k, head_parts(k, width)
    g = head_parts(g_ref[...], width)
    tiles = lanes // 128
    dq, dk, dv = [0.0] * tiles, [0.0] * tiles, [0.0] * tiles
    for h in range(lanes // width):
        t = h // per
        tile = slice(t * 128, (t + 1) * 128)
        probs = frame_probs(q[h], wide_k[:, tile], mask, scale)
        dv[t] = dv[t] + t_dot(probs.astype(BF16), g[h])
        dprobs = dot_t(g[h], v[:, tile])
        inner = jnp.sum(dprobs * probs, axis=-1, keepdims=True)
        dscore = (probs * (dprobs - inner)).astype(BF16)
        dq[t] = dq[t] + dot(dscore, k[h])
        dk[t] = dk[t] + t_dot(dscore, q[h])
    parts = [
        jnp.concatenate([(one * by).astype(BF16) for one in ones], axis=1)
        for ones, by in ((dq, scale), (dk, scale), (dv, 1.0))
    ]
    by_half(core, parts + [m_ref[...]], own_ref, other_ref)


def global_attn_forward(line, packed, lengths, lanes=1024):
    micros, _, items = lengths.shape
    count, wide = packed.shape
    features, frames = wide // 3, count // micros
    width, groups = features // HEADS, features // lanes
    block = (frames, lanes)

    def at(part):
        return lambda m, h, _: (m, part * groups + h)

    def kernel(scalars, ins, outs, _):
        global_attn_fwd_kernel(width, items, scalars[0], *[i[0] for i in ins], *outs)

    return line.launch(
        kernel,
        "global_attn_forward",
        [lengths],
        (micros, groups),
        [(packed, block, at(i)) for i in range(3)],
        [(sds((count, features)), block, at(0))],
        flops=10000 * count * features,
    )[0]


def global_attn_backward(line, here, kept, first, lengths, grads, lanes=1024):
    micros, _, items = lengths.shape
    _, count, features = kept[0].shape
    frames = count // micros
    width, groups = features // HEADS, features // lanes
    block = (frames, lanes)

    def kernel(scalars, ins, outs, _):
        core = scalars[0][0]
        q, k, v = [read(core, i)[0] for i in ins[:3]]
        global_attn_bwd_kernel(
            width, items, core, scalars[1], q, k, v, ins[3][0], ins[4][0], *outs
        )

    half = (sds((2, frames, features)), (2,) + block, lambda h, *_: (0, 0, h))
    return line.launch(
        kernel,
        "global_attn_backward",
        [here, lengths],
        (groups,),
        [(kept, (1,) + block, lambda h, c, _, i=i: (first + i, c[0], h)) for i in range(3)]
        + [(g, block, lambda h, *_: (0, h)) for g in grads],
        [half] * 2,
        flops=30000 * frames * features,
    )


def place_columns(line, here, sources, rows, spots, cut=False):
    features = spots.shape[0]

    def kernel(scalars, ins, outs, _):
        for i, refs in enumerate(ins[1:]):
            block = read(scalars[0][0], refs).reshape(rows, features)
            placed = dot(block, ins[0][0][...]).astype(BF16)
            wide = features // len(outs)
            for k, out in enumerate(outs):
                out[i] = placed[:, k * wide : (k + 1) * wide]

    ins = [whole(spots)]
    for source in sources:
        if isinstance(source, tuple):
            ins.append((source[0], (1, rows, features), lambda _, s, plane=source[1]: (plane, 0, 0)))
        else:
            ins.append(whole(source))
    parts = 2 if cut else 1
    out = line.launch(
        kernel,
        "place_columns",
        [here],
        (1,),
        ins,
        [full((len(sources), rows, features // parts))] * parts,
        flops=2 * len(sources) * rows * features * features,
    )
    return out if cut else out[0]


def place_units(line, table, source, rows, units):
    per = 4

    def kernel(scalars, ins, outs, _):
        for i in range(per):
            outs[0][0, :, i * UNIT : (i + 1) * UNIT] = read(scalars[0][0], ins[i])[0]

    first, count = units

    def at(i):
        return lambda u, t: (0, 0, t[1 + first + u * per + i])

    return line.launch(
        kernel,
        "place_units",
        [table],
        (count // per,),
        [(source, (1, rows, UNIT), at(i)) for i in range(per)],
        [(sds((1, rows, count * UNIT)), (1, rows, per * UNIT), lambda u, t: (0, 0, u))],
    )[0]


def pack(line, here, arrays, features):
    count = arrays[0].shape[0]
    planes = [(i, c) for i, a in enumerate(arrays) for c in range(a.shape[1] // features)]

    def kernel(scalars, ins, outs, _):
        for plane, (i, c) in enumerate(planes):
            outs[0][plane] = ins[i][0][:, c * features : (c + 1) * features].astype(BF16)

    return line.launch(
        kernel,
        "pack",
        [here],
        (1,),
        [whole(a) for a in arrays],
        [full((len(planes), count, features))],
    )[0]


class Group:
    def __init__(self, table, units, lefts, rights, tile, tiles, plane):
        self.table, self.per = table, units // 4
        self.lefts, self.rights = lefts, rights
        self.tile, self.tiles, self.plane = tile, tiles, plane


def joined(core, blocks, ordered):
    if ordered:
        pairs = []
        for a, b in zip(blocks[::2], blocks[1::2]):
            pairs += [jnp.where(core == 0, a, b), jnp.where(core == 0, b, a)]
        blocks = pairs
    return blocks[0] if len(blocks) == 1 else jnp.concatenate(blocks, axis=0)


def weight_grad(line, group, first, steps, per, addends, split):
    lefts, rights, tile = group.lefts, group.rights, group.tile

    def kernel(scalars, ins, outs, _):
        core = scalars[0][0]
        left_refs = [ins[i * per : (i + 1) * per] for i in range(len(lefts))]
        ins = ins[len(lefts) * per :]
        right = joined(
            core, [r[0][0] for r in ins[: len(rights)]], len(rights) > len(lefts)
        )
        add_refs = [r[0] for r in ins[len(rights) :]]
        for i in range(per):
            at = slice(i * UNIT, (i + 1) * UNIT)
            left = joined(
                core, [read(core, r[i])[0] for r in left_refs], len(lefts) > len(rights)
            )
            out = add_all([t_dot(left, right)] + [r[at, :].astype(F32) for r in add_refs])
            out = out.astype(BF16)
            if not split:
                outs[0][at, :] = out
            elif per == 1:
                outs[0][...] = out[: UNIT // 2]
                outs[1][...] = out[UNIT // 2 :]
            else:
                half = per // 2
                outs[i // half][(i % half) * UNIT : (i % half + 1) * UNIT, :] = out

    def left_in(given, start, i):
        rows = (given[0] if isinstance(given, tuple) else given).shape[1]
        return (
            given,
            (1, rows, UNIT),
            lambda u, j, t: (group.plane(j, t), 0, t[start + first + u * per + i]),
        )

    def right_in(given, count, at):
        return given, (1, count, tile), lambda u, j, t: at(j, t)

    def block(skip, rows=per * UNIT):
        return (rows, tile), lambda u, j, t: (skip + u, j)

    wide = group.tiles * tile
    rows = sum(count for _, count, _ in rights)
    if split:
        outs = [(sds((per * UNIT // 2, wide)),) + block(0, per * UNIT // 2)] * 2
    else:
        outs = [(sds((steps * per * UNIT, wide)),) + block(0)]
    out = line.launch(
        kernel,
        "weight_grad",
        [group.table],
        (steps, group.tiles),
        [left_in(a, start, i) for a, start in lefts for i in range(per)]
        + [right_in(*right) for right in rights]
        + [(a,) + block(skip) for a, skip in addends],
        outs,
        flops=2 * steps * per * UNIT * wide * rows,
    )
    return out if split else out[0]


class Devices:
    def __init__(self, size):
        self.size = size
        self.core = lax.axis_index("section")
        self.index = lax.axis_index("dp")

    def bits(self, core, kind):
        near = [1, 2] if core == 0 else [2, 1]
        far = [1 << b for b in range(2, self.size.bit_length() - 1)]
        return far[:1] + near + far[1:] if kind == FAR else near + far

    def swap(self, array, step, kind):
        pairs = []
        for core in range(2):
            by = self.bits(core, kind)[step]
            pairs += [(core * self.size + i, core * self.size + (i ^ by)) for i in range(self.size)]
        return lax.ppermute(array, ("section", "dp"), pairs)

    def cores(self, array):
        return lax.ppermute(array, "section", [(0, 1), (1, 0)])

    def order(self, kind):
        orders = []
        for core in range(2):
            bits = self.bits(core, kind)
            if kind == LINE:
                bits = bits[:2] + bits[:1:-1]
            order = [
                sum(bit for i, bit in enumerate(bits) if (spot >> (len(bits) - 1 - i)) & 1)
                for spot in range(self.size)
            ]
            orders.append(jnp.array(order, jnp.int32))
        return jnp.where(self.core == 0, orders[0], orders[1]) ^ (
            self.index % 4 if kind == LINE else self.index
        )

    def columns(self, count, kind):
        block = count // self.size
        order = self.order(kind)
        return (order[:, None] * block + jnp.arange(block, dtype=jnp.int32)).reshape(-1)

    def spots(self, count, kind):
        at = self.columns(count, kind)[None, :]
        return (lax.broadcasted_iota(jnp.int32, (count, count), 0) == at).astype(BF16)

    def along_z(self, array):
        depth = self.size // 4
        groups = [[4 * z + place for z in range(depth)] for place in range(4)]
        return lax.psum_scatter(
            array, "dp", scatter_dimension=0, axis_index_groups=groups, tiled=True
        )

    def table(self, *orders):
        parts = [self.core[None].astype(jnp.int32)] + [jnp.asarray(o, jnp.int32) for o in orders]
        return jnp.concatenate(parts)


class Sum:
    def __init__(self, devices, line, group, step=0, kind=LINE):
        self.devices, self.line, self.group, self.step = devices, line, group, step
        self.one, self.kind = None, kind
        self.rider = None

    def grad(self, first, count, addends, split=False):
        group = self.group
        steps, per = (count, group.per) if group.per > 1 else (1, count)
        return weight_grad(self.line, group, first * group.per, steps, per, addends, split)

    def send(self, array):
        rows, columns = array.shape
        if self.rider is not None:
            shape, size = self.rider.shape, self.rider.size
            high = self.rider.astype(BF16)
            low = (self.rider - high.astype(F32)).astype(BF16)
            extra = jnp.concatenate([high, low]).reshape(-1, columns)
            extra = jnp.pad(extra, ((0, -extra.shape[0] % RIDER), (0, 0)))
            array = jnp.concatenate([array, extra])
        got = self.devices.swap(array, self.step, self.kind)
        if self.rider is not None:
            extra = got[rows:].astype(F32).reshape(-1)
            self.rider = self.rider + (extra[:size] + extra[size : 2 * size]).reshape(shape)
        self.step += 1
        return got

    def first(self):
        self.one = self.send(self.grad(2, 2, []))

    def second(self):
        self.two = self.send(self.grad(1, 1, [] if self.one is None else [(self.one, 1)]))

    def third(self):
        addends = [(one, 0) for one in (self.one, self.two) if one is not None]
        if self.kind == LINE:
            self.kept = self.devices.along_z(self.grad(0, 1, addends))
            return
        self.kept, sent = self.grad(0, 1, addends, split=True)
        self.got = self.send(sent)

    def rest(self):
        if self.kind == LINE:
            return
        steps = self.devices.size.bit_length() - 1
        total = self.kept
        while self.step < steps:
            got = self.got
            half = total.shape[0] // 2
            sent = (total[half:].astype(F32) + got[half : 2 * half].astype(F32)).astype(BF16)
            total = total[:half].astype(F32) + got[:half].astype(F32)
            if self.step < steps - 1:
                total = total.astype(BF16)
            self.line.wait(sent)
            self.got = self.send(sent)
        self.kept = total

    def last(self):
        return self.kept.astype(F32) + self.got[: self.kept.shape[0]].astype(F32)


PLAN = (
    "g_qkv",
    "g_attn",
    "g_mlp",
    "g_pack",
    "l_qkv",
    "l_attn",
    "l_mlp",
    "l_place",
    "l_down first",
    "l_mlp_back",
    "l_attn_back",
    "l_down second",
    "g_units",
    "g_place",
    "l_up first",
    "l_down third",
    "l_rest first",
    "l_down rest",
    "l_qkv_back",
    "g_mlp_back",
    "wait l_down one",
    "wait active_got",
    "g_attn_back",
    "g_qkv_back",
    "wait placed_got",
    "g_gains",
    "l_rest second",
    "l_up second",
    "g_up second",
    "l_output",
    "l_up third",
    "g_output",
    "wait l_rest two",
    "l_up rest",
    "g_rest second",
    "g_up third",
    "wait l_rights",
    "g_down second",
    "l_rest third",
    "wait l_up one",
    "wait l_down kept",
    "wait l_dz",
    "g_rest third",
    "l_rest rest",
    "g_down third",
    "g_down rest",
    "g_rest rest",
    "g_up rest",
    "up_out",
    "rest_out",
    "down_out",
)


def both_halves(line, here, devices, ours, theirs, parts):
    rows, wide = ours.kept.shape
    half = jax.ShapeDtypeStruct((rows, wide), BF16)
    operands = [[one.kept] if one.kind == LINE else [one.kept, one.got] for one in (ours, theirs)]
    count = len(operands[0])

    def split(scalars, ins, outs, _):
        core = scalars[0][0]
        terms = [i[0][:rows, :].astype(F32) for i in ins]
        mine, other = add_all(terms[:count]), add_all(terms[count:])
        outs[0][...] = jnp.where(core == 0, other, mine).astype(BF16)
        outs[1][...] = jnp.where(core == 0, mine, other)

    sent, mine = line.launch(
        split,
        "split_halves",
        [here],
        (1,),
        [whole(one) for one in operands[0] + operands[1]],
        [full(half.shape), full(half.shape, F32)],
    )
    got = devices.cores(sent)

    def join(scalars, ins, outs, _):
        core = scalars[0][0]
        mine, got = ins[0][0][...], ins[1][0][...].astype(F32)
        joined = jnp.concatenate(
            [jnp.where(core == 0, mine, got), jnp.where(core == 0, got, mine)], axis=1
        )
        start = 0
        for out in outs:
            out[0] = joined[:, start : start + out.shape[2]]
            start += out.shape[2]

    return line.launch(
        join,
        "join_halves",
        [here],
        (1,),
        [whole(mine), whole(got)],
        [full((1, rows, 2 * wide * part // sum(parts)), F32) for part in parts],
    )


def local(codebook_embed, item_lengths, gain_attn, w_qkv, w_out, gain_mlp, w_up, w_down, cotangent):
    size = lax.axis_size("dp")
    micros, frames, books, features = codebook_embed.shape
    half_width = features // 2
    scale_in = books**-0.5
    devices, line = Devices(size), Line()
    core = devices.core
    first_core = core == 0
    here = core[None].astype(jnp.int32)

    def zero(core):
        return 0

    def same(core):
        return core

    gains = jnp.stack([gain_attn[0], gain_mlp[0]])
    own = [w_qkv[0], w_out[0], w_up[0], w_down[0]]
    gains_other = devices.cores(gains)
    other = [devices.cores(w) for w in own]
    w_qkv_g, w_out_g, w_up_g, w_down_g = zip(own, other)
    w_qkv_l, w_out_l, w_up_l, w_down_l = zip(other, own)
    gains_g = [(gains[i : i + 1], gains_other[i : i + 1]) for i in range(2)]
    gains_l = [(b, a) for a, b in gains_g]

    embed = codebook_embed.transpose(0, 2, 1, 3)
    upstream = cotangent.transpose(0, 2, 1, 3).reshape(micros, -1, features)

    def with_first(array):
        return array, devices.cores(array)

    columns = w_down.shape[1]
    unit_rows = columns // size == UNIT
    units = columns // UNIT
    near, far = range(units // 2), range(units // 2, units)
    placed_table = devices.table([0, 1, 2, 3], [0, 2, 1, 3])
    down_order = devices.order(DOWN_KIND) if unit_rows else range(units)
    down_table = devices.table(down_order, range(units))
    local_table = devices.table(devices.order(LOCAL_DOWN_KIND) if unit_rows else range(units))
    spots = devices.spots(features, REST_KIND)
    local_spots = devices.spots(features, LOCAL_REST_KIND)

    def by_units(array, kind):
        if unit_rows:
            return array
        if isinstance(array, tuple):
            return tuple(by_units(a, kind) for a in array)
        return jnp.take(array[:1], devices.columns(columns, kind), axis=2)

    def down_group(table, lefts, rights):
        return Group(table, units, lefts, rights, half_width, 1, lambda j, t: 0)

    def up_group(lefts, rights):
        return Group(
            placed_table,
            4,
            lefts,
            [(a, count, lambda j, t, i=i: (0, i, j)) for a, count, i in rights],
            features,
            2,
            lambda j, t: 2,
        )

    def rest_group(lefts, rights):
        return Group(
            placed_table,
            4,
            lefts,
            [(a, count, lambda j, t, i=i: (j, i, 0)) for a, count, i in rights],
            features,
            2,
            lambda j, t: jnp.where(2 * t[0] + j == 3, 1, 0),
        )

    def my_half(array):
        return jnp.where(first_core, array[..., :half_width], array[..., half_width:])

    def other_half(array):
        return jnp.where(first_core, array[..., half_width:], array[..., :half_width])

    def halves(array):
        got = devices.cores(other_half(array).astype(BF16)).astype(array.dtype)
        mine = my_half(array)
        return jnp.where(first_core, jnp.stack([mine, got]), jnp.stack([got, mine]))

    def both(mine, others):
        return [(mine, mine.shape[1], 0), (devices.cores(others), mine.shape[1], 0)]

    def all_rows(mine, others, kind):
        rights = both(mine, others)
        far = devices.swap(jnp.concatenate([rights[0][0], rights[1][0]], axis=1), 0, kind)
        return rights + [(far, frames, i) for i in range(micros)]

    at = types.SimpleNamespace()

    def g_qkv():
        def frame_rows(core, ins):
            (e_ref,) = ins[0]
            return [
                add_all([e_ref[m, b].astype(F32) for b in range(books)]) * scale_in
                for m in range(micros)
            ]

        at.rows, at.normed, at.packed = qkv_forward(
            line, here, (micros * frames, [whole(embed)]), frame_rows, gains[:1], own[0]
        )

    def g_attn():
        at.mixture = global_attn_forward(line, at.packed, item_lengths)

    def g_mlp():
        result, at.middle, at.normed_two, active = mlp_forward(
            line, here, at.rows, at.mixture, own[1], gains[1:], own[2], own[3], True
        )
        at.states, at.active = with_first(result), with_first(active)
        at.active_units = by_units(at.active, DOWN_KIND)

    def g_pack():
        arrays = [at.normed, at.mixture, at.normed_two, at.packed, at.middle]
        at.kept = with_first(pack(line, here, arrays, features))

    def l_qkv():
        def local_rows(core, ins):
            (e_ref,), s_refs = ins
            state = read(core, s_refs).astype(F32)
            return [e_ref[0, b].astype(F32) + state for b in range(books)]

        parts = [
            (embed, (1, books, frames, features), lambda j, s: (s[0], 0, 0, 0)),
            (at.states, (frames, features), lambda j, s: (s[0], 0)),
        ]
        at.l_rows, at.l_normed, at.l_packed = qkv_forward(
            line, here, (books * frames, parts), local_rows, gains_l[0], w_qkv_l
        )

    def l_attn():
        at.l_mixture = local_attn(line, here, at.l_packed, books)

    def l_mlp():
        at.l_out, at.l_middle, at.l_normed_two, at.l_active, at.l_slope = mlp_forward(
            line, here, at.l_rows, at.l_mixture, w_out_l, gains_l[1], w_up_l, w_down_l, False
        )
        at.l_active_got = devices.cores(at.l_active)
        at.l_down = Sum(
            devices,
            line,
            down_group(
                local_table,
                [
                    (by_units(at.l_active, LOCAL_DOWN_KIND), 1),
                    (by_units(at.l_active_got, LOCAL_DOWN_KIND), 1),
                ],
                [
                    (upstream, books * frames, lambda j, t: (t[0], 0, t[0])),
                    (upstream, books * frames, lambda j, t: (1 - t[0], 0, t[0])),
                ],
            ),
            kind=LOCAL_DOWN_KIND,
        )

    def g_units():
        at.active_got = devices.swap(
            place_units(line, down_table, at.active_units, micros * frames, (far.start, len(far))),
            0,
            DOWN_KIND,
        )

    def g_place():
        at.placed, placed_far = place_columns(
            line, here, [(at.kept, i) for i in range(3)], micros * frames, spots, True
        )
        at.placed_got = devices.swap(placed_far, 0, REST_KIND)

    def l_place():
        placed = place_columns(
            line, here, [at.l_normed, at.l_mixture, at.l_normed_two], books * frames, local_spots
        )
        at.l_placed_got = devices.cores(placed)
        at.l_lefts = [(placed, 1), (at.l_placed_got, 5)]

    def l_mlp_back():
        at.l_low, dz_own, dz_other, at.l_dm, at.l_do, at.l_gain_two = mlp_backward(
            line,
            here,
            (upstream, same, zero, books * frames),
            (at.l_slope, 0, zero),
            (at.l_middle[None], 0, zero),
            w_out_l,
            gains_l[1],
            w_up_l,
            w_down_l,
        )
        at.l_dz = both(dz_own, dz_other)

    def l_attn_back():
        grads = (at.l_do, at.l_low)
        at.l_dp = local_attn(line, here, at.l_packed, books, grads)
        at.l_rights = both(*at.l_dp)

    def l_qkv_back():
        at.local_grad, at.frame_grad, at.l_gain_one = qkv_backward(
            line, here, *at.l_dp, (at.l_rows, zero), at.l_dm, gains_l[0], w_qkv_l, books
        )
        at.g_frame = all_rows(at.frame_grad, at.frame_grad, DOWN_KIND)

    def l_output():
        at.local_out = halves(at.l_out.reshape(books, frames, features))
        line.wait(at.local_out)

    def g_mlp_back():
        at.g_low, dz_own, dz_other, at.g_dm, at.g_do, at.g_gain_two = mlp_backward(
            line,
            here,
            (at.frame_grad, zero, zero, frames),
            (at.active, 1, same),
            (at.kept, 6, same),
            w_out_g,
            gains_g[1],
            w_up_g,
            w_down_g,
        )
        at.g_dz = all_rows(dz_own, dz_other, REST_KIND)

    def g_attn_back():
        grads = (at.g_do, at.g_low)
        at.g_dp = global_attn_backward(line, here, at.kept, 3, item_lengths, grads)
        at.g_rights = all_rows(*at.g_dp, REST_KIND)

    def g_qkv_back():
        at.global_grad, _, at.g_gain_one = qkv_backward(
            line, here, *at.g_dp, (at.rows, same), at.g_dm, gains_g[0], w_qkv_g, 1
        )

    def g_gains():
        gains = [at.g_gain_one, at.g_gain_two, at.l_gain_one, at.l_gain_two]
        gains = jnp.concatenate(gains)
        at.gains = gains + devices.swap(gains, 0, REST_KIND)
        line.wait(at.gains)

    def g_output():
        at.embed_grad = halves(
            at.local_grad.reshape(books, frames, features) + (at.global_grad * scale_in)[None]
        )
        line.wait(at.embed_grad)

    def down_out():
        (at.down,) = both_halves(line, here, devices, at.g_down, at.l_down, (1,))

    def up_out():
        (at.up,) = both_halves(line, here, devices, at.g_up, at.l_up, (1,))

    def rest_out():
        at.qkv, at.out = both_halves(line, here, devices, at.g_rest, at.l_rest, (3, 1))

    def make(name):
        if not hasattr(at, name):
            if name == "l_up":
                one = Sum(devices, line, up_group(at.l_lefts, at.l_dz), kind=LOCAL_REST_KIND)
            elif name == "l_rest":
                one = Sum(devices, line, rest_group(at.l_lefts, at.l_rights), kind=LOCAL_REST_KIND)
            elif name == "g_down":
                lefts = [(at.active_units, 1), (at.active_got, 1 + units)]
                rights = [(a, count, lambda j, t, i=i: (0, i, t[0])) for a, count, i in at.g_frame]
                one = Sum(devices, line, down_group(down_table, lefts, rights), 1, DOWN_KIND)
            else:
                lefts = [(at.placed, 1), (at.placed_got, 1)]
                if name == "g_up":
                    one = Sum(devices, line, up_group(lefts, at.g_dz), 1, REST_KIND)
                    one.rider = at.gains
                else:
                    one = Sum(devices, line, rest_group(lefts, at.g_rights), 1, REST_KIND)
            setattr(at, name, one)
        return getattr(at, name)

    steps = (g_qkv, g_attn, g_mlp, g_pack, l_qkv, l_attn, l_mlp, g_units, g_place, l_place)
    steps += (l_mlp_back, l_attn_back, l_qkv_back, l_output)
    steps += (g_mlp_back, g_attn_back, g_qkv_back, g_gains, g_output)
    steps += (down_out, up_out, rest_out)
    steps = {step.__name__: step for step in steps}
    for words in PLAN:
        name, *rest = words.split()
        if name in steps:
            steps[name]()
        elif name == "wait":
            one = getattr(at, rest[0])
            one = getattr(one, rest[1]) if rest[1:] not in ([], ["far"]) else one
            line.wait(one[2 if "far" in rest else 1][0] if isinstance(one, list) else one)
        else:
            getattr(make(name), rest[0])()
    gain_sums = at.g_up.rider
    gain_sums = gain_sums + devices.cores(gain_sums)
    gain_sums = jnp.where(first_core, gain_sums[:2], gain_sums[2:]).reshape(2, size, -1)
    gain_sums = lax.dynamic_index_in_dim(gain_sums, devices.index, 1, keepdims=False)

    return (
        at.local_out.transpose(0, 2, 1, 3),
        at.embed_grad.transpose(0, 2, 1, 3),
        gain_sums[:1],
        at.qkv,
        at.out,
        gain_sums[1:],
        at.up,
        at.down,
    )


def solution(mesh):
    in_specs = (
        P(None, "dp", None, None),
        P(None, "dp", None),
        P("section", None),
        P("section", None, None),
        P("section", None, None),
        P("section", None),
        P("section", None, None),
        P("section", None, None),
        P(None, "dp", None, None),
    )
    out_specs = (
        P(None, "dp", None, "section"),
        P(None, "dp", None, "section"),
        P("section", "dp"),
        P("section", "dp", None),
        P("section", "dp", None),
        P("section", "dp"),
        P("section", "dp", None),
        P("section", "dp", None),
    )
    return jax.shard_map(local, mesh=mesh, in_specs=in_specs, out_specs=out_specs, check_vma=False)
```
